32 devices in a mesh: doc: 4 (over y, x), blk: 8 (over z, core).
Axes of the slice: x: 2, y: 2, z: 4, core: 2. Of those that a mesh axis runs over, the one named last changes fastest.
Arguments:
- byte_embed: bfloat16 [32, 2048, 768], P('doc', 'blk'), may hold values from -6 to 6
- doc_lengths: int32 [32], P('doc'), may hold values from 200 to 2048, as said below
- key_mask: int32 [32, 2048], P('doc', 'blk'), may hold values from 0 to 1, as said below
- latents: float32 [256, 1280], P('blk'), may hold values from -6 to 6
- gain_query: float32 [1280], replicated, may hold values from 0.1 to 1.9
- gain_bytes: float32 [768], replicated, may hold values from 0.1 to 1.9
- gain_mlp: float32 [1280], replicated, may hold values from 0.1 to 1.9
- w_query: bfloat16 [1280, 256], replicated, may hold values from -0.25 to 0.25
- w_key: bfloat16 [768, 256], replicated, may hold values from -0.21875 to 0.21875
- w_value: bfloat16 [768, 1280], replicated, may hold values from -0.21875 to 0.21875
- w_out: bfloat16 [1280, 1280], replicated, may hold values from -1.25 to 1.25
- w_up: bfloat16 [1280, 1280], replicated, may hold values from -0.15625 to 0.15625
- w_down: bfloat16 [1280, 1280], replicated, may hold values from -0.15625 to 0.15625
- cotangent: float32 [32, 256, 1280], P('doc', 'blk'), may hold values from -6 to 6
Outputs:
- latents_out: float32 [32, 256, 1280], P('doc', 'blk')
- byte_grad: float32 [32, 2048, 768], P('doc', 'blk')
- latents_grad: float32 [256, 1280], P('blk')
- gain_query_grad: float32 [1280], P('blk')
- gain_bytes_grad: float32 [768], P('blk')
- gain_mlp_grad: float32 [1280], P('blk')
- w_query_grad: float32 [1280, 256], P('blk')
- w_key_grad: float32 [768, 256], P('blk')
- w_value_grad: float32 [768, 1280], P('blk')
- w_out_grad: float32 [1280, 1280], P('blk')
- w_up_grad: float32 [1280, 1280], P('blk')
- w_down_grad: float32 [1280, 1280], P('blk')
The draws below stay inside these ranges and needn't reach their ends.
Inputs may be any that keep to these rules, and one draw needn't show every extreme that they name: `doc_lengths`: every group of 8 documents on one index of doc holds one document of length 2048, which one drawn from the seed. `key_mask`: slot 0 of every document is 1.
All inputs are finite; a program needn't handle non-finite values.
Results may differ from the reference program's by a relative error of at most 0.029.
Values may be sent and summed in bfloat16 or wider, within the bound.
A program may use at most 192 MiB of HBM per device.

```python
import jax
import jax.numpy as jnp
from jax import lax

DL = 1280
DIN = 768
LAT = 256
HEADS = 8
QK_HEAD = 32
V_HEAD = 160
DQK = 256
DV = 1280
MAXLEN = 2048
MINLEN = 200
DOCS_G = 8
DOCS = 32


def draw_doc_lengths(key, part):
    key = jax.random.fold_in(key, 11)
    key_lengths, key_choice = jax.random.split(key)
    lengths = jax.random.randint(key_lengths, (DOCS,), MINLEN, MAXLEN + 1, dtype=jnp.int32)
    groups = lengths.reshape(DOCS // DOCS_G, DOCS_G)
    chosen = jax.random.randint(key_choice, (DOCS // DOCS_G, 1), 0, DOCS_G, dtype=jnp.int32)
    slot_ids = jnp.arange(DOCS_G, dtype=jnp.int32)[None, :]
    groups = jnp.where(slot_ids == chosen, MAXLEN, groups)
    return groups.reshape(DOCS).astype(jnp.int32)


def draw_key_mask(key, part):
    key = jax.random.fold_in(key, 23)
    draws_int = jax.random.randint(key, (DOCS, MAXLEN), 0, 4, dtype=jnp.int32)
    keep_mask = jnp.where(draws_int > 0, 1, 0).astype(jnp.int32)
    first_slot = jnp.arange(MAXLEN, dtype=jnp.int32)[None, :] == 0
    return jnp.where(first_slot, 1, keep_mask).astype(jnp.int32)


def level_of(key, extent, cuts, smallest, high):
    level = 1.0
    for dim, blocks in cuts:
        draws = jax.random.uniform(jax.random.fold_in(jax.random.fold_in(key, 6), dim), (blocks,), jnp.float32, smallest / len(cuts), high / len(cuts))
        level = level * jnp.repeat(jnp.exp(draws), extent[dim] // blocks).reshape((-1,) + (1,) * (len(extent) - 1 - dim))
    return level


def bell_draw(key, extent, scale, most, cuts=(), kind=jnp.bfloat16):
    array = jax.random.normal(key, extent, jnp.float32) * scale
    if len(cuts) > 0:
        array = level_of(key, extent, cuts, -0.22, 0.18) * array
    return jnp.clip(array, min=-most, max=most).astype(kind)


def setup_inputs(seed: int = 0) -> dict:
    streams_of = jax.random.split(jax.random.key(seed), 15)
    byte_embed = bell_draw(streams_of[0], (DOCS, MAXLEN, DIN), 1.0, 6.0, ((0, 4), (1, 8)))
    doc_lengths = draw_doc_lengths(jax.random.fold_in(streams_of[14], 71), 0)
    key_mask = draw_key_mask(jax.random.fold_in(streams_of[14], 71), 0)
    latents = bell_draw(streams_of[3], (LAT, DL), 1.0, 6.0, ((0, 8),), jnp.float32)
    gain_query = jnp.clip(1.0 + 0.18 * jax.random.normal(streams_of[4], (DL,), jnp.float32), 0.1, 1.9)
    gain_bytes = jnp.clip(1.0 + 0.18 * jax.random.normal(streams_of[5], (DIN,), jnp.float32), 0.1, 1.9)
    gain_mlp = jnp.clip(1.0 + 0.18 * jax.random.normal(streams_of[6], (DL,), jnp.float32), 0.1, 1.9)
    w_query = bell_draw(streams_of[7], (DL, DQK), (DL // 2) ** -0.5, 0.25)
    w_key = bell_draw(streams_of[8], (DIN, DQK), DIN ** -0.5, 0.21875)
    w_value = bell_draw(streams_of[9], (DIN, DV), DIN ** -0.5, 0.21875)
    w_out = bell_draw(streams_of[10], (DV, DL), (DV // 64) ** -0.5, 1.25)
    w_up = bell_draw(streams_of[11], (DL, DL), DL ** -0.5, 0.15625)
    w_down = bell_draw(streams_of[12], (DL, DL), DL ** -0.5, 0.15625)
    cotangent = bell_draw(streams_of[13], (DOCS, LAT, DL), 1.0, 6.0, ((0, 4), (1, 8)), jnp.float32)
    return {"byte_embed": byte_embed, "doc_lengths": doc_lengths, "key_mask": key_mask, "latents": latents, "gain_query": gain_query, "gain_bytes": gain_bytes, "gain_mlp": gain_mlp, "w_query": w_query, "w_key": w_key, "w_value": w_value, "w_out": w_out, "w_up": w_up, "w_down": w_down, "cotangent": cotangent}


@jax.custom_vjp
def low(v):
    return lax.optimization_barrier(v.astype(jnp.bfloat16)).astype(jnp.float32)

@jax.custom_vjp
def low_back(v):
    return v

def low_keep(v):
    return (low(v), None)

def low_pass(kept, grad):
    return (grad,)

def back_keep(v):
    return (v, None)

def back_low(kept, grad):
    return (low(grad),)
low.defvjp(low_keep, low_pass)
low_back.defvjp(back_keep, back_low)
highest = lax.Precision.HIGHEST
epsilon = 1e-05
masked_score = -1e+30

def layer_norm(matrix, gain_vec):
    centered = matrix - lax.optimization_barrier(jnp.mean(matrix, axis=-1, keepdims=True))
    spread = lax.optimization_barrier(jnp.mean(centered * centered, axis=-1, keepdims=True))
    return centered * lax.rsqrt(spread + epsilon) * gain_vec

def product(left_op, right_op):
    return jnp.dot(left_op, right_op, precision=highest, preferred_element_type=jnp.float32)

def one_document(queries, doc_bytes, usable, latent_rows, g_bytes, g_mlp, w_k, w_v, w_o, w_u, w_d):
    normed = low(layer_norm(doc_bytes, g_bytes))
    key_rows = low_back(low(product(normed, w_k))).reshape(MAXLEN, HEADS, QK_HEAD)
    value_rows = low_back(low(product(normed, w_v))).reshape(MAXLEN, HEADS, V_HEAD)
    heads_q = queries.reshape(LAT, HEADS, QK_HEAD)
    scores = low_back(jnp.einsum('qhd,khd->hqk', heads_q, key_rows, precision=highest) * QK_HEAD ** (-0.5))
    masked = jnp.where(usable[None, None, :], scores, masked_score)
    row_top = lax.optimization_barrier(jnp.max(masked, axis=-1, keepdims=True))
    numerator = jnp.exp(masked - row_top)
    totals = lax.optimization_barrier(jnp.sum(numerator, axis=-1))
    weighted = low_back(jnp.einsum('hqk,khd->qhd', low(numerator), value_rows, precision=highest))
    attended = (weighted / totals.T[:, :, None]).reshape(LAT, HEADS * V_HEAD)
    branch = low_back(product(low(attended), w_o))
    middle = latent_rows + branch
    normed_mid = low(layer_norm(middle, g_mlp))
    up_proj = low_back(product(normed_mid, w_u))
    activated = low(jax.nn.gelu(up_proj))
    return middle + low_back(product(activated, w_d))

def reference(byte_embed, doc_lengths, key_mask, latents, gain_query, gain_bytes, gain_mlp, w_query, w_key, w_value, w_out, w_up, w_down, cotangent):
    positions = jnp.arange(MAXLEN, dtype=jnp.int32)
    usable = (positions[None, :] < doc_lengths[:, None]) & (key_mask == 1)

    def forward(inputs, latent_rows, g_query, g_bytes, g_mlp, w_q, w_k, w_v, w_o, w_u, w_d):
        queries = low_back(low(product(low(layer_norm(latent_rows, g_query)), w_q)))
        checked = jax.checkpoint(one_document)

        def per_document(carried, doc_item):
            doc_bytes, doc_usable = doc_item
            result = checked(queries, doc_bytes, doc_usable, latent_rows, g_bytes, g_mlp, w_k, w_v, w_o, w_u, w_d)
            return (carried, result)
        unused, outputs = lax.scan(per_document, jnp.zeros((), jnp.float32), (inputs, usable))
        return outputs
    outputs, pullback = jax.vjp(forward, byte_embed.astype(jnp.float32), latents, gain_query, gain_bytes, gain_mlp, w_query.astype(jnp.float32), w_key.astype(jnp.float32), w_value.astype(jnp.float32), w_out.astype(jnp.float32), w_up.astype(jnp.float32), w_down.astype(jnp.float32))
    gradients = pullback(cotangent)
    return (outputs, gradients[0], gradients[1], gradients[2], gradients[3], gradients[4], gradients[5], gradients[6], gradients[7], gradients[8], gradients[9], gradients[10])
```

```python
import functools
import math

import jax
import jax.numpy as jnp
from jax import lax
from jax.experimental import pallas as pl
from jax.experimental.pallas import tpu as pltpu
from jax.sharding import PartitionSpec as P

LAT = 256
HEADS = 8
QK_HEAD = 32
V_HEAD = 160
DQK = HEADS * QK_HEAD
DV = HEADS * V_HEAD
MESH = pl.DeviceIdType.MESH
F32 = jnp.float32
BF16 = jnp.bfloat16

epsilon = 1e-05
masked_score = -1e30
LOG2E = math.log2(math.e)
SCORE2 = QK_HEAD ** (-0.5) * LOG2E
SCORE_SCALE = QK_HEAD ** (-0.5)


def dot_nn(a, b):
    return jnp.dot(a, b, preferred_element_type=F32)


def dot_nt(a, b):
    return lax.dot_general(a, b, (((1,), (1,)), ((), ())), preferred_element_type=F32)


def norm_parts(v):
    centered = v - jnp.mean(v, axis=-1, keepdims=True)
    spread = jnp.mean(centered * centered, axis=-1, keepdims=True)
    inv = lax.rsqrt(spread + epsilon)
    return centered * inv, inv


def window(h):
    return V_HEAD * h // 128 * 128


def value_mask(h, rows):
    lane = lax.broadcasted_iota(jnp.int32, (rows, 256), 1) + window(h)
    keep = (lane >= V_HEAD * h) & (lane < V_HEAD * (h + 1))
    return jnp.where(keep, 1.0, 0.0).astype(BF16)


def query_mask(h, rows):
    lane = lax.broadcasted_iota(jnp.int32, (rows, DQK), 1)
    keep = (lane >= QK_HEAD * h) & (lane < QK_HEAD * (h + 1))
    return jnp.where(keep, 1.0, 0.0).astype(BF16)


def row_to_lanes(row):
    return jnp.transpose(jnp.broadcast_to(row, (128, row.shape[1])))


def wide(col, n):
    return jnp.concatenate([col] * (n // 128), axis=1) if n > 128 else col


def remote(src, dst, send, recv, doc, blk):
    return pltpu.make_async_remote_copy(
        src_ref=src, dst_ref=dst, send_sem=send, recv_sem=recv,
        device_id=(doc, blk), device_id_type=MESH,
    )


def forward_kernel(
    nb,
    x_ref, bias_ref, lat_ref, gq_ref, gb_ref, wq_ref, wk_ref, wv_ref,
    att_ref, lse_ref, k_ref, v_ref, nl_ref, qall_ref,
    normed, qm, lloc, lmate, lz, acc, part, mate_in, rin, lin,
    q_s, q_r, l_s, l_r, mate_s, mate_r, rs_s, rs_r, ls_s, ls_r,
):
    D, kc, din = x_ref.shape
    rq = lat_ref.shape[0]
    pos = nb // 2
    doc, blk = lax.axis_index("doc"), lax.axis_index("blk")
    p, c = blk // 2, blk % 2
    mate = 2 * p + 1 - c
    barrier = pltpu.get_barrier_semaphore()
    for i in range(1, nb):
        pl.semaphore_signal(
            barrier, inc=1, device_id=(doc, lax.rem(blk + i, nb)), device_id_type=MESH
        )

    xhat, _ = norm_parts(lat_ref[...])
    nl = (xhat * gq_ref[...]).astype(BF16)
    nl_ref[...] = nl
    own = pl.ds(pl.multiple_of(blk * rq, rq), rq)
    qall_ref[own, :] = dot_nn(nl, wq_ref[...]).astype(BF16)
    pl.semaphore_wait(barrier, nb - 1)

    def q_copy(i, slot):
        return remote(
            qall_ref.at[own, :], qall_ref.at[slot, :], q_s.at[i - 1], q_r.at[i - 1],
            doc, lax.rem(blk + i, nb),
        )

    for i in range(1, nb):
        q_copy(i, own).start()

    @pl.loop(0, D)
    def _(n):
        xh, _ = norm_parts(x_ref[n].astype(F32))
        normed[n] = (xh * gb_ref[...]).astype(BF16)
        k_ref[n] = dot_nn(normed[n], wk_ref[...]).astype(BF16)

    for i in range(1, nb):
        src = lax.rem(blk + nb - i, nb)
        q_copy(i, pl.ds(pl.multiple_of(src * rq, rq), rq)).wait_recv()
    for h in range(HEADS):
        qm[h] = qall_ref[...] * query_mask(h, LAT)

    @pl.loop(0, D)
    def _(n):
        bias = wide(row_to_lanes(bias_ref[pl.ds(n, 1), :]), LAT)
        kn = k_ref[n]
        rows = []
        for h in range(HEADS):
            s = dot_nt(kn, qm[h]) * SCORE2 + bias
            top = jnp.max(s, axis=0, keepdims=True)
            tot = jnp.sum(jnp.exp2(s - top), axis=0, keepdims=True)
            rows.append(top + jnp.log(tot) * LOG2E)
        lloc[n] = jnp.concatenate(rows, axis=0)

    half = D // 2
    mine, other = pl.ds(c * half, half), pl.ds((1 - c) * half, half)

    def merge(a, b):
        top = jnp.maximum(a, b)
        return top + jnp.log(jnp.exp2(a - top) + jnp.exp2(b - top)) * LOG2E

    first = remote(lloc.at[other], lmate, l_s.at[0], l_r.at[0], doc, mate)
    first.start()

    def values(lo, hi):
        @pl.loop(lo, hi)
        def _(n):
            v_ref[n] = dot_nn(normed[n], wv_ref[...]).astype(BF16)

    values(0, D // 4)
    first.wait_recv()
    lz[p] = merge(lloc[mine], lmate[...])

    def z_copy(i, slot):
        return remote(
            lz.at[p], lz.at[slot], l_s.at[i], l_r.at[i],
            doc, 2 * lax.rem(p + i, pos) + c,
        )

    for i in range(1, pos):
        z_copy(i, p).start()
    values(D // 4, 3 * D // 4)
    for i in range(1, pos):
        z_copy(i, lax.rem(p + pos - i, pos)).wait_recv()
    total = lz[0]
    for i in range(1, pos):
        total = merge(total, lz[i])
    lse_ref[mine] = total
    last = remote(lse_ref.at[mine], lse_ref.at[mine], l_s.at[pos], l_r.at[pos], doc, mate)
    last.start()
    values(3 * D // 4, D)
    remote(
        lse_ref.at[other], lse_ref.at[other], l_s.at[pos], l_r.at[pos], doc, mate
    ).wait_recv()

    def mate_copy(n):
        return remote(
            part.at[n, 1 - c], mate_in.at[n], mate_s.at[n], mate_r.at[n], doc, mate
        )

    def right_copy(n, j, src):
        return remote(
            src, rin.at[n, j], rs_s.at[n, j], rs_r.at[n, j],
            doc, 2 * jnp.minimum(p + 1, pos - 1) + c,
        )

    def left_copy(n, j, src):
        return remote(
            src, lin.at[n, j], ls_s.at[n, j], ls_r.at[n, j],
            doc, 2 * jnp.maximum(p - 1, 0) + c,
        )

    def chip_sum(n):
        mate_copy(n).wait_recv()
        for j in range(pos):
            both = part[n, c, j].astype(F32) + mate_in[n, j].astype(F32)
            part[n, c, j] = both.astype(BF16)

            @pl.when((p == 0) & (j > 0))
            def _():
                right_copy(n, j, part.at[n, c, j]).start()

            @pl.when((p == pos - 1) & (j < pos - 1))
            def _():
                left_copy(n, j, part.at[n, c, j]).start()

    @pl.loop(0, D)
    def _(n):
        logs = lse_ref[n]
        logs_t = jnp.transpose(jnp.concatenate([logs] * (128 // HEADS), axis=0))
        bias = bias_ref[pl.ds(n, 1), :]
        kn = k_ref[n]
        acc[...] = jnp.zeros_like(acc)
        for h in range(HEADS):
            s = dot_nt(qm[h], kn) * SCORE2 + bias
            prob = jnp.exp2(s - logs_t[:, h : h + 1]).astype(BF16)
            cols = slice(window(h), window(h) + 256)
            acc[:, cols] += dot_nn(prob, v_ref[n, :, cols] * value_mask(h, kc))
        for j in range(nb):
            part[n, j % 2, j // 2] = acc[rq * j : rq * (j + 1), :].astype(BF16)
        mate_copy(n).start()

        @pl.when(n > 0)
        def _():
            chip_sum(n - 1)

    chip_sum(D - 1)

    @pl.loop(0, D)
    def _(n):
        for j in range(1, pos):
            @pl.when((p > 0) & (j >= p))
            def _():
                right_copy(n, j, part.at[n, c, j]).wait_recv()

            @pl.when((p > 0) & (j > p))
            def _():
                both = rin[n, j].astype(F32) + part[n, c, j].astype(F32)
                part[n, c, j] = both.astype(BF16)
                right_copy(n, j, part.at[n, c, j]).start()

        for j in range(pos - 2, -1, -1):
            @pl.when((p < pos - 1) & (j <= p))
            def _():
                left_copy(n, j, part.at[n, c, j]).wait_recv()

            @pl.when((p < pos - 1) & (j < p))
            def _():
                both = lin[n, j].astype(F32) + part[n, c, j].astype(F32)
                part[n, c, j] = both.astype(BF16)
                left_copy(n, j, part.at[n, c, j]).start()

        att_ref[n] = part[n, c, p].astype(F32)

        @pl.when(p > 0)
        def _():
            att_ref[n] += rin[n, p].astype(F32)

        @pl.when(p < pos - 1)
        def _():
            att_ref[n] += lin[n, p].astype(F32)

    for i in range(1, nb):
        q_copy(i, own).wait_send()
    first.wait_send()
    for i in range(1, pos):
        z_copy(i, p).wait_send()
    last.wait_send()

    @pl.loop(0, D)
    def _(n):
        mate_copy(n).wait_send()
        for j in range(pos):
            @pl.when((j > p) & (p < pos - 1))
            def _():
                right_copy(n, j, part.at[n, c, j]).wait_send()

            @pl.when((j < p) & (p > 0))
            def _():
                left_copy(n, j, part.at[n, c, j]).wait_send()


def forward(nb, byte_embed, bias, latents, gain_query, gain_bytes, w_query, w_key, w_value):
    D, kc, din = byte_embed.shape
    rq, dl = latents.shape
    pos = nb // 2
    vmem = pl.BlockSpec(memory_space=pltpu.VMEM)
    dma = pltpu.SemaphoreType.DMA
    return pl.pallas_call(
        functools.partial(forward_kernel, nb),
        out_shape=(
            jax.ShapeDtypeStruct((D, rq, DV), F32),
            jax.ShapeDtypeStruct((D, HEADS, LAT), F32),
            jax.ShapeDtypeStruct((D, kc, DQK), BF16),
            jax.ShapeDtypeStruct((D, kc, DV), BF16),
            jax.ShapeDtypeStruct((rq, dl), BF16),
            jax.ShapeDtypeStruct((LAT, DQK), BF16),
        ),
        in_specs=[vmem] * 8,
        out_specs=(vmem,) * 6,
        scratch_shapes=[
            pltpu.VMEM((D, kc, din), BF16),
            pltpu.VMEM((HEADS, LAT, DQK), BF16),
            pltpu.VMEM((D, HEADS, LAT), F32),
            pltpu.VMEM((D // 2, HEADS, LAT), F32),
            pltpu.VMEM((pos, D // 2, HEADS, LAT), F32),
            pltpu.VMEM((LAT, DV), F32),
            pltpu.VMEM((D, 2, pos, rq, DV), BF16),
            pltpu.VMEM((D, pos, rq, DV), BF16),
            pltpu.VMEM((D, pos, rq, DV), BF16),
            pltpu.VMEM((D, pos, rq, DV), BF16),
            dma((nb - 1,)), dma((nb - 1,)), dma((pos + 1,)), dma((pos + 1,)),
            dma((D,)), dma((D,)),
            dma((D, pos)), dma((D, pos)), dma((D, pos)), dma((D, pos)),
        ],
        compiler_params=pltpu.CompilerParams(
            collective_id=0, has_side_effects=True, vmem_limit_bytes=56 * 2**20
        ),
        name="forward",
    )(
        byte_embed, bias, latents, gain_query.reshape(1, -1), gain_bytes.reshape(1, -1),
        w_query, w_key, w_value,
    )

def layer_norm(matrix, gain_vec):
    centered = matrix - jnp.mean(matrix, axis=-1, keepdims=True)
    spread = jnp.mean(centered * centered, axis=-1, keepdims=True)
    return centered * lax.rsqrt(spread + epsilon) * gain_vec


def body(
    byte_embed,
    doc_lengths,
    key_mask,
    latents,
    gain_query,
    gain_bytes,
    gain_mlp,
    w_query,
    w_key,
    w_value,
    w_out,
    w_up,
    w_down,
    cotangent,
):
    doc_count, key_count, in_width = byte_embed.shape
    row_count, model_width = latents.shape
    qk_width = HEADS * QK_HEAD
    v_width = HEADS * V_HEAD
    score_scale = QK_HEAD ** (-0.5)
    positions = lax.axis_index("blk") * key_count + jnp.arange(key_count, dtype=jnp.int32)
    usable = (positions[None, :] < doc_lengths[:, None]) & (key_mask == 1)
    bias = jnp.where(usable, 0.0, masked_score).astype(jnp.float32)
    nb = lax.axis_size("blk")
    att, lse, key_rows, value_rows, _, query_all = forward(nb, byte_embed, bias, latents, gain_query, gain_bytes, w_query, w_key, w_value)
    normed_lat, latent_back = jax.vjp(layer_norm, latents, gain_query)
    normed_lat_low = normed_lat.astype(jnp.bfloat16)
    heads_q = query_all.reshape(LAT, HEADS, QK_HEAD)
    normed_bytes, bytes_back = jax.vjp(layer_norm, byte_embed.astype(jnp.float32), gain_bytes)
    flat_bytes = normed_bytes.astype(jnp.bfloat16).reshape(doc_count * key_count, in_width)
    key_rows = key_rows.reshape(doc_count, key_count, HEADS, QK_HEAD)
    value_rows = value_rows.reshape(doc_count, key_count, HEADS, V_HEAD)
    def masked_scores():
        scores = (
            jnp.einsum("qhd,nkhd->nhqk", heads_q, key_rows, preferred_element_type=jnp.float32)
            * score_scale
        )
        return jnp.where(usable[:, None, None, :], scores, masked_score)

    masked = masked_scores()
    attended_heads = att.reshape(doc_count, row_count, HEADS, V_HEAD)
    attended = attended_heads.reshape(doc_count * row_count, v_width)
    attended_low = attended.astype(jnp.bfloat16)
    branch = jnp.dot(attended_low, w_out, preferred_element_type=jnp.float32)
    middle = (latents[None] + branch.reshape(doc_count, row_count, model_width)).reshape(
        doc_count * row_count, model_width
    )
    normed_mid, mid_back = jax.vjp(layer_norm, middle, gain_mlp)
    normed_mid_low = normed_mid.astype(jnp.bfloat16)
    up_proj = jnp.dot(normed_mid_low, w_up, preferred_element_type=jnp.float32)
    activated, gelu_back = jax.vjp(jax.nn.gelu, up_proj)
    activated_low = activated.astype(jnp.bfloat16)
    latents_out = middle + jnp.dot(activated_low, w_down, preferred_element_type=jnp.float32)
    grad_out = cotangent.reshape(doc_count * row_count, model_width)
    grad_mlp = grad_out.astype(jnp.bfloat16)
    grad_w_down = jnp.dot(activated_low.T, grad_mlp, preferred_element_type=jnp.float32)
    grad_act = jnp.dot(grad_mlp, w_down.T, preferred_element_type=jnp.float32)
    (grad_up,) = gelu_back(grad_act)
    grad_up_low = grad_up.astype(jnp.bfloat16)
    grad_w_up = jnp.dot(normed_mid_low.T, grad_up_low, preferred_element_type=jnp.float32)
    grad_norm_mid = jnp.dot(grad_up_low, w_up.T, preferred_element_type=jnp.float32)
    grad_mid_norm, grad_gain_mlp = mid_back(grad_norm_mid)
    grad_middle = grad_out + grad_mid_norm
    grad_branch = grad_middle.astype(jnp.bfloat16)
    grad_w_out = jnp.dot(attended_low.T, grad_branch, preferred_element_type=jnp.float32)
    grad_attended = jnp.dot(grad_branch, w_out.T, preferred_element_type=jnp.float32)
    grad_attended = grad_attended.reshape(doc_count, row_count, HEADS, V_HEAD)
    grad_weighted = (
        grad_attended
        .astype(jnp.bfloat16)
        .reshape(doc_count, row_count, v_width)
    )
    grad_totals = -jnp.sum(grad_attended * attended_heads, axis=-1)
    grad_weighted_all = lax.all_gather(grad_weighted, "blk", axis=1, tiled=True).reshape(
        doc_count, LAT, HEADS, V_HEAD
    )
    grad_totals_all = lax.all_gather(grad_totals, "blk", axis=1, tiled=True).transpose(0, 2, 1)
    numerator = jnp.exp2(masked_scores()*LOG2E - lse[..., None])
    grad_numerator = jnp.einsum(
        "nqhd,nkhd->nhqk", grad_weighted_all, value_rows, preferred_element_type=jnp.float32
    )
    grad_scores = (numerator * (grad_numerator + grad_totals_all[..., None])).astype(jnp.bfloat16)
    grad_keys = (
        jnp.einsum("nhqk,qhd->nkhd", grad_scores, heads_q, preferred_element_type=jnp.float32)
        * score_scale
    )
    grad_keys = grad_keys.astype(jnp.bfloat16).reshape(doc_count * key_count, qk_width)
    grad_values = jnp.einsum(
        "nhqk,nqhd->nkhd",
        numerator.astype(jnp.bfloat16),
        grad_weighted_all,
        preferred_element_type=jnp.float32,
    )
    grad_values = grad_values.astype(jnp.bfloat16).reshape(doc_count * key_count, v_width)
    query_part = jnp.einsum(
        "nhqk,nkhd->qhd", grad_scores, key_rows, preferred_element_type=jnp.float32
    )
    grad_query_part = lax.psum_scatter(
        (query_part * score_scale)
        .reshape(lax.axis_size("blk") * row_count, qk_width)
        .astype(jnp.bfloat16),
        "blk",
        scatter_dimension=0,
        tiled=True,
    )
    grad_w_key = jnp.dot(flat_bytes.T, grad_keys, preferred_element_type=jnp.float32)
    grad_w_value = jnp.dot(flat_bytes.T, grad_values, preferred_element_type=jnp.float32)
    grad_normed_bytes = jnp.dot(grad_keys, w_key.T, preferred_element_type=jnp.float32)
    grad_normed_bytes = grad_normed_bytes + jnp.dot(
        grad_values, w_value.T, preferred_element_type=jnp.float32
    )
    byte_grad, grad_gain_bytes = bytes_back(
        grad_normed_bytes.reshape(doc_count, key_count, in_width)
    )
    direct = jnp.sum(grad_middle.reshape(doc_count, row_count, model_width), axis=0)
    direct_total, query_total = (
        lax.psum(direct.astype(jnp.bfloat16), "doc").astype(jnp.float32),
        lax.psum(grad_query_part, "doc").astype(jnp.float32),
    )
    grad_query_low = query_total.astype(jnp.bfloat16)
    lead_doc = (lax.axis_index("doc") == 0).astype(jnp.float32)
    grad_w_query = (
        jnp.dot(normed_lat_low.T, grad_query_low, preferred_element_type=jnp.float32) * lead_doc
    )
    grad_latent_norm, grad_gain_query = latent_back(
        jnp.dot(grad_query_low, w_query.T, preferred_element_type=jnp.float32)
    )
    latents_grad = direct_total + grad_latent_norm
    grad_gain_query = grad_gain_query * lead_doc
    summed = (
        lax.psum(grad_w_query.astype(jnp.bfloat16), "doc").astype(jnp.float32),
        lax.psum(grad_w_key.astype(jnp.bfloat16), "doc").astype(jnp.float32),
        lax.psum(grad_w_value.astype(jnp.bfloat16), "doc").astype(jnp.float32),
        lax.psum(grad_w_out.astype(jnp.bfloat16), "doc").astype(jnp.float32),
        lax.psum(grad_w_up.astype(jnp.bfloat16), "doc").astype(jnp.float32),
        lax.psum(grad_w_down.astype(jnp.bfloat16), "doc").astype(jnp.float32),
        lax.psum(grad_gain_query.astype(jnp.bfloat16), "doc").astype(jnp.float32),
        lax.psum(grad_gain_bytes.astype(jnp.bfloat16), "doc").astype(jnp.float32),
        lax.psum(grad_gain_mlp.astype(jnp.bfloat16), "doc").astype(jnp.float32),
    )
    sum_query, sum_key, sum_value, sum_out, sum_up, sum_down, sum_gq, sum_gb, sum_gm = summed
    shards = (
        lax.psum_scatter(
            sum_query.astype(jnp.bfloat16), "blk", scatter_dimension=0, tiled=True
        ).astype(jnp.float32),
        lax.psum_scatter(
            sum_key.astype(jnp.bfloat16), "blk", scatter_dimension=0, tiled=True
        ).astype(jnp.float32),
        lax.psum_scatter(
            sum_value.astype(jnp.bfloat16), "blk", scatter_dimension=0, tiled=True
        ).astype(jnp.float32),
        lax.psum_scatter(
            sum_out.astype(jnp.bfloat16), "blk", scatter_dimension=0, tiled=True
        ).astype(jnp.float32),
        lax.psum_scatter(
            sum_up.astype(jnp.bfloat16), "blk", scatter_dimension=0, tiled=True
        ).astype(jnp.float32),
        lax.psum_scatter(
            sum_down.astype(jnp.bfloat16), "blk", scatter_dimension=0, tiled=True
        ).astype(jnp.float32),
        lax.psum_scatter(
            sum_gq.astype(jnp.bfloat16), "blk", scatter_dimension=0, tiled=True
        ).astype(jnp.float32),
        lax.psum_scatter(
            sum_gb.astype(jnp.bfloat16), "blk", scatter_dimension=0, tiled=True
        ).astype(jnp.float32),
        lax.psum_scatter(
            sum_gm.astype(jnp.bfloat16), "blk", scatter_dimension=0, tiled=True
        ).astype(jnp.float32),
    )
    return (
        latents_out.reshape(doc_count, row_count, model_width),
        byte_grad,
        latents_grad,
        shards[6],
        shards[7],
        shards[8],
        shards[0],
        shards[1],
        shards[2],
        shards[3],
        shards[4],
        shards[5],
    )


def solution(mesh):
    in_specs = (
        P("doc", "blk", None),
        P("doc"),
        P("doc", "blk"),
        P("blk", None),
        P(),
        P(),
        P(),
        P(),
        P(),
        P(),
        P(),
        P(),
        P(),
        P("doc", "blk", None),
    )
    out_specs = (
        P("doc", "blk", None),
        P("doc", "blk", None),
        P("blk", None),
        P("blk"),
        P("blk"),
        P("blk"),
        P("blk", None),
        P("blk", None),
        P("blk", None),
        P("blk", None),
        P("blk", None),
        P("blk", None),
    )
    return jax.shard_map(body, mesh=mesh, in_specs=in_specs, out_specs=out_specs, check_vma=False)
```

```python
import functools
import math

import jax
import jax.numpy as jnp
from jax import lax
from jax.experimental import pallas as pl
from jax.experimental.pallas import tpu as pltpu
from jax.sharding import PartitionSpec as P

LAT = 256
HEADS = 8
QK_HEAD = 32
V_HEAD = 160
DQK = HEADS * QK_HEAD
DV = HEADS * V_HEAD
MESH = pl.DeviceIdType.MESH
F32 = jnp.float32
BF16 = jnp.bfloat16

epsilon = 1e-05
masked_score = -1e30
LOG2E = math.log2(math.e)
SCORE2 = QK_HEAD ** (-0.5) * LOG2E
SCORE_SCALE = QK_HEAD ** (-0.5)


def dot_nn(a, b):
    return jnp.dot(a, b, preferred_element_type=F32)


def dot_nt(a, b):
    return lax.dot_general(a, b, (((1,), (1,)), ((), ())), preferred_element_type=F32)


def norm_parts(v):
    centered = v - jnp.mean(v, axis=-1, keepdims=True)
    spread = jnp.mean(centered * centered, axis=-1, keepdims=True)
    inv = lax.rsqrt(spread + epsilon)
    return centered * inv, inv


def window(h):
    return V_HEAD * h // 128 * 128


def value_mask(h, rows):
    lane = lax.broadcasted_iota(jnp.int32, (rows, 256), 1) + window(h)
    keep = (lane >= V_HEAD * h) & (lane < V_HEAD * (h + 1))
    return jnp.where(keep, 1.0, 0.0).astype(BF16)


def query_mask(h, rows):
    lane = lax.broadcasted_iota(jnp.int32, (rows, DQK), 1)
    keep = (lane >= QK_HEAD * h) & (lane < QK_HEAD * (h + 1))
    return jnp.where(keep, 1.0, 0.0).astype(BF16)


def row_to_lanes(row):
    return jnp.transpose(jnp.broadcast_to(row, (128, row.shape[1])))


def wide(col, n):
    return jnp.concatenate([col] * (n // 128), axis=1) if n > 128 else col


def remote(src, dst, send, recv, doc, blk):
    return pltpu.make_async_remote_copy(
        src_ref=src, dst_ref=dst, send_sem=send, recv_sem=recv,
        device_id=(doc, blk), device_id_type=MESH,
    )


def forward_kernel(
    nb,
    x_ref, bias_ref, lat_ref, gq_ref, gb_ref, wq_ref, wk_ref, wv_ref,
    att_ref, lse_ref, k_ref, v_ref, nlw_ref, qall_ref,
    nl_cols, normed, qm, lloc, lmate, lz, acc, part, mate_in, rin, lin,
    q_s, q_r, n_s, n_r, l_s, l_r, mate_s, mate_r, rs_s, rs_r, ls_s, ls_r,
):
    D, kc, din = x_ref.shape
    rq = lat_ref.shape[0]
    pos = nb // 2
    doc, blk = lax.axis_index("doc"), lax.axis_index("blk")
    p, c = blk // 2, blk % 2
    mate = 2 * p + 1 - c
    barrier = pltpu.get_barrier_semaphore()
    for i in range(1, nb):
        pl.semaphore_signal(
            barrier, inc=1, device_id=(doc, lax.rem(blk + i, nb)), device_id_type=MESH
        )

    xhat, _ = norm_parts(lat_ref[...])
    nl = (xhat * gq_ref[...]).astype(BF16)
    step = nl.shape[1] // nb
    for j in range(nb):
        at = min(j * step // 128 * 128, nl.shape[1] - 256)
        nl_cols[j] = nl[:, at : at + 256]
    own = pl.ds(pl.multiple_of(blk * rq, rq), rq)
    qall_ref[own, :] = dot_nn(nl, wq_ref[...]).astype(BF16)
    pl.semaphore_wait(barrier, nb - 1)

    def q_copy(i, slot):
        return remote(
            qall_ref.at[own, :], qall_ref.at[slot, :], q_s.at[i - 1], q_r.at[i - 1],
            doc, lax.rem(blk + i, nb),
        )

    def n_copy(i, slot):
        peer = lax.rem(blk + i, nb)
        return remote(
            nl_cols.at[peer], nlw_ref.at[slot, :], n_s.at[i - 1], n_r.at[i - 1], doc, peer
        )

    for i in range(1, nb):
        q_copy(i, own).start()
    for i in range(1, nb):
        n_copy(i, own).start()
    nlw_ref[own, :] = nl_cols[blk]

    @pl.loop(0, D)
    def _(n):
        xh, _ = norm_parts(x_ref[n].astype(F32))
        normed[n] = (xh * gb_ref[...]).astype(BF16)
        k_ref[n] = dot_nn(normed[n], wk_ref[...]).astype(BF16)

    for i in range(1, nb):
        src = lax.rem(blk + nb - i, nb)
        q_copy(i, pl.ds(pl.multiple_of(src * rq, rq), rq)).wait_recv()
    for h in range(HEADS):
        qm[h] = qall_ref[...] * query_mask(h, LAT)

    @pl.loop(0, D)
    def _(n):
        bias = wide(row_to_lanes(bias_ref[pl.ds(n, 1), :]), LAT)
        kn = k_ref[n]
        rows = []
        for h in range(HEADS):
            s = dot_nt(kn, qm[h]) * SCORE2 + bias
            top = jnp.max(s, axis=0, keepdims=True)
            tot = jnp.sum(jnp.exp2(s - top), axis=0, keepdims=True)
            rows.append(top + jnp.log(tot) * LOG2E)
        lloc[n] = jnp.concatenate(rows, axis=0)

    half = D // 2
    mine, other = pl.ds(c * half, half), pl.ds((1 - c) * half, half)

    def merge(a, b):
        top = jnp.maximum(a, b)
        return top + jnp.log(jnp.exp2(a - top) + jnp.exp2(b - top)) * LOG2E

    first = remote(lloc.at[other], lmate, l_s.at[0], l_r.at[0], doc, mate)
    first.start()

    def values(lo, hi):
        @pl.loop(lo, hi)
        def _(n):
            v_ref[n] = dot_nn(normed[n], wv_ref[...]).astype(BF16)

    values(0, D // 4)
    first.wait_recv()
    lz[p] = merge(lloc[mine], lmate[...])

    def z_copy(i, slot):
        return remote(
            lz.at[p], lz.at[slot], l_s.at[i], l_r.at[i],
            doc, 2 * lax.rem(p + i, pos) + c,
        )

    for i in range(1, pos):
        z_copy(i, p).start()
    values(D // 4, 3 * D // 4)
    for i in range(1, pos):
        z_copy(i, lax.rem(p + pos - i, pos)).wait_recv()
    total = lz[0]
    for i in range(1, pos):
        total = merge(total, lz[i])
    lse_ref[mine] = total
    last = remote(lse_ref.at[mine], lse_ref.at[mine], l_s.at[pos], l_r.at[pos], doc, mate)
    last.start()
    values(3 * D // 4, D)
    remote(
        lse_ref.at[other], lse_ref.at[other], l_s.at[pos], l_r.at[pos], doc, mate
    ).wait_recv()

    def mate_copy(n):
        return remote(
            part.at[n, 1 - c], mate_in.at[n], mate_s.at[n], mate_r.at[n], doc, mate
        )

    def right_copy(n, j, src):
        return remote(
            src, rin.at[n, j], rs_s.at[n, j], rs_r.at[n, j],
            doc, 2 * jnp.minimum(p + 1, pos - 1) + c,
        )

    def left_copy(n, j, src):
        return remote(
            src, lin.at[n, j], ls_s.at[n, j], ls_r.at[n, j],
            doc, 2 * jnp.maximum(p - 1, 0) + c,
        )

    def chip_sum(n):
        mate_copy(n).wait_recv()
        for j in range(pos):
            both = part[n, c, j].astype(F32) + mate_in[n, j].astype(F32)
            part[n, c, j] = both.astype(BF16)

            @pl.when((p == 0) & (j > 0))
            def _():
                right_copy(n, j, part.at[n, c, j]).start()

            @pl.when((p == pos - 1) & (j < pos - 1))
            def _():
                left_copy(n, j, part.at[n, c, j]).start()

    @pl.loop(0, D)
    def _(n):
        logs = lse_ref[n]
        logs_t = jnp.transpose(jnp.concatenate([logs] * (128 // HEADS), axis=0))
        bias = bias_ref[pl.ds(n, 1), :]
        kn = k_ref[n]
        acc[...] = jnp.zeros_like(acc)
        for h in range(HEADS):
            s = dot_nt(qm[h], kn) * SCORE2 + bias
            prob = jnp.exp2(s - logs_t[:, h : h + 1]).astype(BF16)
            cols = slice(window(h), window(h) + 256)
            acc[:, cols] += dot_nn(prob, v_ref[n, :, cols] * value_mask(h, kc))
        for j in range(nb):
            part[n, j % 2, j // 2] = acc[rq * j : rq * (j + 1), :].astype(BF16)
        mate_copy(n).start()

        @pl.when(n > 0)
        def _():
            chip_sum(n - 1)

    chip_sum(D - 1)

    def from_left(n):
        for j in range(1, pos):
            @pl.when(j >= p)
            def _():
                right_copy(n, j, part.at[n, c, j]).wait_recv()

            @pl.when(j > p)
            def _():
                both = rin[n, j].astype(F32) + part[n, c, j].astype(F32)
                part[n, c, j] = both.astype(BF16)
                right_copy(n, j, part.at[n, c, j]).start()

    def from_right(n):
        for j in range(pos - 2, -1, -1):
            @pl.when(j <= p)
            def _():
                left_copy(n, j, part.at[n, c, j]).wait_recv()

            @pl.when(j < p)
            def _():
                both = lin[n, j].astype(F32) + part[n, c, j].astype(F32)
                part[n, c, j] = both.astype(BF16)
                left_copy(n, j, part.at[n, c, j]).start()

    def finish(n):
        att_ref[n] = part[n, c, p].astype(F32)

        @pl.when(p > 0)
        def _():
            att_ref[n] += rin[n, p].astype(F32)

        @pl.when(p < pos - 1)
        def _():
            att_ref[n] += lin[n, p].astype(F32)

    @pl.loop(0, D + pos - 1)
    def _(t):
        right_n, left_n, done_n = t - p, t - (pos - 1 - p), t - (pos - 1)

        @pl.when((p > 0) & (right_n >= 0) & (right_n < D))
        def _():
            from_left(right_n)

        @pl.when((p < pos - 1) & (left_n >= 0) & (left_n < D))
        def _():
            from_right(left_n)

        @pl.when(done_n >= 0)
        def _():
            finish(done_n)

    for i in range(1, nb):
        src = lax.rem(blk + nb - i, nb)
        n_copy(i, pl.ds(pl.multiple_of(src * rq, rq), rq)).wait_recv()

    for i in range(1, nb):
        q_copy(i, own).wait_send()
        n_copy(i, own).wait_send()
    first.wait_send()
    for i in range(1, pos):
        z_copy(i, p).wait_send()
    last.wait_send()

    @pl.loop(0, D)
    def _(n):
        mate_copy(n).wait_send()
        for j in range(pos):
            @pl.when((j > p) & (p < pos - 1))
            def _():
                right_copy(n, j, part.at[n, c, j]).wait_send()

            @pl.when((j < p) & (p > 0))
            def _():
                left_copy(n, j, part.at[n, c, j]).wait_send()


def forward(nb, byte_embed, bias, latents, gain_query, gain_bytes, w_query, w_key, w_value):
    D, kc, din = byte_embed.shape
    rq, dl = latents.shape
    pos = nb // 2
    vmem = pl.BlockSpec(memory_space=pltpu.VMEM)
    dma = pltpu.SemaphoreType.DMA
    return pl.pallas_call(
        functools.partial(forward_kernel, nb),
        out_shape=(
            jax.ShapeDtypeStruct((D, rq, DV), F32),
            jax.ShapeDtypeStruct((D, HEADS, LAT), F32),
            jax.ShapeDtypeStruct((D, kc, DQK), BF16),
            jax.ShapeDtypeStruct((D, kc, DV), BF16),
            jax.ShapeDtypeStruct((LAT, 256), BF16),
            jax.ShapeDtypeStruct((LAT, DQK), BF16),
        ),
        in_specs=[vmem] * 8,
        out_specs=(vmem,) * 6,
        scratch_shapes=[
            pltpu.VMEM((nb, rq, 256), BF16),
            pltpu.VMEM((D, kc, din), BF16),
            pltpu.VMEM((HEADS, LAT, DQK), BF16),
            pltpu.VMEM((D, HEADS, LAT), F32),
            pltpu.VMEM((D // 2, HEADS, LAT), F32),
            pltpu.VMEM((pos, D // 2, HEADS, LAT), F32),
            pltpu.VMEM((LAT, DV), F32),
            pltpu.VMEM((D, 2, pos, rq, DV), BF16),
            pltpu.VMEM((D, pos, rq, DV), BF16),
            pltpu.VMEM((D, pos, rq, DV), BF16),
            pltpu.VMEM((D, pos, rq, DV), BF16),
            dma((nb - 1,)), dma((nb - 1,)), dma((nb - 1,)), dma((nb - 1,)),
            dma((pos + 1,)), dma((pos + 1,)),
            dma((D,)), dma((D,)),
            dma((D, pos)), dma((D, pos)), dma((D, pos)), dma((D, pos)),
        ],
        compiler_params=pltpu.CompilerParams(
            collective_id=0, has_side_effects=True, vmem_limit_bytes=56 * 2**20
        ),
        name="forward",
    )(
        byte_embed, bias, latents, gain_query.reshape(1, -1), gain_bytes.reshape(1, -1),
        w_query, w_key, w_value,
    )


def gelu_parts(u):
    k = math.sqrt(2.0 / math.pi)
    sq = u * u
    t = jnp.tanh(k * u * (1.0 + 0.044715 * sq))
    value = 0.5 * u * (1.0 + t)
    slope = 0.5 * (1.0 + t) + 0.5 * k * u * (1.0 - t * t) * (1.0 + 3 * 0.044715 * sq)
    return value, slope


def mlp_kernel(
    nb, half,
    att_ref, lat_ref, gm_ref, wo_ref, wu_ref, wd_ref, cot_ref,
    out_ref, ga_ref, delta_ref, wg_ref, direct_ref, gain_ref,
    mid, xhat, slope, low_t, gmid,
):
    D, rq, dv = att_ref.shape
    rows = D * rq
    dl = lat_ref.shape[1]
    step = dl // nb
    blocks = dl // 256

    def weight_grad(m, left, right_ref_cols):
        low_t[...] = jnp.transpose(left)
        for b in range(blocks):
            r = dot_nn(low_t[...], right_ref_cols(b)).astype(BF16)
            for i in range(2):
                col = 256 * b + 128 * i
                at, lane = col // half, col % half
                for k in range(nb):
                    wg_ref[m, k, at * step : (at + 1) * step, lane : lane + 128] = r[
                        k * step : (k + 1) * step, 128 * i : 128 * (i + 1)
                    ]

    att = att_ref[...].reshape(rows, dv)
    att_low = att.astype(BF16)
    lat = lat_ref[...]
    mid[...] = dot_nn(att_low, wo_ref[...]) + jnp.concatenate([lat] * D, axis=0)
    xh, inv = norm_parts(mid[...])
    xhat[...] = xh
    nm = (xh * gm_ref[...]).astype(BF16)
    up = dot_nn(nm, wu_ref[...])
    act, sl = gelu_parts(up)
    slope[...] = sl
    act_low = act.astype(BF16)
    out_ref[...] = (mid[...] + dot_nn(act_low, wd_ref[...])).reshape(D, rq, dl)
    cot = cot_ref[...].reshape(rows, dl)
    gm = cot.astype(BF16)
    weight_grad(0, act_low, lambda b: gm[:, 256 * b : 256 * (b + 1)])
    g_up = (dot_nt(gm, wd_ref[...]) * slope[...]).astype(BF16)
    weight_grad(1, nm, lambda b: g_up[:, 256 * b : 256 * (b + 1)])
    g_nm = dot_nt(g_up, wu_ref[...])
    xh = xhat[...]
    gain_ref[...] = jnp.sum(g_nm * xh, axis=0, keepdims=True)
    dxh = g_nm * gm_ref[...]
    dmid = inv * (
        dxh
        - jnp.mean(dxh, axis=-1, keepdims=True)
        - xh * jnp.mean(dxh * xh, axis=-1, keepdims=True)
    )
    gmid[...] = cot + dmid
    direct = gmid[0:rq, :]
    for n in range(1, D):
        direct = direct + gmid[n * rq : (n + 1) * rq, :]
    direct_ref[...] = direct.astype(BF16)
    gb = gmid[...].astype(BF16)
    weight_grad(2, att_low, lambda b: gb[:, 256 * b : 256 * (b + 1)])
    ga = dot_nt(gb, wo_ref[...])
    ga_ref[...] = ga.astype(BF16).reshape(D, rq, dv)
    prod = ga * att
    lane = lax.broadcasted_iota(jnp.int32, (rq, 128), 1)
    delta = jnp.zeros((rq, 128), F32)
    for h in range(HEADS):
        cols = lax.broadcasted_iota(jnp.int32, (rows, 256), 1) + window(h)
        keep = (cols >= V_HEAD * h) & (cols < V_HEAD * (h + 1))
        one = jnp.sum(
            jnp.where(keep, prod[:, window(h) : window(h) + 256], 0.0), axis=1, keepdims=True
        )
        for n in range(D):
            delta = delta + jnp.where(lane == n * HEADS + h, one[n * rq : (n + 1) * rq], 0.0)
    delta_ref[...] = delta


def owner_rows(total, docs):
    return -(-total // (16 * docs)) * 16


def mlp(nb, nd, att, latents, gain_mlp, w_out, w_up, w_down, cotangent):
    D, rq, dv = att.shape
    dl = latents.shape[1]
    half = dl // 2
    rows = owner_rows(2 * dl // nb, nd) * nd
    vmem = pl.BlockSpec(memory_space=pltpu.VMEM)
    return pl.pallas_call(
        functools.partial(mlp_kernel, nb, half),
        out_shape=(
            jax.ShapeDtypeStruct((D, rq, dl), F32),
            jax.ShapeDtypeStruct((D, rq, dv), BF16),
            jax.ShapeDtypeStruct((rq, 128), F32),
            jax.ShapeDtypeStruct((3, nb, rows, half), BF16),
            jax.ShapeDtypeStruct((rq, dl), BF16),
            jax.ShapeDtypeStruct((1, dl), F32),
        ),
        in_specs=[vmem] * 7,
        out_specs=(vmem,) * 6,
        scratch_shapes=[
            pltpu.VMEM((D * rq, dl), F32),
            pltpu.VMEM((D * rq, dl), F32),
            pltpu.VMEM((D * rq, dl), F32),
            pltpu.VMEM((dl, D * rq), BF16),
            pltpu.VMEM((D * rq, dl), F32),
        ],
        compiler_params=pltpu.CompilerParams(vmem_limit_bytes=60 * 2**20),
        name="feed_forward",
    )(att, latents, gain_mlp.reshape(1, -1), w_out, w_up, w_down, cotangent)


class ShardSums:
    def __init__(self, doc, blk, nd, nb, count, unit, own, mate_in, inbox, rin, lin, out, sems):
        self.doc, self.p, self.c = doc, blk // 2, blk % 2
        self.nd, self.pos, self.count, self.unit = nd, nb // 2, count, unit
        self.bits = nd.bit_length() - 1
        self.own, self.mate_in, self.inbox = own, mate_in, inbox
        self.rin, self.lin, self.out = rin, lin, out
        (
            self.mate_s, self.mate_r, self.own_s, self.in_s, self.in_r,
            self.right_s, self.right_r, self.left_s, self.left_r, self.out_s, self.out_r,
        ) = sems
        self.lag = self.bits + self.pos - 1

    def weight(self, s, k):
        b = (s + k) % self.bits
        return 1 + b * (b + 1) // 2

    def my_bit(self, w):
        return (self.doc // w) % 2

    def quarter(self, s, k, i, sent):
        q = 0
        for r in range(k):
            w = self.weight(s, r)
            q = q + self.my_bit(w) * w
        w = self.weight(s, k)
        mine = self.my_bit(w)
        q = q + ((1 - mine) if sent else mine) * w
        for r in range(k + 1, self.bits):
            q = q + ((i >> (r - k - 1)) & 1) * self.weight(s, r)
        return q

    def width(self, k):
        return 2 ** (self.bits - 1 - k)

    def slot(self, k, i):
        return sum(self.width(r) for r in range(k)) + i

    def rows(self, q):
        return pl.ds(pl.multiple_of(q * self.unit, self.unit), self.unit)

    def halving(self, s, k, i):
        w = self.weight(s, k)
        peer = self.doc + w * (1 - 2 * self.my_bit(w))
        slot = self.slot(k, i)
        return remote(
            self.own.at[s, self.rows(self.quarter(s, k, i, True)), :], self.inbox.at[s, slot],
            self.in_s.at[s, slot], self.in_r.at[s, slot], peer, 2 * self.p + self.c,
        )

    def right(self, s):
        return remote(
            self.own.at[s, self.rows(self.doc), :], self.rin.at[s],
            self.right_s.at[s], self.right_r.at[s],
            self.doc, 2 * jnp.minimum(self.p + 1, self.pos - 1) + self.c,
        )

    def left(self, s):
        return remote(
            self.own.at[s, self.rows(self.doc), :], self.lin.at[s],
            self.left_s.at[s], self.left_r.at[s],
            self.doc, 2 * jnp.maximum(self.p - 1, 0) + self.c,
        )

    def share(self, m, i):
        return remote(
            self.out.at[m, self.rows(self.doc), :], self.out.at[m, self.rows(self.doc), :],
            self.out_s.at[m, i - 1], self.out_r.at[m, i - 1],
            lax.rem(self.doc + i, self.nd), 2 * self.p + self.c,
        )

    def shared(self, m, i):
        src = lax.rem(self.doc + self.nd - i, self.nd)
        return remote(
            self.out.at[m, self.rows(src), :], self.out.at[m, self.rows(src), :],
            self.out_s.at[m, i - 1], self.out_r.at[m, i - 1], src, 2 * self.p + self.c,
        )

    def add(self, s, q, other):
        rows = self.rows(q)
        self.own[s, rows, :] = (
            self.own[s, rows, :].astype(F32) + other.astype(F32)
        ).astype(BF16)

    def begin(self, s, mate_copy, own_copy):
        own_copy(s).wait()
        mate_copy(s).wait_recv()
        for q in range(self.nd):
            self.add(s, q, self.mate_in[s, self.unit * q : self.unit * (q + 1), :])
        for i in range(self.width(0)):
            self.halving(s, 0, i).start()

    def halve(self, s, k):
        for i in range(self.width(k - 1)):
            self.halving(s, k - 1, i).wait_recv()
            self.add(s, self.quarter(s, k - 1, i, False), self.inbox[s, self.slot(k - 1, i)])
        if k < self.bits:
            for i in range(self.width(k)):
                self.halving(s, k, i).start()
            return
        j = s % self.pos

        @pl.when((self.p == 0) & (j > 0))
        def _():
            self.right(s).start()

        @pl.when((self.p == self.pos - 1) & (j < self.pos - 1))
        def _():
            self.left(s).start()

    def from_left(self, s):
        j = s % self.pos

        @pl.when(j >= self.p)
        def _():
            self.right(s).wait_recv()

        @pl.when(j > self.p)
        def _():
            self.add(s, self.doc, self.rin[s])
            self.right(s).start()

    def from_right(self, s):
        j = s % self.pos

        @pl.when(j <= self.p)
        def _():
            self.left(s).wait_recv()

        @pl.when(j < self.p)
        def _():
            self.add(s, self.doc, self.lin[s])
            self.left(s).start()

    def finish(self, s):
        @pl.when(s % self.pos == self.p)
        def _():
            m = s // self.pos

            @pl.when(self.p > 0)
            def _():
                self.add(s, self.doc, self.rin[s])

            @pl.when(self.p < self.pos - 1)
            def _():
                self.add(s, self.doc, self.lin[s])

            self.out[m, self.rows(self.doc), :] = self.own[s, self.rows(self.doc), :]
            for i in range(1, self.nd):
                self.share(m, i).start()

    def step(self, t, mate_copy, own_copy):
        def at(s, when, run):
            @pl.when((s >= 0) & (s < self.count) & when)
            def _():
                run(s)

        at(t, True, lambda s: self.begin(s, mate_copy, own_copy))
        for k in range(1, self.bits + 1):
            at(t - k, True, functools.partial(self.halve, k=k))
        base = t - self.bits
        at(base - self.p, self.p > 0, self.from_left)
        at(base - (self.pos - 1 - self.p), self.p < self.pos - 1, self.from_right)
        at(base - (self.pos - 1), True, self.finish)

    def drain(self, mate_copy):
        for m in range(self.count // self.pos):
            for i in range(1, self.nd):
                self.shared(m, i).wait_recv()
                self.share(m, i).wait_send()

        @pl.loop(0, self.count)
        def _(s):
            mate_copy(s).wait_send()
            for k in range(self.bits):
                for i in range(self.width(k)):
                    self.halving(s, k, i).wait_send()
            j = s % self.pos

            @pl.when((j > self.p) & (self.p < self.pos - 1))
            def _():
                self.right(s).wait_send()

            @pl.when((j < self.p) & (self.p > 0))
            def _():
                self.left(s).wait_send()


def shard_sum_scratch(nd, nb, count, unit, width):
    dma = pltpu.SemaphoreType.DMA
    arrays = count // (nb // 2)
    return [
        pltpu.VMEM((count, unit * nd, width), BF16),
        pltpu.VMEM((count, unit * nd, width), BF16),
        pltpu.VMEM((count, nd - 1, unit, width), BF16),
        pltpu.VMEM((count, unit, width), BF16),
        pltpu.VMEM((count, unit, width), BF16),
        dma((count,)), dma((count,)), dma((count,)),
        dma((count, nd - 1)), dma((count, nd - 1)),
        dma((count,)), dma((count,)), dma((count,)), dma((count,)),
        dma((arrays, nd - 1)), dma((arrays, nd - 1)),
    ]


def backward_kernel(nb, nd, wunit, vunit, *refs):
    (
        x_hbm, k_hbm, v_hbm, wg_hbm, bias_ref, gb_ref, wk_ref, wv_ref, qall_ref, lse_ref,
        ga_ref, delta_ref, direct_ref, gain_ref,
    ) = refs[:14]
    bg_hbm, wsum_ref, vsum_ref, dsum_ref, gq_ref, gains_ref = refs[14:20]
    wscr, vscr = refs[20:36], refs[36:52]
    (
        x_ref, k_ref, v_ref, ga_all, delta_all, delta_t, qm, ds_all, gv_acc, gq_acc,
        kv_acc, kv_part, gain_acc, bg_buf, dir_in, misc_out, misc_in, misc2_out, misc2_in, gq_own,
        load_s, bg_s, ar_s, ar_r, al_s, al_r, am_s, am_r, d_s, d_r, dir_s, dir_r,
        m1_s, m1_r, m2_s, m2_r, m3_s, m3_r,
    ) = refs[52:]
    D, kc, din = x_ref.shape
    rq = ga_ref.shape[1]
    pos = nb // 2
    doc, blk = lax.axis_index("doc"), lax.axis_index("blk")
    p, c = blk // 2, blk % 2
    mate = 2 * p + 1 - c

    barrier = pltpu.get_barrier_semaphore()
    for i in range(1, nb):
        pl.semaphore_signal(
            barrier, inc=1, device_id=(doc, lax.rem(blk + i, nb)), device_id_type=MESH
        )
    for i in range(1, nd):
        pl.semaphore_signal(
            barrier, inc=1, device_id=(lax.rem(doc + i, nd), blk), device_id_type=MESH
        )

    loads = [
        pltpu.make_async_copy(src, dst, load_s.at[i])
        for i, (src, dst) in enumerate(((k_hbm, k_ref), (v_hbm, v_ref), (x_hbm, x_ref)))
    ]
    for load in loads:
        load.start()

    weights = ShardSums(
        doc, blk, nd, nb, 3 * pos, wunit, *wscr[:5], wsum_ref, wscr[5:]
    )
    values = ShardSums(doc, blk, nd, nb, pos, vunit, *vscr[:5], vsum_ref, vscr[5:])

    def w_mate(s):
        return remote(
            wg_hbm.at[s // pos, 2 * (s % pos) + 1 - c], weights.mate_in.at[s],
            weights.mate_s.at[s], weights.mate_r.at[s], doc, mate,
        )

    def w_own(s):
        return pltpu.make_async_copy(
            wg_hbm.at[s // pos, 2 * (s % pos) + c], weights.own.at[s], weights.own_s.at[s]
        )

    def v_mate(s):
        return remote(
            kv_part.at[2 * s + 1 - c], values.mate_in.at[s],
            values.mate_s.at[s], values.mate_r.at[s], doc, mate,
        )

    def v_own(s):
        return pltpu.make_async_copy(
            kv_part.at[2 * s + c], values.own.at[s], values.own_s.at[s]
        )

    def chunk(j, core):
        return pl.ds(pl.multiple_of((2 * j + core) * rq, rq), rq)

    def right_copy(n, hop, j):
        rows = ga_all.at[n, chunk(j, c), :]
        return remote(
            rows, rows, ar_s.at[n, hop], ar_r.at[n, hop],
            doc, 2 * jnp.minimum(p + 1, pos - 1) + c,
        )

    def left_copy(n, hop, j):
        rows = ga_all.at[n, chunk(j, c), :]
        return remote(
            rows, rows, al_s.at[n, hop], al_r.at[n, hop],
            doc, 2 * jnp.maximum(p - 1, 0) + c,
        )

    def mate_copy(n, j, core):
        rows = ga_all.at[n, chunk(j, core), :]
        return remote(rows, rows, am_s.at[n, j], am_r.at[n, j], doc, mate)

    own_rows = pl.ds(pl.multiple_of(blk * rq, rq), rq)

    def delta_copy(i, rows):
        return remote(
            delta_all.at[rows, :], delta_all.at[rows, :], d_s.at[i - 1], d_r.at[i - 1],
            doc, lax.rem(blk + i, nb),
        )

    def direct_copy(i):
        return remote(
            direct_ref, dir_in.at[i - 1], dir_s.at[i - 1], dir_r.at[i - 1],
            lax.rem(doc + i, nd), blk,
        )

    for h in range(HEADS):
        qm[h * LAT : (h + 1) * LAT, :] = qall_ref[...] * query_mask(h, LAT)
    gq_acc[...] = jnp.zeros_like(gq_acc)
    kv_acc[...] = jnp.zeros_like(kv_acc)
    gain_acc[...] = jnp.zeros_like(gain_acc)
    delta_all[own_rows, :] = delta_ref[...]
    for n in range(D):
        ga_all[n, own_rows, :] = ga_ref[n]

    pl.semaphore_wait(barrier, nb - 1 + nd - 1)
    for i in range(1, nb):
        delta_copy(i, own_rows).start()

    @pl.loop(0, D)
    def _(n):
        @pl.when(p < pos - 1)
        def _():
            right_copy(n, 0, p).start()

        @pl.when(p > 0)
        def _():
            left_copy(n, 0, p).start()

        mate_copy(n, p, c).start()

    @pl.loop(0, weights.count)
    def _(s):
        w_own(s).start()
        w_mate(s).start()

    for i in range(1, nd):
        direct_copy(i).start()

    def forward_chunks(n, hop):
        j = p - 1 - hop

        @pl.when(j >= 0)
        def _():
            right_copy(n, hop, j).wait_recv()
            if hop + 1 < pos - 1:
                @pl.when(p < pos - 1)
                def _():
                    right_copy(n, hop + 1, j).start()

            mate_copy(n, j, c).start()

        i = p + 1 + hop

        @pl.when(i < pos)
        def _():
            left_copy(n, hop, i).wait_recv()
            if hop + 1 < pos - 1:
                @pl.when(p > 0)
                def _():
                    left_copy(n, hop + 1, i).start()

            mate_copy(n, i, c).start()

    def bytes_back(n):
        for j in range(pos):
            mate_copy(n, j, 1 - c).wait_recv()
        bias = wide(row_to_lanes(bias_ref[pl.ds(n, 1), :]), LAT)
        logs, deltas = lse_ref[n], delta_t[n]
        kn = k_ref[n]
        kt = jnp.transpose(kn)
        gv_acc[...] = jnp.zeros_like(gv_acc)
        for h in range(HEADS):
            cols = slice(window(h), window(h) + 256)
            gah = ga_all[n, :, cols] * value_mask(h, LAT)
            s = dot_nt(kn, qm[h * LAT : (h + 1) * LAT, :]) * SCORE2 + bias
            prob = jnp.exp2(s - logs[h : h + 1, :])
            dprob = dot_nt(v_ref[n, :, cols], gah)
            ds = (prob * (dprob - deltas[h : h + 1, :])).astype(BF16)
            ds_all[:, h * LAT : (h + 1) * LAT] = ds
            gv_acc[:, cols] += dot_nn(prob.astype(BF16), gah)
            head = slice(QK_HEAD * h, QK_HEAD * (h + 1))
            gq_acc[head, :] += dot_nn(kt[head, :], ds)
        gk = (dot_nn(ds_all[...], qm[...]) * SCORE_SCALE).astype(BF16)
        gv = gv_acc[...].astype(BF16)
        gx = dot_nt(gv, wv_ref[...]) + dot_nt(gk, wk_ref[...])
        xh, inv = norm_parts(x_ref[n].astype(F32))
        gain_acc[...] += jnp.sum(gx * xh, axis=0, keepdims=True)
        dxh = gx * gb_ref[...]
        slot = lax.rem(n, 2)

        @pl.when(n >= 2)
        def _():
            pltpu.make_async_copy(bg_buf.at[slot], bg_hbm.at[n - 2], bg_s.at[slot]).wait()

        bg_buf[slot] = inv * (
            dxh
            - jnp.mean(dxh, axis=-1, keepdims=True)
            - xh * jnp.mean(dxh * xh, axis=-1, keepdims=True)
        )
        pltpu.make_async_copy(bg_buf.at[slot], bg_hbm.at[n], bg_s.at[slot]).start()
        normed_t = jnp.transpose((xh * gb_ref[...]).astype(BF16))
        kv_acc[:, 0:DV] += dot_nn(normed_t, gv)
        kv_acc[:, DV : DV + DQK] += dot_nn(normed_t, gk)

    @pl.loop(0, D + pos)
    def _(t):
        for hop in range(pos - 1):
            @pl.when((t >= hop) & (t - hop < D))
            def _():
                forward_chunks(t - hop, hop)

        weights.step(t, w_mate, w_own)

        @pl.when(t == pos)
        def _():
            for i in range(1, nb):
                src = lax.rem(blk + nb - i, nb)
                delta_copy(i, pl.ds(pl.multiple_of(src * rq, rq), rq)).wait_recv()
            turned = jnp.transpose(delta_all[...])
            for n in range(D):
                delta_t[n] = turned[n * HEADS : (n + 1) * HEADS, :]
            for load in loads:
                load.wait()

        @pl.when(t >= pos)
        def _():
            bytes_back(t - pos)

    gq_rows = (jnp.transpose(gq_acc[...]) * SCORE_SCALE).astype(BF16)
    gains = jnp.concatenate([gain_ref[...], gain_acc[...]], axis=1)
    rows8 = [gains[:, 256 * i : 256 * (i + 1)] for i in range(8)]
    gains8 = jnp.concatenate(rows8 + [jnp.zeros((8, 256), F32)], axis=0).astype(BF16)
    for j in range(nb):
        misc_out[j, 0:rq] = gq_rows[j * rq : (j + 1) * rq, :]
        misc_out[j, rq : rq + 16] = gains8

    def misc1(i, slot):
        peer = lax.rem(blk + i, nb)
        return remote(
            misc_out.at[peer], misc_in.at[slot], m1_s.at[i - 1], m1_r.at[i - 1], doc, peer
        )

    for i in range(1, nb):
        misc1(i, blk).start()

    step = din // nb
    for k in range(nb):
        rows = slice(k * step, (k + 1) * step)
        kv_part[k, 0:step, :] = kv_acc[rows, 0:din].astype(BF16)
        kv_part[k, step : 2 * step, :] = kv_acc[rows, din : 2 * din].astype(BF16)

    @pl.loop(0, values.count)
    def _(s):
        v_own(s).start()
        v_mate(s).start()

    misc_in[blk] = misc_out[blk]
    for i in range(1, nb):
        misc1(i, lax.rem(blk + nb - i, nb)).wait_recv()
    total = misc_in[0].astype(F32)
    for i in range(1, nb):
        total = total + misc_in[i].astype(F32)
    misc2_out[...] = total.astype(BF16)

    def misc2(i, slot):
        return remote(
            misc2_out, misc2_in.at[slot], m2_s.at[i - 1], m2_r.at[i - 1],
            lax.rem(doc + i, nd), blk,
        )

    for i in range(1, nd):
        misc2(i, doc).start()
    misc2_in[doc] = misc2_out[...]

    first, last = D + pos, weights.count + weights.lag
    last = max(last, first + values.count + values.lag)

    def misc3(i, rows):
        return remote(
            gq_ref.at[rows, :], gq_ref.at[rows, :], m3_s.at[i - 1], m3_r.at[i - 1],
            doc, lax.rem(blk + i, nb),
        )

    @pl.loop(first, last)
    def _(t):
        weights.step(t, w_mate, w_own)
        values.step(t - first, v_mate, v_own)

        @pl.when(t == first + 2)
        def _():
            for i in range(1, nd):
                misc2(i, lax.rem(doc + nd - i, nd)).wait_recv()
            total = misc2_in[0].astype(F32)
            for i in range(1, nd):
                total = total + misc2_in[i].astype(F32)
            gains_ref[...] = total[rq : rq + 8, :]
            gq_ref[own_rows, :] = total[0:rq].astype(BF16)
            for i in range(1, nb):
                misc3(i, own_rows).start()

    for i in range(1, nb):
        src = lax.rem(blk + nb - i, nb)
        misc3(i, pl.ds(pl.multiple_of(src * rq, rq), rq)).wait_recv()

    total = direct_ref[...].astype(F32)
    for i in range(1, nd):
        direct_copy(i).wait_recv()
        total = total + dir_in[i - 1].astype(F32)
    dsum_ref[...] = total

    for n in range(D - 2, D):
        pltpu.make_async_copy(bg_buf.at[n % 2], bg_hbm.at[n], bg_s.at[n % 2]).wait()
    weights.drain(w_mate)
    values.drain(v_mate)
    for i in range(1, nb):
        delta_copy(i, own_rows).wait_send()
        misc1(i, blk).wait_send()
        misc3(i, own_rows).wait_send()
    for i in range(1, nd):
        direct_copy(i).wait_send()
        misc2(i, doc).wait_send()

    @pl.loop(0, D)
    def _(n):
        mate_copy(n, p, c).wait_send()

        @pl.when(p < pos - 1)
        def _():
            right_copy(n, 0, p).wait_send()

        @pl.when(p > 0)
        def _():
            left_copy(n, 0, p).wait_send()

        for hop in range(pos - 1):
            j = p - 1 - hop

            @pl.when(j >= 0)
            def _():
                mate_copy(n, j, c).wait_send()
                if hop + 1 < pos - 1:
                    @pl.when(p < pos - 1)
                    def _():
                        right_copy(n, hop + 1, j).wait_send()

            i = p + 1 + hop

            @pl.when(i < pos)
            def _():
                mate_copy(n, i, c).wait_send()
                if hop + 1 < pos - 1:
                    @pl.when(p > 0)
                    def _():
                        left_copy(n, hop + 1, i).wait_send()


def backward(
    nb, nd, byte_embed, keys, values, wgrads, bias, gain_bytes, w_key, w_value, queries, lse,
    ga, delta, direct, gain_part,
):
    D, kc, din = byte_embed.shape
    rq, dl = direct.shape
    pos = nb // 2
    wunit, vunit = owner_rows(2 * dl // nb, nd), owner_rows(2 * din // nb, nd)
    whalf = dl // 2
    vmem = pl.BlockSpec(memory_space=pltpu.VMEM)
    anywhere = pl.BlockSpec(memory_space=pl.ANY)
    dma = pltpu.SemaphoreType.DMA
    scratch = (
        shard_sum_scratch(nd, nb, 3 * pos, wunit, whalf)
        + shard_sum_scratch(nd, nb, pos, vunit, din)
        + [
            pltpu.VMEM((D, kc, din), BF16),
            pltpu.VMEM((D, kc, DQK), BF16),
            pltpu.VMEM((D, kc, DV), BF16),
            pltpu.VMEM((D, LAT, DV), BF16),
            pltpu.VMEM((LAT, 128), F32),
            pltpu.VMEM((D, HEADS, LAT), F32),
            pltpu.VMEM((HEADS * LAT, DQK), BF16),
            pltpu.VMEM((kc, HEADS * LAT), BF16),
            pltpu.VMEM((kc, DV), F32),
            pltpu.VMEM((DQK, LAT), F32),
            pltpu.VMEM((din, DV + DQK), F32),
            pltpu.VMEM((nb, vunit * nd, din), BF16),
            pltpu.VMEM((1, din), F32),
            pltpu.VMEM((2, kc, din), F32),
            pltpu.VMEM((nd - 1, rq, dl), BF16),
            pltpu.VMEM((nb, rq + 16, 256), BF16),
            pltpu.VMEM((nb, rq + 16, 256), BF16),
            pltpu.VMEM((rq + 16, 256), BF16),
            pltpu.VMEM((nd, rq + 16, 256), BF16),
            pltpu.VMEM((rq, 256), BF16),
            dma((3,)), dma((2,)),
            dma((D, pos - 1)), dma((D, pos - 1)), dma((D, pos - 1)), dma((D, pos - 1)),
            dma((D, pos)), dma((D, pos)),
            dma((nb - 1,)), dma((nb - 1,)), dma((nd - 1,)), dma((nd - 1,)),
            dma((nb - 1,)), dma((nb - 1,)), dma((nd - 1,)), dma((nd - 1,)),
            dma((nb - 1,)), dma((nb - 1,)),
        ]
    )
    return pl.pallas_call(
        functools.partial(backward_kernel, nb, nd, wunit, vunit),
        out_shape=(
            jax.ShapeDtypeStruct((D, kc, din), F32),
            jax.ShapeDtypeStruct((3, wunit * nd, whalf), BF16),
            jax.ShapeDtypeStruct((1, vunit * nd, din), BF16),
            jax.ShapeDtypeStruct((rq, dl), F32),
            jax.ShapeDtypeStruct((LAT, DQK), BF16),
            jax.ShapeDtypeStruct((8, 256), F32),
        ),
        in_specs=[anywhere] * 4 + [vmem] * 10,
        out_specs=(anywhere,) + (vmem,) * 5,
        scratch_shapes=scratch,
        compiler_params=pltpu.CompilerParams(
            collective_id=1, has_side_effects=True, vmem_limit_bytes=62 * 2**20
        ),
        name="backward",
    )(
        byte_embed, keys, values, wgrads, bias, gain_bytes.reshape(1, -1), w_key, w_value,
        queries, lse, ga, delta, direct, gain_part,
    )


def body(
    byte_embed,
    doc_lengths,
    key_mask,
    latents,
    gain_query,
    gain_bytes,
    gain_mlp,
    w_query,
    w_key,
    w_value,
    w_out,
    w_up,
    w_down,
    cotangent,
):
    nb, nd = lax.axis_size("blk"), lax.axis_size("doc")
    blk = lax.axis_index("blk")
    key_count, din = byte_embed.shape[1:]
    dl = latents.shape[1]
    positions = blk * key_count + jnp.arange(key_count, dtype=jnp.int32)
    usable = (positions[None, :] < doc_lengths[:, None]) & (key_mask == 1)
    bias = jnp.where(usable, 0.0, masked_score).astype(F32)
    attended, lse, keys, values, norm_cols, queries = forward(
        nb, byte_embed, bias, latents, gain_query, gain_bytes, w_query, w_key, w_value
    )
    latents_out, ga, delta, wgrads, direct, gain_part = mlp(
        nb, nd, attended, latents, gain_mlp, w_out, w_up, w_down, cotangent
    )
    byte_grad, wsum, vsum, direct_sum, gq, gains = backward(
        nb, nd, byte_embed, keys, values, wgrads, bias, gain_bytes, w_key, w_value, queries, lse,
        ga, delta, direct, gain_part,
    )

    def unfold(shard, rows):
        return jnp.concatenate([shard[:rows], shard[rows : 2 * rows]], axis=1).astype(F32)

    step = dl // nb
    grad_w_down, grad_w_up, grad_w_out = (unfold(wsum[m], step) for m in range(3))
    grad_kv = unfold(vsum[0], din // nb)
    grad_w_value, grad_w_key = grad_kv[:, :DV], grad_kv[:, DV:]
    gains = gains.reshape(-1)
    gain_mlp_grad = lax.dynamic_slice(gains[:dl], (blk * step,), (step,))
    gain_bytes_grad = lax.dynamic_slice(gains[dl:], (blk * (din // nb),), (din // nb,))
    skip = blk * step - jnp.minimum(blk * step // 128 * 128, dl - 256)
    cols = lax.dynamic_slice(norm_cols, (0, skip), (LAT, step))
    grad_w_query = lax.dot_general(
        cols, gq, (((0,), (0,)), ((), ())), preferred_element_type=F32
    )
    wq_rows = lax.dynamic_slice(w_query, (blk * step, 0), (step, DQK))
    dy_cols = dot_nt(gq, wq_rows)
    gain_rows = lax.dynamic_slice(gain_query, (blk * step,), (step,))
    gain_query_grad = jnp.sum(dy_cols * cols.astype(F32), axis=0) / gain_rows
    own = lax.dynamic_slice(gq, (blk * latents.shape[0], 0), (latents.shape[0], DQK))
    dxh = dot_nt(own, w_query) * gain_query
    xh, inv = norm_parts(latents)
    latents_grad = direct_sum + inv * (
        dxh
        - jnp.mean(dxh, axis=-1, keepdims=True)
        - xh * jnp.mean(dxh * xh, axis=-1, keepdims=True)
    )
    return (
        latents_out,
        byte_grad,
        latents_grad,
        gain_query_grad,
        gain_bytes_grad,
        gain_mlp_grad,
        grad_w_query,
        grad_w_key,
        grad_w_value,
        grad_w_out,
        grad_w_up,
        grad_w_down,
    )


def solution(mesh):
    in_specs = (
        P("doc", "blk", None),
        P("doc"),
        P("doc", "blk"),
        P("blk", None),
        P(),
        P(),
        P(),
        P(),
        P(),
        P(),
        P(),
        P(),
        P(),
        P("doc", "blk", None),
    )
    out_specs = (
        P("doc", "blk", None),
        P("doc", "blk", None),
        P("blk", None),
        P("blk"),
        P("blk"),
        P("blk"),
        P("blk", None),
        P("blk", None),
        P("blk", None),
        P("blk", None),
        P("blk", None),
        P("blk", None),
    )
    return jax.shard_map(body, mesh=mesh, in_specs=in_specs, out_specs=out_specs, check_vma=False)
```

```python
import functools
import math

import jax
import jax.numpy as jnp
from jax import lax
from jax.experimental import pallas as pl
from jax.experimental.pallas import tpu as pltpu
from jax.sharding import PartitionSpec as P

LAT = 256
HEADS = 8
QK_HEAD = 32
V_HEAD = 160
DQK = HEADS * QK_HEAD
DV = HEADS * V_HEAD
MESH = pl.DeviceIdType.MESH
F32 = jnp.float32
BF16 = jnp.bfloat16

epsilon = 1e-05
masked_score = -1e30
LOG2E = math.log2(math.e)
SCORE2 = QK_HEAD ** (-0.5) * LOG2E
SCORE_SCALE = QK_HEAD ** (-0.5)


def dot_nn(a, b):
    return jnp.dot(a, b, preferred_element_type=F32)


def dot_nt(a, b):
    return lax.dot_general(a, b, (((1,), (1,)), ((), ())), preferred_element_type=F32)


def norm_parts(v):
    centered = v - jnp.mean(v, axis=-1, keepdims=True)
    spread = jnp.mean(centered * centered, axis=-1, keepdims=True)
    inv = lax.rsqrt(spread + epsilon)
    return centered * inv, inv


def window(h):
    return V_HEAD * h // 128 * 128


def value_mask(h, rows):
    lane = lax.broadcasted_iota(jnp.int32, (rows, 256), 1) + window(h)
    keep = (lane >= V_HEAD * h) & (lane < V_HEAD * (h + 1))
    return jnp.where(keep, 1.0, 0.0).astype(BF16)


def query_mask(h, rows):
    lane = lax.broadcasted_iota(jnp.int32, (rows, DQK), 1)
    keep = (lane >= QK_HEAD * h) & (lane < QK_HEAD * (h + 1))
    return jnp.where(keep, 1.0, 0.0).astype(BF16)


def row_to_lanes(row):
    return jnp.transpose(jnp.broadcast_to(row, (128, row.shape[1])))


def wide(col, n):
    return jnp.concatenate([col] * (n // 128), axis=1) if n > 128 else col


def remote(src, dst, send, recv, doc, blk):
    return pltpu.make_async_remote_copy(
        src_ref=src, dst_ref=dst, send_sem=send, recv_sem=recv,
        device_id=(doc, blk), device_id_type=MESH,
    )


def forward_kernel(
    nb,
    x_ref, bias_ref, lat_ref, gq_ref, gb_ref, wq_ref, wk_ref, wv_ref,
    att_ref, lse_ref, k_ref, v_ref, nlw_ref, qall_ref,
    nl_cols, normed, qm, lloc, lmate, lz, acc, part, mate_in, rin, lin,
    q_s, q_r, n_s, n_r, l_s, l_r, mate_s, mate_r, rs_s, rs_r, ls_s, ls_r,
):
    D, kc, din = x_ref.shape
    rq = lat_ref.shape[0]
    pos = nb // 2
    doc, blk = lax.axis_index("doc"), lax.axis_index("blk")
    p, c = blk // 2, blk % 2
    mate = 2 * p + 1 - c
    barrier = pltpu.get_barrier_semaphore()
    for i in range(1, nb):
        pl.semaphore_signal(
            barrier, inc=1, device_id=(doc, lax.rem(blk + i, nb)), device_id_type=MESH
        )

    xhat, _ = norm_parts(lat_ref[...])
    nl = (xhat * gq_ref[...]).astype(BF16)
    step = nl.shape[1] // nb
    for j in range(nb):
        at = min(j * step // 128 * 128, nl.shape[1] - 256)
        nl_cols[j] = nl[:, at : at + 256]
    own = pl.ds(pl.multiple_of(blk * rq, rq), rq)
    qall_ref[own, :] = dot_nn(nl, wq_ref[...]).astype(BF16)
    pl.semaphore_wait(barrier, nb - 1)

    def q_copy(i, slot):
        return remote(
            qall_ref.at[own, :], qall_ref.at[slot, :], q_s.at[i - 1], q_r.at[i - 1],
            doc, lax.rem(blk + i, nb),
        )

    def n_copy(i, slot):
        peer = lax.rem(blk + i, nb)
        return remote(
            nl_cols.at[peer], nlw_ref.at[slot, :], n_s.at[i - 1], n_r.at[i - 1], doc, peer
        )

    for i in range(1, nb):
        q_copy(i, own).start()
    for i in range(1, nb):
        n_copy(i, own).start()
    nlw_ref[own, :] = nl_cols[blk]

    @pl.loop(0, D)
    def _(n):
        xh, _ = norm_parts(x_ref[n].astype(F32))
        normed[n] = (xh * gb_ref[...]).astype(BF16)
        k_ref[n] = dot_nn(normed[n], wk_ref[...]).astype(BF16)

    for i in range(1, nb):
        src = lax.rem(blk + nb - i, nb)
        q_copy(i, pl.ds(pl.multiple_of(src * rq, rq), rq)).wait_recv()
    for h in range(HEADS):
        qm[h] = qall_ref[...] * query_mask(h, LAT)

    @pl.loop(0, D)
    def _(n):
        bias = wide(row_to_lanes(bias_ref[pl.ds(n, 1), :]), LAT)
        kn = k_ref[n]
        rows = []
        for h in range(HEADS):
            s = dot_nt(kn, qm[h]) * SCORE2 + bias
            top = jnp.max(s, axis=0, keepdims=True)
            tot = jnp.sum(jnp.exp2(s - top), axis=0, keepdims=True)
            rows.append(top + jnp.log(tot) * LOG2E)
        lloc[n] = jnp.concatenate(rows, axis=0)

    half = D // 2
    mine, other = pl.ds(c * half, half), pl.ds((1 - c) * half, half)

    def merge(a, b):
        top = jnp.maximum(a, b)
        return top + jnp.log(jnp.exp2(a - top) + jnp.exp2(b - top)) * LOG2E

    first = remote(lloc.at[other], lmate, l_s.at[0], l_r.at[0], doc, mate)
    first.start()

    def values(lo, hi):
        @pl.loop(lo, hi)
        def _(n):
            v_ref[n] = dot_nn(normed[n], wv_ref[...]).astype(BF16)

    values(0, D // 4)
    first.wait_recv()
    lz[p] = merge(lloc[mine], lmate[...])

    def z_copy(i, slot):
        return remote(
            lz.at[p], lz.at[slot], l_s.at[i], l_r.at[i],
            doc, 2 * lax.rem(p + i, pos) + c,
        )

    for i in range(1, pos):
        z_copy(i, p).start()
    values(D // 4, 3 * D // 4)
    for i in range(1, pos):
        z_copy(i, lax.rem(p + pos - i, pos)).wait_recv()
    total = lz[0]
    for i in range(1, pos):
        total = merge(total, lz[i])
    lse_ref[mine] = total
    last = remote(lse_ref.at[mine], lse_ref.at[mine], l_s.at[pos], l_r.at[pos], doc, mate)
    last.start()
    values(3 * D // 4, D)
    remote(
        lse_ref.at[other], lse_ref.at[other], l_s.at[pos], l_r.at[pos], doc, mate
    ).wait_recv()

    def mate_copy(n):
        return remote(
            part.at[n, 1 - c], mate_in.at[n], mate_s.at[n], mate_r.at[n], doc, mate
        )

    def right_copy(n, j, src):
        return remote(
            src, rin.at[n, j], rs_s.at[n, j], rs_r.at[n, j],
            doc, 2 * jnp.minimum(p + 1, pos - 1) + c,
        )

    def left_copy(n, j, src):
        return remote(
            src, lin.at[n, j], ls_s.at[n, j], ls_r.at[n, j],
            doc, 2 * jnp.maximum(p - 1, 0) + c,
        )

    def chip_sum(n):
        mate_copy(n).wait_recv()
        for j in range(pos):
            both = part[n, c, j].astype(F32) + mate_in[n, j].astype(F32)
            part[n, c, j] = both.astype(BF16)

            @pl.when((p == 0) & (j > 0))
            def _():
                right_copy(n, j, part.at[n, c, j]).start()

            @pl.when((p == pos - 1) & (j < pos - 1))
            def _():
                left_copy(n, j, part.at[n, c, j]).start()

    @pl.loop(0, D)
    def _(n):
        logs = lse_ref[n]
        logs_t = jnp.transpose(jnp.concatenate([logs] * (128 // HEADS), axis=0))
        bias = bias_ref[pl.ds(n, 1), :]
        kn = k_ref[n]
        acc[...] = jnp.zeros_like(acc)
        for h in range(HEADS):
            s = dot_nt(qm[h], kn) * SCORE2 + bias
            prob = jnp.exp2(s - logs_t[:, h : h + 1]).astype(BF16)
            cols = slice(window(h), window(h) + 256)
            acc[:, cols] += dot_nn(prob, v_ref[n, :, cols] * value_mask(h, kc))
        for j in range(nb):
            part[n, j % 2, j // 2] = acc[rq * j : rq * (j + 1), :].astype(BF16)
        mate_copy(n).start()

        @pl.when(n > 0)
        def _():
            chip_sum(n - 1)

    chip_sum(D - 1)

    def from_left(n):
        for j in range(1, pos):
            @pl.when(j >= p)
            def _():
                right_copy(n, j, part.at[n, c, j]).wait_recv()

            @pl.when(j > p)
            def _():
                both = rin[n, j].astype(F32) + part[n, c, j].astype(F32)
                part[n, c, j] = both.astype(BF16)
                right_copy(n, j, part.at[n, c, j]).start()

    def from_right(n):
        for j in range(pos - 2, -1, -1):
            @pl.when(j <= p)
            def _():
                left_copy(n, j, part.at[n, c, j]).wait_recv()

            @pl.when(j < p)
            def _():
                both = lin[n, j].astype(F32) + part[n, c, j].astype(F32)
                part[n, c, j] = both.astype(BF16)
                left_copy(n, j, part.at[n, c, j]).start()

    def finish(n):
        acc[0:rq, :] = part[n, c, p].astype(F32)

        @pl.when(p > 0)
        def _():
            acc[0:rq, :] += rin[n, p].astype(F32)

        @pl.when(p < pos - 1)
        def _():
            acc[0:rq, :] += lin[n, p].astype(F32)

        att_ref[n] = acc[0:rq, :].astype(BF16)

    @pl.loop(0, D + pos - 1)
    def _(t):
        right_n, left_n, done_n = t - p, t - (pos - 1 - p), t - (pos - 1)

        @pl.when((p > 0) & (right_n >= 0) & (right_n < D))
        def _():
            from_left(right_n)

        @pl.when((p < pos - 1) & (left_n >= 0) & (left_n < D))
        def _():
            from_right(left_n)

        @pl.when(done_n >= 0)
        def _():
            finish(done_n)

    for i in range(1, nb):
        src = lax.rem(blk + nb - i, nb)
        n_copy(i, pl.ds(pl.multiple_of(src * rq, rq), rq)).wait_recv()

    for i in range(1, nb):
        q_copy(i, own).wait_send()
        n_copy(i, own).wait_send()
    first.wait_send()
    for i in range(1, pos):
        z_copy(i, p).wait_send()
    last.wait_send()

    @pl.loop(0, D)
    def _(n):
        mate_copy(n).wait_send()
        for j in range(pos):
            @pl.when((j > p) & (p < pos - 1))
            def _():
                right_copy(n, j, part.at[n, c, j]).wait_send()

            @pl.when((j < p) & (p > 0))
            def _():
                left_copy(n, j, part.at[n, c, j]).wait_send()


def forward(nb, byte_embed, bias, latents, gain_query, gain_bytes, w_query, w_key, w_value):
    D, kc, din = byte_embed.shape
    rq, dl = latents.shape
    pos = nb // 2
    vmem = pl.BlockSpec(memory_space=pltpu.VMEM)
    dma = pltpu.SemaphoreType.DMA
    return pl.pallas_call(
        functools.partial(forward_kernel, nb),
        out_shape=(
            jax.ShapeDtypeStruct((D, rq, DV), BF16),
            jax.ShapeDtypeStruct((D, HEADS, LAT), F32),
            jax.ShapeDtypeStruct((D, kc, DQK), BF16),
            jax.ShapeDtypeStruct((D, kc, DV), BF16),
            jax.ShapeDtypeStruct((LAT, 256), BF16),
            jax.ShapeDtypeStruct((LAT, DQK), BF16),
        ),
        in_specs=[vmem] * 8,
        out_specs=(vmem,) * 6,
        scratch_shapes=[
            pltpu.VMEM((nb, rq, 256), BF16),
            pltpu.VMEM((D, kc, din), BF16),
            pltpu.VMEM((HEADS, LAT, DQK), BF16),
            pltpu.VMEM((D, HEADS, LAT), F32),
            pltpu.VMEM((D // 2, HEADS, LAT), F32),
            pltpu.VMEM((pos, D // 2, HEADS, LAT), F32),
            pltpu.VMEM((LAT, DV), F32),
            pltpu.VMEM((D, 2, pos, rq, DV), BF16),
            pltpu.VMEM((D, pos, rq, DV), BF16),
            pltpu.VMEM((D, pos, rq, DV), BF16),
            pltpu.VMEM((D, pos, rq, DV), BF16),
            dma((nb - 1,)), dma((nb - 1,)), dma((nb - 1,)), dma((nb - 1,)),
            dma((pos + 1,)), dma((pos + 1,)),
            dma((D,)), dma((D,)),
            dma((D, pos)), dma((D, pos)), dma((D, pos)), dma((D, pos)),
        ],
        compiler_params=pltpu.CompilerParams(
            collective_id=0, has_side_effects=True, vmem_limit_bytes=56 * 2**20
        ),
        name="forward",
    )(
        byte_embed, bias, latents, gain_query.reshape(1, -1), gain_bytes.reshape(1, -1),
        w_query, w_key, w_value,
    )


def gelu_parts(u):
    k = math.sqrt(2.0 / math.pi)
    sq = u * u
    t = jnp.tanh(k * u * (1.0 + 0.044715 * sq))
    value = 0.5 * u * (1.0 + t)
    slope = 0.5 * (1.0 + t) + 0.5 * k * u * (1.0 - t * t) * (1.0 + 3 * 0.044715 * sq)
    return value, slope


def owner_rows(total, docs):
    return -(-total // (16 * docs)) * 16


class ShardSums:
    def __init__(
        self, doc, blk, nd, nb, count, unit, group, lags,
        own, mate_in, inbox, rin, lin, out, sems,
    ):
        self.doc, self.p, self.c = doc, blk // 2, blk % 2
        self.nd, self.pos, self.count, self.unit = nd, nb // 2, count, unit
        self.bits = nd.bit_length() - 1
        self.own, self.mate_in, self.inbox = own, mate_in, inbox
        self.rin, self.lin, self.out = rin, lin, out
        (
            self.mate_s, self.mate_r, self.in_s, self.in_r,
            self.right_s, self.right_r, self.left_s, self.left_r, self.out_s, self.out_r,
        ) = sems
        self.group, self.lags = group, lags
        self.steps = count // group + lags[-1] + self.pos - 1

    def weight(self, s, k):
        b = (s + k) % self.bits
        return 1 + b * (b + 1) // 2

    def my_bit(self, w):
        return (self.doc // w) % 2

    def quarter(self, s, k, i, sent):
        q = 0
        for r in range(k):
            w = self.weight(s, r)
            q = q + self.my_bit(w) * w
        w = self.weight(s, k)
        mine = self.my_bit(w)
        q = q + ((1 - mine) if sent else mine) * w
        for r in range(k + 1, self.bits):
            q = q + ((i >> (r - k - 1)) & 1) * self.weight(s, r)
        return q

    def width(self, k):
        return 2 ** (self.bits - 1 - k)

    def slot(self, k, i):
        return sum(self.width(r) for r in range(k)) + i

    def rows(self, q):
        return pl.ds(pl.multiple_of(q * self.unit, self.unit), self.unit)

    def halving(self, s, k, i):
        w = self.weight(s, k)
        peer = self.doc + w * (1 - 2 * self.my_bit(w))
        slot = self.slot(k, i)
        return remote(
            self.own.at[s, self.rows(self.quarter(s, k, i, True)), :], self.inbox.at[s, slot],
            self.in_s.at[s, slot], self.in_r.at[s, slot], peer, 2 * self.p + self.c,
        )

    def right(self, s):
        return remote(
            self.own.at[s, self.rows(self.doc), :], self.rin.at[s],
            self.right_s.at[s], self.right_r.at[s],
            self.doc, 2 * jnp.minimum(self.p + 1, self.pos - 1) + self.c,
        )

    def left(self, s):
        return remote(
            self.own.at[s, self.rows(self.doc), :], self.lin.at[s],
            self.left_s.at[s], self.left_r.at[s],
            self.doc, 2 * jnp.maximum(self.p - 1, 0) + self.c,
        )

    def share(self, m, i):
        return remote(
            self.out.at[m, self.rows(self.doc), :], self.out.at[m, self.rows(self.doc), :],
            self.out_s.at[m, i - 1], self.out_r.at[m, i - 1],
            lax.rem(self.doc + i, self.nd), 2 * self.p + self.c,
        )

    def shared(self, m, i):
        src = lax.rem(self.doc + self.nd - i, self.nd)
        return remote(
            self.out.at[m, self.rows(src), :], self.out.at[m, self.rows(src), :],
            self.out_s.at[m, i - 1], self.out_r.at[m, i - 1], src, 2 * self.p + self.c,
        )

    def add(self, s, q, other):
        rows = self.rows(q)
        self.own[s, rows, :] = (
            self.own[s, rows, :].astype(F32) + other.astype(F32)
        ).astype(BF16)

    def begin(self, s, mate_copy):
        mate_copy(s).wait_recv()
        rows = self.mate_in.shape[1]
        self.own[s, 0:rows, :] = (
            self.own[s, 0:rows, :].astype(F32) + self.mate_in[s].astype(F32)
        ).astype(BF16)
        for i in range(self.width(0)):
            self.halving(s, 0, i).start()

    def halve(self, s, k):
        for i in range(self.width(k - 1)):
            self.halving(s, k - 1, i).wait_recv()
            self.add(s, self.quarter(s, k - 1, i, False), self.inbox[s, self.slot(k - 1, i)])
        if k < self.bits:
            for i in range(self.width(k)):
                self.halving(s, k, i).start()
            return
        j = s % self.pos

        @pl.when((self.p == 0) & (j > 0))
        def _():
            self.right(s).start()

        @pl.when((self.p == self.pos - 1) & (j < self.pos - 1))
        def _():
            self.left(s).start()

    def from_left(self, s):
        j = s % self.pos

        @pl.when(j >= self.p)
        def _():
            self.right(s).wait_recv()

        @pl.when(j > self.p)
        def _():
            self.add(s, self.doc, self.rin[s])
            self.right(s).start()

    def from_right(self, s):
        j = s % self.pos

        @pl.when(j <= self.p)
        def _():
            self.left(s).wait_recv()

        @pl.when(j < self.p)
        def _():
            self.add(s, self.doc, self.lin[s])
            self.left(s).start()

    def finish(self, s):
        @pl.when(s % self.pos == self.p)
        def _():
            m = s // self.pos

            @pl.when(self.p > 0)
            def _():
                self.add(s, self.doc, self.rin[s])

            @pl.when(self.p < self.pos - 1)
            def _():
                self.add(s, self.doc, self.lin[s])

            self.out[m, self.rows(self.doc), :] = self.own[s, self.rows(self.doc), :]
            for i in range(1, self.nd):
                self.share(m, i).start()

    def step(self, t, mate_copy, entered=0):
        def at(t, when, run, turned=False):
            @pl.when((t >= 0) & (t < self.count // self.group) & when)
            def _():
                for i in range(self.group):
                    run(t * self.group + (self.group - 1 - i if turned else i))

        at(t, t >= entered, lambda s: self.begin(s, mate_copy))
        for k in range(1, self.bits + 1):
            at(t - self.lags[k - 1], True, functools.partial(self.halve, k=k))
        base = t - self.lags[-1]
        at(base - self.p, self.p > 0, self.from_left, True)
        at(base - (self.pos - 1 - self.p), self.p < self.pos - 1, self.from_right)
        at(base - (self.pos - 1), True, self.finish)

    def drain(self):
        for m in range(self.count // self.pos):
            for i in range(1, self.nd):
                self.shared(m, i).wait_recv()
                self.share(m, i).wait_send()

        @pl.loop(0, self.count)
        def _(s):
            for k in range(self.bits):
                for i in range(self.width(k)):
                    self.halving(s, k, i).wait_send()
            j = s % self.pos

            @pl.when((j > self.p) & (self.p < self.pos - 1))
            def _():
                self.right(s).wait_send()

            @pl.when((j < self.p) & (self.p > 0))
            def _():
                self.left(s).wait_send()


def shard_sum_scratch(nd, nb, count, unit, rows, width):
    dma = pltpu.SemaphoreType.DMA
    arrays = count // (nb // 2)
    return [
        pltpu.VMEM((count, unit * nd, width), BF16),
        pltpu.VMEM((count, rows, width), BF16),
        pltpu.VMEM((count, nd - 1, unit, width), BF16),
        pltpu.VMEM((count, unit, width), BF16),
        pltpu.VMEM((count, unit, width), BF16),
        dma((count,)), dma((count,)),
        dma((count, nd - 1)), dma((count, nd - 1)),
        dma((count,)), dma((count,)), dma((count,)), dma((count,)),
        dma((arrays, nd - 1)), dma((arrays, nd - 1)),
    ]


def backward_kernel(nb, nd, wunit, vunit, *refs):
    (
        x_hbm, k_hbm, v_hbm, wo_hbm, wu_hbm, wd_hbm, wk_hbm, wv_hbm, cot_hbm,
        att_ref, lat_ref, gm_ref, bias_ref, gb_ref, qall_ref, lse_ref,
    ) = refs[:16]
    out_hbm, bg_hbm, wsum_ref, vsum0_ref, vsum1_ref, dsum_ref, gq_ref, gains_ref = refs[16:24]
    wscr, vscr = refs[24:39], (refs[39:54], refs[54:69])
    (
        wpool, x_ref, k_ref, ga_all, delta_all, delta_t, qm, wkv, ds_all, gv_acc, gq_acc,
        fpool, frames, low_t, right, stage, vstage, gain_acc, gmlp_acc, direct_out, dir_in,
        misc_out, misc_in, misc2_out, misc2_in,
        load_s, out_s, bg_s, ar_s, ar_r, al_s, al_r, am_s, am_r, d_s, d_r, dir_s, dir_r,
        m1_s, m1_r, m2_s, m2_r, m3_s, m3_r,
    ) = refs[69:]
    D, kc, din = x_ref.shape
    rq, dl = lat_ref.shape
    rows_all = D * rq
    pos = nb // 2
    hh, vh, qh = HEADS // 2, DV // 2, DQK // 2
    bits = nd.bit_length() - 1
    doc, blk = lax.axis_index("doc"), lax.axis_index("blk")
    p, c = blk // 2, blk % 2
    mate = 2 * p + 1 - c

    barrier = pltpu.get_barrier_semaphore()
    for i in range(1, nb):
        pl.semaphore_signal(
            barrier, inc=1, device_id=(doc, lax.rem(blk + i, nb)), device_id_type=MESH
        )
    for i in range(1, nd):
        pl.semaphore_signal(
            barrier, inc=1, device_id=(lax.rem(doc + i, nd), blk), device_id_type=MESH
        )

    def load(src, dst, i):
        return pltpu.make_async_copy(src, dst, load_s.at[i])

    slot0, slot1 = wpool.at[0:dl, :], wpool.at[dl : 2 * dl, :]
    load_out, load_up = load(wo_hbm, slot0, 0), load(wu_hbm, slot1, 1)
    load_down, load_out2 = load(wd_hbm, slot0, 2), load(wo_hbm, slot0, 3)
    load_v = load(v_hbm, wpool.at[0 : D * kc, :], 4)
    load_cot = load(cot_hbm, frames.at[1], 5)
    later = [load(k_hbm, k_ref, 6), load(x_hbm, x_ref, 7)]
    for g in range(2):
        later.append(load(wv_hbm.at[:, g * vh : (g + 1) * vh], wkv.at[g, :, 0:vh], 8 + g))
        later.append(
            load(wk_hbm.at[:, g * qh : (g + 1) * qh], wkv.at[g, :, vh : vh + qh], 10 + g)
        )
    load_out.start()
    load_up.start()
    load_cot.start()

    weights = ShardSums(
        doc, blk, nd, nb, 3 * pos, wunit, 2, [3 + k for k in range(bits)],
        *wscr[:5], wsum_ref, wscr[5:],
    )
    values = [
        ShardSums(
            doc, blk, nd, nb, pos, vunit, pos, lags, *vscr[g][:5], out, vscr[g][5:],
        )
        for g, (lags, out) in enumerate(
            (
                ([2 + k for k in range(bits)], vsum0_ref),
                ([1 + k for k in range(bits)], vsum1_ref),
            )
        )
    ]

    wrows, whalf = 2 * dl // nb, dl // 2
    vhalf = (vh + qh) // 2

    def w_mate(s):
        rows = pl.ds(pl.multiple_of(s % (2 * pos) * wrows, wrows), wrows)
        return remote(
            stage.at[rows, 0:whalf], weights.mate_in.at[s],
            weights.mate_s.at[s], weights.mate_r.at[s], doc, mate,
        )

    def v_mate(g):
        return lambda s: remote(
            vstage.at[g, s], values[g].mate_in.at[s],
            values[g].mate_s.at[s], values[g].mate_r.at[s], doc, mate,
        )

    parts, ahead = 2 * D, 4

    def chunk(j, core):
        return pl.ds(pl.multiple_of((2 * j + core) * rq, rq), rq)

    def right_copy(e, hop, j):
        rows = ga_all.at[e, chunk(j, c), :]
        return remote(
            rows, rows, ar_s.at[e, hop], ar_r.at[e, hop],
            doc, 2 * jnp.minimum(p + 1, pos - 1) + c,
        )

    def left_copy(e, hop, j):
        rows = ga_all.at[e, chunk(j, c), :]
        return remote(
            rows, rows, al_s.at[e, hop], al_r.at[e, hop],
            doc, 2 * jnp.maximum(p - 1, 0) + c,
        )

    def mate_copy(e, j, core):
        rows = ga_all.at[e, chunk(j, core), :]
        return remote(rows, rows, am_s.at[e, j], am_r.at[e, j], doc, mate)

    own_rows = pl.ds(pl.multiple_of(blk * rq, rq), rq)

    def delta_copy(i, rows):
        return remote(
            delta_all.at[rows, :], delta_all.at[rows, :], d_s.at[i - 1], d_r.at[i - 1],
            doc, lax.rem(blk + i, nb),
        )

    def direct_copy(i):
        return remote(
            direct_out, dir_in.at[i - 1], dir_s.at[i - 1], dir_r.at[i - 1],
            lax.rem(doc + i, nd), blk,
        )

    def send_own(e):
        @pl.when(p < pos - 1)
        def _():
            right_copy(e, 0, p).start()

        @pl.when(p > 0)
        def _():
            left_copy(e, 0, p).start()

        mate_copy(e, p, c).start()

    mid = fpool.at[0:rows_all, :]
    xhat = fpool.at[rows_all : 2 * rows_all, :]
    slope = fpool.at[2 * rows_all : 3 * rows_all, :]
    kv_acc = fpool.at[0:din, 0 : vh + qh]
    step_w = dl // nb

    def weight_grad(m, left):
        low_t[...] = jnp.transpose(left)

        @pl.loop(0, pos)
        def _(j):
            s = m * pos + j
            for core in (1 - c, c):
                rows = pl.ds(pl.multiple_of((2 * j + core) * step_w, step_w), step_w)
                shard = dot_nn(low_t[rows, :], right[...]).astype(BF16)
                for i in range(2):
                    part = shard[:, i * whalf : (i + 1) * whalf]
                    if core is c:
                        weights.own[s, i * step_w : (i + 1) * step_w, :] = part
                    else:
                        at = pl.multiple_of(s % (2 * pos) * wrows, wrows) + i * step_w
                        stage[pl.ds(pl.multiple_of(at, 16), step_w), 0:whalf] = part
                if core is not c:
                    w_mate(s).start()

    att_low = att_ref[...].reshape(rows_all, DV)
    load_out.wait()
    mid[...] = dot_nn(att_low, slot0[...]) + jnp.concatenate([lat_ref[...]] * D, axis=0)
    load_down.start()
    xh, inv = norm_parts(mid[...])
    xhat[...] = xh
    nm = (xh * gm_ref[...]).astype(BF16)
    load_up.wait()
    act, sl = gelu_parts(dot_nn(nm, slot1[...]))
    slope[...] = sl
    act_low = act.astype(BF16)
    load_cot.wait()
    gm = frames[1].astype(BF16)
    right[...] = gm
    pl.semaphore_wait(barrier, nb - 1 + nd - 1)
    weight_grad(0, act_low)
    load_down.wait()
    frames[0] = mid[...] + dot_nn(act_low, slot0[...])
    store_out = pltpu.make_async_copy(frames.at[0], out_hbm, out_s)
    store_out.start()
    g_up = (dot_nt(gm, slot0[...]) * slope[...]).astype(BF16)
    load_out2.start()
    for item in later:
        item.start()
    for s in range(pos):
        weights.begin(s, w_mate)
    right[...] = g_up
    weight_grad(1, nm)
    g_nm = dot_nt(g_up, slot1[...])
    gmlp_acc[...] = jnp.sum(g_nm * xhat[...], axis=0, keepdims=True)
    dxh = g_nm * gm_ref[...]
    mid[...] = frames[1] + inv * (
        dxh
        - jnp.mean(dxh, axis=-1, keepdims=True)
        - xhat[...] * jnp.mean(dxh * xhat[...], axis=-1, keepdims=True)
    )
    gb = mid[...].astype(BF16)
    right[...] = gb
    load_out2.wait()
    ga = dot_nt(gb, slot0[...])
    load_v.start()
    for g in range(2):
        for n in range(D):
            ga_all[g * D + n, own_rows, :] = ga[
                n * rq : (n + 1) * rq, g * vh : (g + 1) * vh
            ].astype(BF16)
    for e in range(ahead):
        send_own(e)
    lane = lax.broadcasted_iota(jnp.int32, (rq, 128), 1)
    delta = jnp.zeros((rq, 128), F32)
    for h in range(HEADS):
        cols = slice(window(h), window(h) + 256)
        prod = ga[:, cols] * (att_low[:, cols] * value_mask(h, rows_all)).astype(F32)
        one = jnp.sum(prod, axis=1, keepdims=True)
        for n in range(D):
            delta = delta + jnp.where(lane == n * HEADS + h, one[n * rq : (n + 1) * rq], 0.0)
    delta_all[own_rows, :] = delta
    for i in range(1, nb):
        delta_copy(i, own_rows).start()
    direct = mid[0:rq, :]
    for n in range(1, D):
        direct = direct + mid[n * rq : (n + 1) * rq, :]
    direct_out[...] = direct.astype(BF16)
    for i in range(1, nd):
        direct_copy(i).start()
    for s in range(pos):
        w_mate(s).wait_send()
    weight_grad(2, att_low)

    for h in range(HEADS):
        half = slice(h // hh * qh, h // hh * qh + qh)
        qm[h] = (qall_ref[...] * query_mask(h, LAT))[:, half]
    gq_acc[...] = jnp.zeros_like(gq_acc)
    kv_acc[...] = jnp.zeros((din, vh + qh), F32)
    gain_acc[...] = jnp.zeros_like(gain_acc)

    def forward_chunks(e, hop):
        j = p - 1 - hop

        @pl.when(j >= 0)
        def _():
            right_copy(e, hop, j).wait_recv()
            if hop + 1 < pos - 1:
                @pl.when(p < pos - 1)
                def _():
                    right_copy(e, hop + 1, j).start()

            mate_copy(e, j, c).start()

        i = p + 1 + hop

        @pl.when(i < pos)
        def _():
            left_copy(e, hop, i).wait_recv()
            if hop + 1 < pos - 1:
                @pl.when(p > 0)
                def _():
                    left_copy(e, hop + 1, i).start()

            mate_copy(e, i, c).start()

    def doc_rows(n):
        return pl.ds(pl.multiple_of(n * kc, kc), kc)

    def bytes_back(g, n):
        e = g * D + n
        for j in range(pos):
            mate_copy(e, j, 1 - c).wait_recv()
        bias = wide(row_to_lanes(bias_ref[pl.ds(n, 1), :]), LAT)
        logs, deltas = lse_ref[n], delta_t[n]
        kn = k_ref[n, :, g * qh : (g + 1) * qh]
        kt = jnp.transpose(kn)
        gv_acc[...] = jnp.zeros_like(gv_acc)
        for i in range(hh):
            h = g * hh + i
            cols = slice(window(i), window(i) + 256)
            vcols = slice(g * vh + window(i), g * vh + window(i) + 256)
            gah = ga_all[e, :, cols] * value_mask(i, LAT)
            s = dot_nt(kn, qm[h]) * SCORE2 + bias
            prob = jnp.exp2(s - logs[h : h + 1, :])
            dprob = dot_nt(wpool[doc_rows(n), vcols], gah)
            ds = (prob * (dprob - deltas[h : h + 1, :])).astype(BF16)
            ds_all[:, i * LAT : (i + 1) * LAT] = ds
            gv_acc[:, cols] += dot_nn(prob.astype(BF16), gah)
            head = slice(QK_HEAD * i, QK_HEAD * (i + 1))
            rows = slice(QK_HEAD * h, QK_HEAD * (h + 1))
            gq_acc[rows, :] += dot_nn(kt[head, :], ds)
        gk = dot_nn(ds_all[:, 0:LAT], qm[g * hh])
        for i in range(1, hh):
            gk = gk + dot_nn(ds_all[:, i * LAT : (i + 1) * LAT], qm[g * hh + i])
        grads_now = jnp.concatenate(
            [gv_acc[...].astype(BF16), (gk * SCORE_SCALE).astype(BF16)], axis=1
        )
        xh, inv = norm_parts(x_ref[n].astype(F32))
        kept = stage.at[doc_rows(n), 0 : vh + qh]
        if g == 0:
            kept[...] = grads_now
        else:
            gx = dot_nt(kept[...], wkv[0]) + dot_nt(grads_now, wkv[1])
            gain_acc[...] += jnp.sum(gx * xh, axis=0, keepdims=True)
            dxh = gx * gb_ref[...]
            slot = lax.rem(n, 2)

            @pl.when(n >= 2)
            def _():
                pltpu.make_async_copy(frames.at[slot, 0:kc, 0:din], bg_hbm.at[n - 2], bg_s.at[slot]).wait()

            frames[slot, 0:kc, 0:din] = inv * (
                dxh
                - jnp.mean(dxh, axis=-1, keepdims=True)
                - xh * jnp.mean(dxh * xh, axis=-1, keepdims=True)
            )
            pltpu.make_async_copy(frames.at[slot, 0:kc, 0:din], bg_hbm.at[n], bg_s.at[slot]).start()
        normed_t = jnp.transpose((xh * gb_ref[...]).astype(BF16))
        kv_acc[...] += dot_nn(normed_t, grads_now)

    def cut_values(g):
        step = din // nb
        for s in range(pos):
            for core in (1 - c, c):
                rows = pl.ds(pl.multiple_of((2 * s + core) * step, step), step)
                to = values[g].own if core is c else vstage.at[g]
                for i in range(2):
                    to[s, i * step : (i + 1) * step, :] = fpool[
                        rows, i * vhalf : (i + 1) * vhalf
                    ].astype(BF16)
            v_mate(g)(s).start()
        if g == 0:
            kv_acc[...] = jnp.zeros((din, vh + qh), F32)

    start0 = (pos + D + 2) // 2

    @pl.loop(0, parts + pos)
    def _(t):
        @pl.when(t < parts - ahead)
        def _():
            send_own(t + ahead)

        for hop in range(pos - 1):
            @pl.when((t >= hop) & (t - hop < parts))
            def _():
                forward_chunks(t - hop, hop)

        @pl.when(t % 2 == 0)
        def _():
            weights.step(t // 2 + 2, w_mate, pos // 2)
            values[0].step(t // 2 - start0, v_mate(0))

        @pl.when(t == pos)
        def _():
            for i in range(1, nb):
                src = lax.rem(blk + nb - i, nb)
                delta_copy(i, pl.ds(pl.multiple_of(src * rq, rq), rq)).wait_recv()
            turned = jnp.transpose(delta_all[...])
            for n in range(D):
                delta_t[n] = turned[n * HEADS : (n + 1) * HEADS, :]
            for item in later:
                item.wait()
            load_v.wait()
            store_out.wait()
            for s in range(pos, 3 * pos):
                w_mate(s).wait_send()

        @pl.when((t >= pos) & (t < pos + D))
        def _():
            bytes_back(0, t - pos)

        @pl.when(t == pos + D)
        def _():
            cut_values(0)

        @pl.when(t >= pos + D)
        def _():
            bytes_back(1, t - pos - D)

    cut_values(1)

    gq_rows = (jnp.transpose(gq_acc[...]) * SCORE_SCALE).astype(BF16)
    gains = jnp.concatenate([gmlp_acc[...], gain_acc[...]], axis=1)
    rows8 = [gains[:, 256 * i : 256 * (i + 1)] for i in range(8)]
    gains8 = jnp.concatenate(rows8 + [jnp.zeros((8, 256), F32)], axis=0).astype(BF16)
    for j in range(nb):
        misc_out[j, 0:rq] = gq_rows[j * rq : (j + 1) * rq, :]
        misc_out[j, rq : rq + 16] = gains8

    def misc1(i, slot):
        peer = lax.rem(blk + i, nb)
        return remote(
            misc_out.at[peer], misc_in.at[slot], m1_s.at[i - 1], m1_r.at[i - 1], doc, peer
        )

    def misc2(i, slot):
        return remote(
            misc2_out, misc2_in.at[slot], m2_s.at[i - 1], m2_r.at[i - 1],
            lax.rem(doc + i, nd), blk,
        )

    def misc3(i, rows):
        return remote(
            gq_ref.at[rows, :], gq_ref.at[rows, :], m3_s.at[i - 1], m3_r.at[i - 1],
            doc, lax.rem(blk + i, nb),
        )

    for i in range(1, nb):
        misc1(i, blk).start()
    misc_in[blk] = misc_out[blk]

    first = (parts + pos + 1) // 2
    last = max(weights.steps - 2, start0 + values[0].steps, first + values[1].steps)

    @pl.loop(first, last)
    def _(t):
        values[1].step(t - first, v_mate(1))
        values[0].step(t - start0, v_mate(0))
        weights.step(t + 2, w_mate, pos // 2)

        @pl.when(t == first + 1)
        def _():
            for i in range(1, nb):
                misc1(i, lax.rem(blk + nb - i, nb)).wait_recv()
            total = misc_in[0].astype(F32)
            for i in range(1, nb):
                total = total + misc_in[i].astype(F32)
            misc2_out[...] = total.astype(BF16)
            for i in range(1, nd):
                misc2(i, doc).start()
            misc2_in[doc] = misc2_out[...]

        @pl.when(t == first + 3)
        def _():
            for i in range(1, nd):
                misc2(i, lax.rem(doc + nd - i, nd)).wait_recv()
            total = misc2_in[0].astype(F32)
            for i in range(1, nd):
                total = total + misc2_in[i].astype(F32)
            gains_ref[...] = total[rq : rq + 8, :]
            gq_ref[own_rows, :] = total[0:rq].astype(BF16)
            for i in range(1, nb):
                misc3(i, own_rows).start()

    for i in range(1, nb):
        src = lax.rem(blk + nb - i, nb)
        misc3(i, pl.ds(pl.multiple_of(src * rq, rq), rq)).wait_recv()

    total = direct_out[...].astype(F32)
    for i in range(1, nd):
        direct_copy(i).wait_recv()
        total = total + dir_in[i - 1].astype(F32)
    dsum_ref[...] = total

    for n in range(D - 2, D):
        pltpu.make_async_copy(frames.at[n % 2, 0:kc, 0:din], bg_hbm.at[n], bg_s.at[n % 2]).wait()
    weights.drain()
    for g in range(2):
        values[g].drain()
        for s in range(pos):
            v_mate(g)(s).wait_send()
    for i in range(1, nb):
        delta_copy(i, own_rows).wait_send()
        misc1(i, blk).wait_send()
        misc3(i, own_rows).wait_send()
    for i in range(1, nd):
        direct_copy(i).wait_send()
        misc2(i, doc).wait_send()

    @pl.loop(0, parts)
    def _(e):
        mate_copy(e, p, c).wait_send()

        @pl.when(p < pos - 1)
        def _():
            right_copy(e, 0, p).wait_send()

        @pl.when(p > 0)
        def _():
            left_copy(e, 0, p).wait_send()

        for hop in range(pos - 1):
            j = p - 1 - hop

            @pl.when(j >= 0)
            def _():
                mate_copy(e, j, c).wait_send()
                if hop + 1 < pos - 1:
                    @pl.when(p < pos - 1)
                    def _():
                        right_copy(e, hop + 1, j).wait_send()

            i = p + 1 + hop

            @pl.when(i < pos)
            def _():
                mate_copy(e, i, c).wait_send()
                if hop + 1 < pos - 1:
                    @pl.when(p > 0)
                    def _():
                        left_copy(e, hop + 1, i).wait_send()


def backward(
    nb, nd, byte_embed, keys, values, w_out, w_up, w_down, w_key, w_value, cotangent,
    attended, latents, gain_mlp, bias, gain_bytes, queries, lse,
):
    D, kc, din = byte_embed.shape
    rq, dl = latents.shape
    pos = nb // 2
    rows = D * rq
    wunit, vunit = owner_rows(2 * dl // nb, nd), owner_rows(2 * din // nb, nd)
    whalf, vhalf = dl // 2, (DV + DQK) // 4
    vmem = pl.BlockSpec(memory_space=pltpu.VMEM)
    anywhere = pl.BlockSpec(memory_space=pl.ANY)
    dma = pltpu.SemaphoreType.DMA
    scratch = (
        shard_sum_scratch(nd, nb, 3 * pos, wunit, 2 * dl // nb, whalf)
        + shard_sum_scratch(nd, nb, pos, vunit, 2 * din // nb, vhalf)
        + shard_sum_scratch(nd, nb, pos, vunit, 2 * din // nb, vhalf)
        + [
            pltpu.VMEM((max(2 * dl, D * kc), dl), BF16),
            pltpu.VMEM((D, kc, din), BF16),
            pltpu.VMEM((D, kc, DQK), BF16),
            pltpu.VMEM((2 * D, LAT, DV // 2), BF16),
            pltpu.VMEM((LAT, 128), F32),
            pltpu.VMEM((D, HEADS, LAT), F32),
            pltpu.VMEM((HEADS, LAT, DQK // 2), BF16),
            pltpu.VMEM((2, din, (DV + DQK) // 2), BF16),
            pltpu.VMEM((kc, HEADS // 2 * LAT), BF16),
            pltpu.VMEM((kc, DV // 2), F32),
            pltpu.VMEM((DQK, LAT), F32),
            pltpu.VMEM((max(3 * rows, din), dl), F32),
            pltpu.VMEM((2, rows, dl), F32),
            pltpu.VMEM((dl, rows), BF16),
            pltpu.VMEM((rows, dl), BF16),
            pltpu.VMEM((max(2 * dl, D * kc), (DV + DQK) // 2), BF16),
            pltpu.VMEM((2, pos, 2 * din // nb, vhalf), BF16),
            pltpu.VMEM((1, din), F32),
            pltpu.VMEM((1, dl), F32),
            pltpu.VMEM((rq, dl), BF16),
            pltpu.VMEM((nd - 1, rq, dl), BF16),
            pltpu.VMEM((nb, rq + 16, 256), BF16),
            pltpu.VMEM((nb, rq + 16, 256), BF16),
            pltpu.VMEM((rq + 16, 256), BF16),
            pltpu.VMEM((nd, rq + 16, 256), BF16),
            dma((12,)), dma, dma((2,)),
            dma((2 * D, pos - 1)), dma((2 * D, pos - 1)),
            dma((2 * D, pos - 1)), dma((2 * D, pos - 1)),
            dma((2 * D, pos)), dma((2 * D, pos)),
            dma((nb - 1,)), dma((nb - 1,)), dma((nd - 1,)), dma((nd - 1,)),
            dma((nb - 1,)), dma((nb - 1,)), dma((nd - 1,)), dma((nd - 1,)),
            dma((nb - 1,)), dma((nb - 1,)),
        ]
    )
    return pl.pallas_call(
        functools.partial(backward_kernel, nb, nd, wunit, vunit),
        out_shape=(
            jax.ShapeDtypeStruct((rows, dl), F32),
            jax.ShapeDtypeStruct((D, kc, din), F32),
            jax.ShapeDtypeStruct((3, wunit * nd, whalf), BF16),
            jax.ShapeDtypeStruct((1, vunit * nd, vhalf), BF16),
            jax.ShapeDtypeStruct((1, vunit * nd, vhalf), BF16),
            jax.ShapeDtypeStruct((rq, dl), F32),
            jax.ShapeDtypeStruct((LAT, DQK), BF16),
            jax.ShapeDtypeStruct((8, 256), F32),
        ),
        in_specs=[anywhere] * 9 + [vmem] * 7,
        out_specs=(anywhere,) * 2 + (vmem,) * 6,
        scratch_shapes=scratch,
        compiler_params=pltpu.CompilerParams(
            collective_id=1, has_side_effects=True, vmem_limit_bytes=63 * 2**20
        ),
        name="backward",
    )(
        byte_embed, keys, values.reshape(D * kc, DV), w_out, w_up, w_down, w_key, w_value,
        cotangent.reshape(rows, dl), attended, latents, gain_mlp.reshape(1, -1), bias,
        gain_bytes.reshape(1, -1), queries, lse,
    )


def body(
    byte_embed,
    doc_lengths,
    key_mask,
    latents,
    gain_query,
    gain_bytes,
    gain_mlp,
    w_query,
    w_key,
    w_value,
    w_out,
    w_up,
    w_down,
    cotangent,
):
    nb, nd = lax.axis_size("blk"), lax.axis_size("doc")
    blk = lax.axis_index("blk")
    key_count, din = byte_embed.shape[1:]
    dl = latents.shape[1]
    positions = blk * key_count + jnp.arange(key_count, dtype=jnp.int32)
    usable = (positions[None, :] < doc_lengths[:, None]) & (key_mask == 1)
    bias = jnp.where(usable, 0.0, masked_score).astype(F32)
    attended, lse, keys, values, norm_cols, queries = forward(
        nb, byte_embed, bias, latents, gain_query, gain_bytes, w_query, w_key, w_value
    )
    latents_out, byte_grad, wsum, vsum0, vsum1, direct_sum, gq, gains = backward(
        nb, nd, byte_embed, keys, values, w_out, w_up, w_down, w_key, w_value, cotangent,
        attended, latents, gain_mlp, bias, gain_bytes, queries, lse,
    )
    latents_out = latents_out.reshape(cotangent.shape)

    def unfold(shard, rows):
        return jnp.concatenate([shard[:rows], shard[rows : 2 * rows]], axis=1).astype(F32)

    step = dl // nb
    grad_w_down, grad_w_up, grad_w_out = (unfold(wsum[m], step) for m in range(3))
    halves = [unfold(v[0], din // nb) for v in (vsum0, vsum1)]
    grad_w_value = jnp.concatenate([v[:, : DV // 2] for v in halves], axis=1)
    grad_w_key = jnp.concatenate([v[:, DV // 2 :] for v in halves], axis=1)
    gains = gains.reshape(-1)
    gain_mlp_grad = lax.dynamic_slice(gains[:dl], (blk * step,), (step,))
    gain_bytes_grad = lax.dynamic_slice(gains[dl:], (blk * (din // nb),), (din // nb,))
    skip = blk * step - jnp.minimum(blk * step // 128 * 128, dl - 256)
    cols = lax.dynamic_slice(norm_cols, (0, skip), (LAT, step))
    grad_w_query = lax.dot_general(
        cols, gq, (((0,), (0,)), ((), ())), preferred_element_type=F32
    )
    wq_rows = lax.dynamic_slice(w_query, (blk * step, 0), (step, DQK))
    dy_cols = dot_nt(gq, wq_rows)
    gain_rows = lax.dynamic_slice(gain_query, (blk * step,), (step,))
    gain_query_grad = jnp.sum(dy_cols * cols.astype(F32), axis=0) / gain_rows
    own = lax.dynamic_slice(gq, (blk * latents.shape[0], 0), (latents.shape[0], DQK))
    dxh = dot_nt(own, w_query) * gain_query
    xh, inv = norm_parts(latents)
    latents_grad = direct_sum + inv * (
        dxh
        - jnp.mean(dxh, axis=-1, keepdims=True)
        - xh * jnp.mean(dxh * xh, axis=-1, keepdims=True)
    )
    return (
        latents_out,
        byte_grad,
        latents_grad,
        gain_query_grad,
        gain_bytes_grad,
        gain_mlp_grad,
        grad_w_query,
        grad_w_key,
        grad_w_value,
        grad_w_out,
        grad_w_up,
        grad_w_down,
    )


def solution(mesh):
    in_specs = (
        P("doc", "blk", None),
        P("doc"),
        P("doc", "blk"),
        P("blk", None),
        P(),
        P(),
        P(),
        P(),
        P(),
        P(),
        P(),
        P(),
        P(),
        P("doc", "blk", None),
    )
    out_specs = (
        P("doc", "blk", None),
        P("doc", "blk", None),
        P("blk", None),
        P("blk"),
        P("blk"),
        P("blk"),
        P("blk", None),
        P("blk", None),
        P("blk", None),
        P("blk", None),
        P("blk", None),
        P("blk", None),
    )
    return jax.shard_map(body, mesh=mesh, in_specs=in_specs, out_specs=out_specs, check_vma=False)
```

```python
import functools
import math

import jax
import jax.numpy as jnp
from jax import lax
from jax.experimental import pallas as pl
from jax.experimental.pallas import tpu as pltpu
from jax.sharding import PartitionSpec as P

LAT = 256
HEADS = 8
QK_HEAD = 32
V_HEAD = 160
DQK = HEADS * QK_HEAD
DV = HEADS * V_HEAD
MESH = pl.DeviceIdType.MESH
F32 = jnp.float32
BF16 = jnp.bfloat16

epsilon = 1e-05
masked_score = -1e30
LOG2E = math.log2(math.e)
SCORE2 = QK_HEAD ** (-0.5) * LOG2E
SCORE_SCALE = QK_HEAD ** (-0.5)


def dot_nn(a, b):
    return jnp.dot(a, b, preferred_element_type=F32)


def dot_nt(a, b):
    return lax.dot_general(a, b, (((1,), (1,)), ((), ())), preferred_element_type=F32)


def norm_parts(v):
    centered = v - jnp.mean(v, axis=-1, keepdims=True)
    spread = jnp.mean(centered * centered, axis=-1, keepdims=True)
    inv = lax.rsqrt(spread + epsilon)
    return centered * inv, inv


def window(h):
    return V_HEAD * h // 128 * 128


def value_mask(h, rows):
    lane = lax.broadcasted_iota(jnp.int32, (rows, 256), 1) + window(h)
    keep = (lane >= V_HEAD * h) & (lane < V_HEAD * (h + 1))
    return jnp.where(keep, 1.0, 0.0).astype(BF16)


def query_mask(h, rows):
    lane = lax.broadcasted_iota(jnp.int32, (rows, DQK), 1)
    keep = (lane >= QK_HEAD * h) & (lane < QK_HEAD * (h + 1))
    return jnp.where(keep, 1.0, 0.0).astype(BF16)


def row_to_lanes(row):
    return jnp.transpose(jnp.broadcast_to(row, (128, row.shape[1])))


def wide(col, n):
    return jnp.concatenate([col] * (n // 128), axis=1) if n > 128 else col


def remote(src, dst, send, recv, doc, blk):
    return pltpu.make_async_remote_copy(
        src_ref=src, dst_ref=dst, send_sem=send, recv_sem=recv,
        device_id=(doc, blk), device_id_type=MESH,
    )


def forward_kernel(
    nb,
    x_ref, len_ref, mask_ref, lat_ref, gq_ref, gb_ref, wq_ref, wk_ref, wv_ref,
    att_ref, lse_ref, k_ref, v_ref, nlw_ref, qall_ref, bias_ref,
    nl_cols, normed, qm, lloc, lmate, lz, acc, part, mate_in, rin, lin,
    q_s, q_r, n_s, n_r, l_s, l_r, mate_s, mate_r, rs_s, rs_r, ls_s, ls_r,
):
    D, kc, din = x_ref.shape
    rq = lat_ref.shape[0]
    pos = nb // 2
    doc, blk = lax.axis_index("doc"), lax.axis_index("blk")
    p, c = blk // 2, blk % 2
    mate = 2 * p + 1 - c
    barrier = pltpu.get_barrier_semaphore()
    for i in range(1, nb):
        pl.semaphore_signal(
            barrier, inc=1, device_id=(doc, lax.rem(blk + i, nb)), device_id_type=MESH
        )

    slots = blk * kc + lax.broadcasted_iota(jnp.int32, (1, kc), 1)
    for n in range(D):
        usable = (slots < len_ref[n]) & (mask_ref[n : n + 1, :] == 1)
        bias_ref[n : n + 1, :] = jnp.where(usable, 0.0, masked_score)

    xhat, _ = norm_parts(lat_ref[...])
    nl = (xhat * gq_ref[...].reshape(1, -1)).astype(BF16)
    step = nl.shape[1] // nb
    for j in range(nb):
        at = min(j * step // 128 * 128, nl.shape[1] - 256)
        nl_cols[j] = nl[:, at : at + 256]
    own = pl.ds(pl.multiple_of(blk * rq, rq), rq)
    qall_ref[own, :] = dot_nn(nl, wq_ref[...]).astype(BF16)
    pl.semaphore_wait(barrier, nb - 1)

    def q_copy(i, slot):
        return remote(
            qall_ref.at[own, :], qall_ref.at[slot, :], q_s.at[i - 1], q_r.at[i - 1],
            doc, lax.rem(blk + i, nb),
        )

    def n_copy(i, slot):
        peer = lax.rem(blk + i, nb)
        return remote(
            nl_cols.at[peer], nlw_ref.at[slot, :], n_s.at[i - 1], n_r.at[i - 1], doc, peer
        )

    for i in range(1, nb):
        q_copy(i, own).start()
    for i in range(1, nb):
        n_copy(i, own).start()
    nlw_ref[own, :] = nl_cols[blk]

    @pl.loop(0, D)
    def _(n):
        xh, _ = norm_parts(x_ref[n].astype(F32))
        normed[n] = (xh * gb_ref[...].reshape(1, -1)).astype(BF16)
        k_ref[n] = dot_nn(normed[n], wk_ref[...]).astype(BF16)

    for i in range(1, nb):
        src = lax.rem(blk + nb - i, nb)
        q_copy(i, pl.ds(pl.multiple_of(src * rq, rq), rq)).wait_recv()
    for h in range(HEADS):
        qm[h] = qall_ref[...] * query_mask(h, LAT)

    @pl.loop(0, D)
    def _(n):
        bias = wide(row_to_lanes(bias_ref[pl.ds(n, 1), :]), LAT)
        kn = k_ref[n]
        rows = []
        for h in range(HEADS):
            s = dot_nt(kn, qm[h]) * SCORE2 + bias
            top = jnp.max(s, axis=0, keepdims=True)
            tot = jnp.sum(jnp.exp2(s - top), axis=0, keepdims=True)
            rows.append(top + jnp.log(tot) * LOG2E)
        lloc[n] = jnp.concatenate(rows, axis=0)

    half = D // 2
    mine, other = pl.ds(c * half, half), pl.ds((1 - c) * half, half)

    def merge(a, b):
        top = jnp.maximum(a, b)
        return top + jnp.log(jnp.exp2(a - top) + jnp.exp2(b - top)) * LOG2E

    first = remote(lloc.at[other], lmate, l_s.at[0], l_r.at[0], doc, mate)
    first.start()

    def values(lo, hi):
        @pl.loop(lo, hi)
        def _(n):
            v_ref[n] = dot_nn(normed[n], wv_ref[...]).astype(BF16)

    values(0, D // 4)
    first.wait_recv()
    lz[p] = merge(lloc[mine], lmate[...])

    def z_copy(i, slot):
        return remote(
            lz.at[p], lz.at[slot], l_s.at[i], l_r.at[i],
            doc, 2 * lax.rem(p + i, pos) + c,
        )

    for i in range(1, pos):
        z_copy(i, p).start()
    values(D // 4, 3 * D // 4)
    for i in range(1, pos):
        z_copy(i, lax.rem(p + pos - i, pos)).wait_recv()
    total = lz[0]
    for i in range(1, pos):
        total = merge(total, lz[i])
    lse_ref[mine] = total
    last = remote(lse_ref.at[mine], lse_ref.at[mine], l_s.at[pos], l_r.at[pos], doc, mate)
    last.start()
    values(3 * D // 4, D)
    remote(
        lse_ref.at[other], lse_ref.at[other], l_s.at[pos], l_r.at[pos], doc, mate
    ).wait_recv()

    def mate_copy(n):
        return remote(
            part.at[n, 1 - c], mate_in.at[n], mate_s.at[n], mate_r.at[n], doc, mate
        )

    def right_copy(n, j, src):
        return remote(
            src, rin.at[n, j], rs_s.at[n, j], rs_r.at[n, j],
            doc, 2 * jnp.minimum(p + 1, pos - 1) + c,
        )

    def left_copy(n, j, src):
        return remote(
            src, lin.at[n, j], ls_s.at[n, j], ls_r.at[n, j],
            doc, 2 * jnp.maximum(p - 1, 0) + c,
        )

    def chip_sum(n):
        mate_copy(n).wait_recv()
        for j in range(pos):
            both = part[n, c, j].astype(F32) + mate_in[n, j].astype(F32)
            part[n, c, j] = both.astype(BF16)

            @pl.when((p == 0) & (j > 0))
            def _():
                right_copy(n, j, part.at[n, c, j]).start()

            @pl.when((p == pos - 1) & (j < pos - 1))
            def _():
                left_copy(n, j, part.at[n, c, j]).start()

    @pl.loop(0, D)
    def _(n):
        logs = lse_ref[n]
        logs_t = jnp.transpose(jnp.concatenate([logs] * (128 // HEADS), axis=0))
        bias = bias_ref[pl.ds(n, 1), :]
        kn = k_ref[n]
        acc[...] = jnp.zeros_like(acc)
        for h in range(HEADS):
            s = dot_nt(qm[h], kn) * SCORE2 + bias
            prob = jnp.exp2(s - logs_t[:, h : h + 1]).astype(BF16)
            cols = slice(window(h), window(h) + 256)
            acc[:, cols] += dot_nn(prob, v_ref[n, :, cols] * value_mask(h, kc))
        for j in range(nb):
            part[n, j % 2, j // 2] = acc[rq * j : rq * (j + 1), :].astype(BF16)
        mate_copy(n).start()

        @pl.when(n > 0)
        def _():
            chip_sum(n - 1)

    chip_sum(D - 1)

    def from_left(n):
        for j in range(1, pos):
            @pl.when(j >= p)
            def _():
                right_copy(n, j, part.at[n, c, j]).wait_recv()

            @pl.when(j > p)
            def _():
                both = rin[n, j].astype(F32) + part[n, c, j].astype(F32)
                part[n, c, j] = both.astype(BF16)
                right_copy(n, j, part.at[n, c, j]).start()

    def from_right(n):
        for j in range(pos - 2, -1, -1):
            @pl.when(j <= p)
            def _():
                left_copy(n, j, part.at[n, c, j]).wait_recv()

            @pl.when(j < p)
            def _():
                both = lin[n, j].astype(F32) + part[n, c, j].astype(F32)
                part[n, c, j] = both.astype(BF16)
                left_copy(n, j, part.at[n, c, j]).start()

    def finish(n):
        acc[0:rq, :] = part[n, c, p].astype(F32)

        @pl.when(p > 0)
        def _():
            acc[0:rq, :] += rin[n, p].astype(F32)

        @pl.when(p < pos - 1)
        def _():
            acc[0:rq, :] += lin[n, p].astype(F32)

        att_ref[n] = acc[0:rq, :].astype(BF16)

    @pl.loop(0, D + pos - 1)
    def _(t):
        right_n, left_n, done_n = t - p, t - (pos - 1 - p), t - (pos - 1)

        @pl.when((p > 0) & (right_n >= 0) & (right_n < D))
        def _():
            from_left(right_n)

        @pl.when((p < pos - 1) & (left_n >= 0) & (left_n < D))
        def _():
            from_right(left_n)

        @pl.when(done_n >= 0)
        def _():
            finish(done_n)

    for i in range(1, nb):
        src = lax.rem(blk + nb - i, nb)
        n_copy(i, pl.ds(pl.multiple_of(src * rq, rq), rq)).wait_recv()

    for i in range(1, nb):
        q_copy(i, own).wait_send()
        n_copy(i, own).wait_send()
    first.wait_send()
    for i in range(1, pos):
        z_copy(i, p).wait_send()
    last.wait_send()

    @pl.loop(0, D)
    def _(n):
        mate_copy(n).wait_send()
        for j in range(pos):
            @pl.when((j > p) & (p < pos - 1))
            def _():
                right_copy(n, j, part.at[n, c, j]).wait_send()

            @pl.when((j < p) & (p > 0))
            def _():
                left_copy(n, j, part.at[n, c, j]).wait_send()


def forward(
    nb, byte_embed, doc_lengths, key_mask, latents, gain_query, gain_bytes, w_query, w_key, w_value
):
    D, kc, din = byte_embed.shape
    rq, dl = latents.shape
    pos = nb // 2
    vmem = pl.BlockSpec(memory_space=pltpu.VMEM)
    dma = pltpu.SemaphoreType.DMA
    return pl.pallas_call(
        functools.partial(forward_kernel, nb),
        out_shape=(
            jax.ShapeDtypeStruct((D, rq, DV), BF16),
            jax.ShapeDtypeStruct((D, HEADS, LAT), F32),
            jax.ShapeDtypeStruct((D, kc, DQK), BF16),
            jax.ShapeDtypeStruct((D, kc, DV), BF16),
            jax.ShapeDtypeStruct((LAT, 256), BF16),
            jax.ShapeDtypeStruct((LAT, DQK), BF16),
            jax.ShapeDtypeStruct((D, kc), F32),
        ),
        in_specs=[vmem, pl.BlockSpec(memory_space=pltpu.SMEM)] + [vmem] * 7,
        out_specs=(vmem,) * 7,
        scratch_shapes=[
            pltpu.VMEM((nb, rq, 256), BF16),
            pltpu.VMEM((D, kc, din), BF16),
            pltpu.VMEM((HEADS, LAT, DQK), BF16),
            pltpu.VMEM((D, HEADS, LAT), F32),
            pltpu.VMEM((D // 2, HEADS, LAT), F32),
            pltpu.VMEM((pos, D // 2, HEADS, LAT), F32),
            pltpu.VMEM((LAT, DV), F32),
            pltpu.VMEM((D, 2, pos, rq, DV), BF16),
            pltpu.VMEM((D, pos, rq, DV), BF16),
            pltpu.VMEM((D, pos, rq, DV), BF16),
            pltpu.VMEM((D, pos, rq, DV), BF16),
            dma((nb - 1,)), dma((nb - 1,)), dma((nb - 1,)), dma((nb - 1,)),
            dma((pos + 1,)), dma((pos + 1,)),
            dma((D,)), dma((D,)),
            dma((D, pos)), dma((D, pos)), dma((D, pos)), dma((D, pos)),
        ],
        compiler_params=pltpu.CompilerParams(
            collective_id=0, has_side_effects=True, vmem_limit_bytes=56 * 2**20
        ),
        name="forward",
    )(
        byte_embed, doc_lengths, key_mask, latents, gain_query, gain_bytes, w_query, w_key, w_value,
    )


def gelu_parts(u):
    k = math.sqrt(2.0 / math.pi)
    sq = u * u
    t = jnp.tanh(k * u * (1.0 + 0.044715 * sq))
    value = 0.5 * u * (1.0 + t)
    slope = 0.5 * (1.0 + t) + 0.5 * k * u * (1.0 - t * t) * (1.0 + 3 * 0.044715 * sq)
    return value, slope


def owner_rows(total, docs):
    return -(-total // (16 * docs)) * 16


class ShardSums:
    def __init__(
        self, doc, blk, nd, nb, count, unit, group, lags, direct,
        own, mate_in, inbox, rin, lin, out, sems,
    ):
        self.doc, self.p, self.c = doc, blk // 2, blk % 2
        self.nd, self.pos, self.count, self.unit = nd, nb // 2, count, unit
        self.bits = nd.bit_length() - 1
        self.own, self.mate_in, self.inbox = own, mate_in, inbox
        self.rin, self.lin, self.out = rin, lin, out
        (
            self.mate_s, self.mate_r, self.in_s, self.in_r,
            self.right_s, self.right_r, self.left_s, self.left_r, self.out_s, self.out_r,
        ) = sems
        self.group, self.lags, self.direct = group, lags, direct
        self.steps = count // group + lags[-1] + (1 if direct else self.pos - 1)

    def weight(self, s, k):
        b = (s + k) % self.bits
        return 1 + b * (b + 1) // 2

    def my_bit(self, w):
        return (self.doc // w) % 2

    def quarter(self, s, k, i, sent):
        q = 0
        for r in range(k):
            w = self.weight(s, r)
            q = q + self.my_bit(w) * w
        w = self.weight(s, k)
        mine = self.my_bit(w)
        q = q + ((1 - mine) if sent else mine) * w
        for r in range(k + 1, self.bits):
            q = q + ((i >> (r - k - 1)) & 1) * self.weight(s, r)
        return q

    def width(self, k):
        return 2 ** (self.bits - 1 - k)

    def slot(self, k, i):
        return sum(self.width(r) for r in range(k)) + i

    def rows(self, q):
        return pl.ds(pl.multiple_of(q * self.unit, self.unit), self.unit)

    def halving(self, s, k, i):
        w = self.weight(s, k)
        peer = self.doc + w * (1 - 2 * self.my_bit(w))
        slot = self.slot(k, i)
        return remote(
            self.own.at[s, self.rows(self.quarter(s, k, i, True)), :], self.inbox.at[s, slot],
            self.in_s.at[s, slot], self.in_r.at[s, slot], peer, 2 * self.p + self.c,
        )

    def right(self, s):
        return remote(
            self.own.at[s, self.rows(self.doc), :], self.rin.at[s],
            self.right_s.at[s], self.right_r.at[s],
            self.doc, 2 * jnp.minimum(self.p + 1, self.pos - 1) + self.c,
        )

    def left(self, s):
        return remote(
            self.own.at[s, self.rows(self.doc), :], self.lin.at[s],
            self.left_s.at[s], self.left_r.at[s],
            self.doc, 2 * jnp.maximum(self.p - 1, 0) + self.c,
        )

    def share(self, m, i):
        return remote(
            self.out.at[m, self.rows(self.doc), :], self.out.at[m, self.rows(self.doc), :],
            self.out_s.at[m, i - 1], self.out_r.at[m, i - 1],
            lax.rem(self.doc + i, self.nd), 2 * self.p + self.c,
        )

    def shared(self, m, i):
        src = lax.rem(self.doc + self.nd - i, self.nd)
        return remote(
            self.out.at[m, self.rows(src), :], self.out.at[m, self.rows(src), :],
            self.out_s.at[m, i - 1], self.out_r.at[m, i - 1], src, 2 * self.p + self.c,
        )

    def add(self, s, q, other):
        rows = self.rows(q)
        self.own[s, rows, :] = (
            self.own[s, rows, :].astype(F32) + other.astype(F32)
        ).astype(BF16)

    def begin(self, s, mate_copy):
        mate_copy(s).wait_recv()
        rows = self.mate_in.shape[1]
        self.own[s, 0:rows, :] = (
            self.own[s, 0:rows, :].astype(F32) + self.mate_in[s].astype(F32)
        ).astype(BF16)
        for i in range(self.width(0)):
            self.halving(s, 0, i).start()

    def halve(self, s, k):
        for i in range(self.width(k - 1)):
            self.halving(s, k - 1, i).wait_recv()
            self.add(s, self.quarter(s, k - 1, i, False), self.inbox[s, self.slot(k - 1, i)])
        if k < self.bits:
            for i in range(self.width(k)):
                self.halving(s, k, i).start()
            return
        if self.direct:
            return
        j = s % self.pos

        @pl.when((self.p == 0) & (j > 0))
        def _():
            self.right(s).start()

        @pl.when((self.p == self.pos - 1) & (j < self.pos - 1))
        def _():
            self.left(s).start()

    def from_left(self, s):
        j = s % self.pos

        @pl.when(j >= self.p)
        def _():
            self.right(s).wait_recv()

        @pl.when(j > self.p)
        def _():
            self.add(s, self.doc, self.rin[s])
            self.right(s).start()

    def from_right(self, s):
        j = s % self.pos

        @pl.when(j <= self.p)
        def _():
            self.left(s).wait_recv()

        @pl.when(j < self.p)
        def _():
            self.add(s, self.doc, self.lin[s])
            self.left(s).start()

    def finish(self, s):
        @pl.when(s % self.pos == self.p)
        def _():
            m = s // self.pos

            @pl.when(self.p > 0)
            def _():
                self.add(s, self.doc, self.rin[s])

            @pl.when(self.p < self.pos - 1)
            def _():
                self.add(s, self.doc, self.lin[s])

            self.out[m, self.rows(self.doc), :] = self.own[s, self.rows(self.doc), :]
            for i in range(1, self.nd):
                self.share(m, i).start()

    def spread(self, i, back):
        to = lax.rem(self.p + (self.pos - i if back else i), self.pos)
        return remote(
            self.own.at[to, self.rows(self.doc), :], self.rin.at[i - 1],
            self.right_s.at[i - 1], self.right_r.at[i - 1], self.doc, 2 * to + self.c,
        )

    def scatter(self):
        for i in range(1, self.pos):
            self.spread(i, False).start()

    def collect(self):
        rows = self.rows(self.doc)
        total = self.own[self.p, rows, :].astype(F32)
        for i in range(1, self.pos):
            self.spread(i, True).wait_recv()
            total = total + self.rin[i - 1].astype(F32)
        self.out[0, rows, :] = total.astype(BF16)
        for i in range(1, self.nd):
            self.share(0, i).start()

    def step(self, t, mate_copy):
        def at(t, when, run, turned=False):
            @pl.when((t >= 0) & (t < self.count // self.group) & when)
            def _():
                for i in range(self.group):
                    run(t * self.group + (self.group - 1 - i if turned else i))

        at(t, True, lambda s: self.begin(s, mate_copy))
        for k in range(1, self.bits + 1):
            at(t - self.lags[k - 1], True, functools.partial(self.halve, k=k))
        base = t - self.lags[-1]
        if self.direct:
            pl.when(base == 0)(self.scatter)
            pl.when(base == 1)(self.collect)
            return
        at(base - self.p, self.p > 0, self.from_left, True)
        at(base - (self.pos - 1 - self.p), self.p < self.pos - 1, self.from_right)
        at(base - (self.pos - 1), True, self.finish)

    def drain(self):
        if self.direct:
            for i in range(1, self.pos):
                self.spread(i, False).wait_send()
        for m in range(self.count // self.pos):
            for i in range(1, self.nd):
                self.shared(m, i).wait_recv()
                self.share(m, i).wait_send()

        @pl.loop(0, self.count)
        def _(s):
            for k in range(self.bits):
                for i in range(self.width(k)):
                    self.halving(s, k, i).wait_send()
            if self.direct:
                return
            j = s % self.pos

            @pl.when((j > self.p) & (self.p < self.pos - 1))
            def _():
                self.right(s).wait_send()

            @pl.when((j < self.p) & (self.p > 0))
            def _():
                self.left(s).wait_send()


def shard_sum_scratch(nd, nb, count, unit, rows, width):
    dma = pltpu.SemaphoreType.DMA
    arrays = count // (nb // 2)
    return [
        pltpu.VMEM((count, unit * nd, width), BF16),
        pltpu.VMEM((count, rows, width), BF16),
        pltpu.VMEM((count, nd - 1, unit, width), BF16),
        pltpu.VMEM((count, unit, width), BF16),
        pltpu.VMEM((count, unit, width), BF16),
        dma((count,)), dma((count,)),
        dma((count, nd - 1)), dma((count, nd - 1)),
        dma((count,)), dma((count,)), dma((count,)), dma((count,)),
        dma((arrays, nd - 1)), dma((arrays, nd - 1)),
    ]


def backward_kernel(nb, nd, wunit, vunit, *refs):
    (
        x_hbm, k_hbm, v_hbm, wo_hbm, wu_hbm, wd_hbm, wk_hbm, wv_hbm, cot_hbm,
        att_ref, lat_ref, gm_ref, bias_ref, gb_ref, qall_ref, lse_ref,
    ) = refs[:16]
    out_hbm, bg_hbm, wsum_ref, vsum0_ref, vsum1_ref, dsum_ref, gq_ref, gains_ref = refs[16:24]
    wscr, vscr = refs[24:39], (refs[39:54], refs[54:69])
    (
        wpool, x_ref, k_ref, ga_all, delta_all, delta_t, qm, wkv, ds_all, gv_acc, gq_acc,
        fpool, frames, low_t, nm, act_low, gm, g_up, gb, stage, vstage, gain_acc, gmlp_acc, direct_out, dir_in,
        misc_out, misc_in, misc2_out, misc2_in,
        load_s, out_s, bg_s, ar_s, ar_r, al_s, al_r, am_s, am_r, d_s, d_r, dir_s, dir_r,
        m1_s, m1_r, m2_s, m2_r, m3_s, m3_r,
    ) = refs[69:]
    D, kc, din = x_ref.shape
    rq, dl = lat_ref.shape
    rows_all = D * rq
    pos = nb // 2
    hh, vh, qh = HEADS // 2, DV // 2, DQK // 2
    bits = nd.bit_length() - 1
    doc, blk = lax.axis_index("doc"), lax.axis_index("blk")
    p, c = blk // 2, blk % 2
    mate = 2 * p + 1 - c

    barrier = pltpu.get_barrier_semaphore()
    for i in range(1, nb):
        pl.semaphore_signal(
            barrier, inc=1, device_id=(doc, lax.rem(blk + i, nb)), device_id_type=MESH
        )
    for i in range(1, nd):
        pl.semaphore_signal(
            barrier, inc=1, device_id=(lax.rem(doc + i, nd), blk), device_id_type=MESH
        )

    def load(src, dst, i):
        return pltpu.make_async_copy(src, dst, load_s.at[i])

    slot0, slot1 = wpool.at[0:dl, :], wpool.at[dl : 2 * dl, :]
    load_out, load_up = load(wo_hbm, slot0, 0), load(wu_hbm, slot1, 1)
    load_down, load_out2 = load(wd_hbm, slot0, 2), load(wo_hbm, slot0, 3)
    load_v = load(v_hbm, wpool.at[0 : D * kc, :], 4)
    load_cot = load(cot_hbm, frames.at[1], 5)
    later = [load(k_hbm, k_ref, 6), load(x_hbm, x_ref, 7)]
    for g in range(2):
        later.append(load(wv_hbm.at[:, g * vh : (g + 1) * vh], wkv.at[g, :, 0:vh], 8 + g))
        later.append(
            load(wk_hbm.at[:, g * qh : (g + 1) * qh], wkv.at[g, :, vh : vh + qh], 10 + g)
        )
    load_out.start()
    load_up.start()
    load_cot.start()

    weights = ShardSums(
        doc, blk, nd, nb, 3 * pos, wunit, 2, [4 + k for k in range(bits)], False,
        *wscr[:5], wsum_ref, wscr[5:],
    )
    values = [
        ShardSums(
            doc, blk, nd, nb, pos, vunit, pos, lags, True, *vscr[g][:5], out, vscr[g][5:],
        )
        for g, (lags, out) in enumerate(
            (
                ([2 + k for k in range(bits)], vsum0_ref),
                ([1 + k for k in range(bits)], vsum1_ref),
            )
        )
    ]

    wrows, whalf = 2 * dl // nb, dl // 2
    vhalf = (vh + qh) // 2

    def w_mate(s):
        rows = pl.ds(pl.multiple_of(s % (2 * pos) * wrows, wrows), wrows)
        return remote(
            stage.at[rows, 0:whalf], weights.mate_in.at[s],
            weights.mate_s.at[s], weights.mate_r.at[s], doc, mate,
        )

    def v_mate(g):
        return lambda s: remote(
            vstage.at[g, s], values[g].mate_in.at[s],
            values[g].mate_s.at[s], values[g].mate_r.at[s], doc, mate,
        )

    parts, ahead = 2 * D, 4

    def chunk(j, core):
        return pl.ds(pl.multiple_of((2 * j + core) * rq, rq), rq)

    def right_copy(e, hop, j):
        rows = ga_all.at[e, chunk(j, c), :]
        return remote(
            rows, rows, ar_s.at[e, hop], ar_r.at[e, hop],
            doc, 2 * jnp.minimum(p + 1, pos - 1) + c,
        )

    def left_copy(e, hop, j):
        rows = ga_all.at[e, chunk(j, c), :]
        return remote(
            rows, rows, al_s.at[e, hop], al_r.at[e, hop],
            doc, 2 * jnp.maximum(p - 1, 0) + c,
        )

    def mate_copy(e, j, core):
        rows = ga_all.at[e, chunk(j, core), :]
        return remote(rows, rows, am_s.at[e, j], am_r.at[e, j], doc, mate)

    own_rows = pl.ds(pl.multiple_of(blk * rq, rq), rq)

    def delta_copy(i, rows):
        return remote(
            delta_all.at[rows, :], delta_all.at[rows, :], d_s.at[i - 1], d_r.at[i - 1],
            doc, lax.rem(blk + i, nb),
        )

    def direct_copy(i):
        return remote(
            direct_out, dir_in.at[i - 1], dir_s.at[i - 1], dir_r.at[i - 1],
            lax.rem(doc + i, nd), blk,
        )

    def send_own(e):
        @pl.when(p < pos - 1)
        def _():
            right_copy(e, 0, p).start()

        @pl.when(p > 0)
        def _():
            left_copy(e, 0, p).start()

        mate_copy(e, p, c).start()

    mid = fpool.at[0:rows_all, :]
    xhat = fpool.at[rows_all : 2 * rows_all, :]
    slope = fpool.at[2 * rows_all : 3 * rows_all, :]
    kv_acc = fpool.at[0:din, 0 : vh + qh]
    step_w = dl // nb

    def weight_grad(m, left, right):
        low_t[...] = jnp.transpose(left[...])

        @pl.loop(0, pos)
        def _(j):
            s = m * pos + j
            for core in (1 - c, c):
                rows = pl.ds(pl.multiple_of((2 * j + core) * step_w, step_w), step_w)
                shard = dot_nn(low_t[rows, :], right[...]).astype(BF16)
                for i in range(2):
                    part = shard[:, i * whalf : (i + 1) * whalf]
                    if core is c:
                        weights.own[s, i * step_w : (i + 1) * step_w, :] = part
                    else:
                        at = pl.multiple_of(s % (2 * pos) * wrows, wrows) + i * step_w
                        stage[pl.ds(pl.multiple_of(at, 16), step_w), 0:whalf] = part
                if core is not c:
                    w_mate(s).start()

    att_low = att_ref[...].reshape(rows_all, DV)
    load_out.wait()
    mid[...] = dot_nn(att_low, slot0[...]) + jnp.concatenate([lat_ref[...]] * D, axis=0)
    load_down.start()
    xh, inv = norm_parts(mid[...])
    xhat[...] = xh
    nm[...] = (xh * gm_ref[...].reshape(1, -1)).astype(BF16)
    load_up.wait()
    act, sl = gelu_parts(dot_nn(nm[...], slot1[...]))
    slope[...] = sl
    act_low[...] = act.astype(BF16)
    load_cot.wait()
    gm[...] = frames[1].astype(BF16)
    load_down.wait()
    frames[0] = mid[...] + dot_nn(act_low[...], slot0[...])
    store_out = pltpu.make_async_copy(frames.at[0], out_hbm, out_s)
    store_out.start()
    g_up[...] = (dot_nt(gm[...], slot0[...]) * slope[...]).astype(BF16)
    load_out2.start()
    for item in later:
        item.start()
    g_nm = dot_nt(g_up[...], slot1[...])
    gmlp_acc[...] = jnp.sum(g_nm * xhat[...], axis=0, keepdims=True)
    dxh = g_nm * gm_ref[...].reshape(1, -1)
    mid[...] = frames[1] + inv * (
        dxh
        - jnp.mean(dxh, axis=-1, keepdims=True)
        - xhat[...] * jnp.mean(dxh * xhat[...], axis=-1, keepdims=True)
    )
    gb[...] = mid[...].astype(BF16)
    load_out2.wait()
    ga = dot_nt(gb[...], slot0[...])
    load_v.start()
    for g in range(2):
        for n in range(D):
            ga_all[g * D + n, own_rows, :] = ga[
                n * rq : (n + 1) * rq, g * vh : (g + 1) * vh
            ].astype(BF16)
    pl.semaphore_wait(barrier, nb - 1 + nd - 1)
    for e in range(ahead):
        send_own(e)
    weight_grad(0, act_low, gm)
    lane = lax.broadcasted_iota(jnp.int32, (rq, 128), 1)
    delta = jnp.zeros((rq, 128), F32)
    for h in range(HEADS):
        cols = slice(window(h), window(h) + 256)
        prod = ga[:, cols] * (att_low[:, cols] * value_mask(h, rows_all)).astype(F32)
        one = jnp.sum(prod, axis=1, keepdims=True)
        for n in range(D):
            delta = delta + jnp.where(lane == n * HEADS + h, one[n * rq : (n + 1) * rq], 0.0)
    delta_all[own_rows, :] = delta
    for i in range(1, nb):
        delta_copy(i, own_rows).start()
    direct = mid[0:rq, :]
    for n in range(1, D):
        direct = direct + mid[n * rq : (n + 1) * rq, :]
    direct_out[...] = direct.astype(BF16)
    for i in range(1, nd):
        direct_copy(i).start()
    weight_grad(1, nm, g_up)
    for s in range(pos):
        w_mate(s).wait_send()
    weight_grad(2, att_low, gb)

    for h in range(HEADS):
        half = slice(h // hh * qh, h // hh * qh + qh)
        qm[h] = (qall_ref[...] * query_mask(h, LAT))[:, half]
    gq_acc[...] = jnp.zeros_like(gq_acc)
    kv_acc[...] = jnp.zeros((din, vh + qh), F32)
    gain_acc[...] = jnp.zeros_like(gain_acc)

    def forward_chunks(e, hop):
        j = p - 1 - hop

        @pl.when(j >= 0)
        def _():
            right_copy(e, hop, j).wait_recv()
            if hop + 1 < pos - 1:
                @pl.when(p < pos - 1)
                def _():
                    right_copy(e, hop + 1, j).start()

            mate_copy(e, j, c).start()

        i = p + 1 + hop

        @pl.when(i < pos)
        def _():
            left_copy(e, hop, i).wait_recv()
            if hop + 1 < pos - 1:
                @pl.when(p > 0)
                def _():
                    left_copy(e, hop + 1, i).start()

            mate_copy(e, i, c).start()

    def doc_rows(n):
        return pl.ds(pl.multiple_of(n * kc, kc), kc)

    def bytes_back(g, n):
        e = g * D + n
        for j in range(pos):
            mate_copy(e, j, 1 - c).wait_recv()
        bias = wide(row_to_lanes(bias_ref[pl.ds(n, 1), :]), LAT)
        logs, deltas = lse_ref[n], delta_t[n]
        kn = k_ref[n, :, g * qh : (g + 1) * qh]
        kt = jnp.transpose(kn)
        gv_acc[...] = jnp.zeros_like(gv_acc)
        for i in range(hh):
            h = g * hh + i
            cols = slice(window(i), window(i) + 256)
            vcols = slice(g * vh + window(i), g * vh + window(i) + 256)
            gah = ga_all[e, :, cols] * value_mask(i, LAT)
            s = dot_nt(kn, qm[h]) * SCORE2 + bias
            prob = jnp.exp2(s - logs[h : h + 1, :])
            dprob = dot_nt(wpool[doc_rows(n), vcols], gah)
            ds = (prob * (dprob - deltas[h : h + 1, :])).astype(BF16)
            ds_all[:, i * LAT : (i + 1) * LAT] = ds
            gv_acc[:, cols] += dot_nn(prob.astype(BF16), gah)
            head = slice(QK_HEAD * i, QK_HEAD * (i + 1))
            rows = slice(QK_HEAD * h, QK_HEAD * (h + 1))
            gq_acc[rows, :] += dot_nn(kt[head, :], ds)
        gk = dot_nn(ds_all[:, 0:LAT], qm[g * hh])
        for i in range(1, hh):
            gk = gk + dot_nn(ds_all[:, i * LAT : (i + 1) * LAT], qm[g * hh + i])
        grads_now = jnp.concatenate(
            [gv_acc[...].astype(BF16), (gk * SCORE_SCALE).astype(BF16)], axis=1
        )
        xh, inv = norm_parts(x_ref[n].astype(F32))
        kept = stage.at[doc_rows(n), 0:din]
        if g == 0:
            kept[...] = dot_nt(grads_now, wkv[0]).astype(BF16)
        else:
            gx = kept[...].astype(F32) + dot_nt(grads_now, wkv[1])
            gain_acc[...] += jnp.sum(gx * xh, axis=0, keepdims=True)
            dxh = gx * gb_ref[...].reshape(1, -1)
            slot = lax.rem(n, 2)

            @pl.when(n >= 2)
            def _():
                pltpu.make_async_copy(frames.at[slot, 0:kc, 0:din], bg_hbm.at[n - 2], bg_s.at[slot]).wait()

            frames[slot, 0:kc, 0:din] = inv * (
                dxh
                - jnp.mean(dxh, axis=-1, keepdims=True)
                - xh * jnp.mean(dxh * xh, axis=-1, keepdims=True)
            )
            pltpu.make_async_copy(frames.at[slot, 0:kc, 0:din], bg_hbm.at[n], bg_s.at[slot]).start()
        normed_t = jnp.transpose((xh * gb_ref[...].reshape(1, -1)).astype(BF16))
        kv_acc[...] += dot_nn(normed_t, grads_now)

    def cut_values(g):
        step = din // nb
        for s in range(pos):
            for core in (1 - c, c):
                rows = pl.ds(pl.multiple_of((2 * s + core) * step, step), step)
                to = values[g].own if core is c else vstage.at[g]
                for i in range(2):
                    to[s, i * step : (i + 1) * step, :] = fpool[
                        rows, i * vhalf : (i + 1) * vhalf
                    ].astype(BF16)
            v_mate(g)(s).start()
        if g == 0:
            kv_acc[...] = jnp.zeros((din, vh + qh), F32)

    start0 = (pos + D + 2) // 2

    @pl.loop(0, parts + pos)
    def _(t):
        @pl.when(t < parts - ahead)
        def _():
            send_own(t + ahead)

        for hop in range(pos - 1):
            @pl.when((t >= hop) & (t - hop < parts))
            def _():
                forward_chunks(t - hop, hop)

        @pl.when(t % 2 == 0)
        def _():
            weights.step(t // 2, w_mate)
            values[0].step(t // 2 - start0, v_mate(0))

        @pl.when(t == pos)
        def _():
            for i in range(1, nb):
                src = lax.rem(blk + nb - i, nb)
                delta_copy(i, pl.ds(pl.multiple_of(src * rq, rq), rq)).wait_recv()
            turned = jnp.transpose(delta_all[...])
            for n in range(D):
                delta_t[n] = turned[n * HEADS : (n + 1) * HEADS, :]
            for item in later:
                item.wait()
            load_v.wait()
            store_out.wait()
            for s in range(pos, 3 * pos):
                w_mate(s).wait_send()

        @pl.when((t >= pos) & (t < pos + D))
        def _():
            bytes_back(0, t - pos)

        @pl.when(t == pos + D)
        def _():
            cut_values(0)

        @pl.when(t >= pos + D)
        def _():
            bytes_back(1, t - pos - D)

    cut_values(1)

    gq_rows = (jnp.transpose(gq_acc[...]) * SCORE_SCALE).astype(BF16)
    gains = jnp.concatenate([gmlp_acc[...], gain_acc[...]], axis=1)
    rows8 = [gains[:, 256 * i : 256 * (i + 1)] for i in range(8)]
    gains8 = jnp.concatenate(rows8 + [jnp.zeros((8, 256), F32)], axis=0).astype(BF16)
    for j in range(nb):
        misc_out[j, 0:rq] = gq_rows[j * rq : (j + 1) * rq, :]
        misc_out[j, rq : rq + 16] = gains8

    def misc1(i, slot):
        peer = lax.rem(blk + i, nb)
        return remote(
            misc_out.at[peer], misc_in.at[slot], m1_s.at[i - 1], m1_r.at[i - 1], doc, peer
        )

    def misc2(i, slot):
        return remote(
            misc2_out, misc2_in.at[slot], m2_s.at[i - 1], m2_r.at[i - 1],
            lax.rem(doc + i, nd), blk,
        )

    def misc3(i, rows):
        return remote(
            gq_ref.at[rows, :], gq_ref.at[rows, :], m3_s.at[i - 1], m3_r.at[i - 1],
            doc, lax.rem(blk + i, nb),
        )

    for i in range(1, nb):
        misc1(i, blk).start()
    misc_in[blk] = misc_out[blk]

    first = (parts + pos + 1) // 2
    last = max(weights.steps, start0 + values[0].steps, first + values[1].steps)

    @pl.loop(first, last)
    def _(t):
        values[1].step(t - first, v_mate(1))
        values[0].step(t - start0, v_mate(0))
        weights.step(t, w_mate)

        @pl.when(t == first + 1)
        def _():
            for i in range(1, nb):
                misc1(i, lax.rem(blk + nb - i, nb)).wait_recv()
            total = misc_in[0].astype(F32)
            for i in range(1, nb):
                total = total + misc_in[i].astype(F32)
            misc2_out[...] = total.astype(BF16)
            for i in range(1, nd):
                misc2(i, doc).start()
            misc2_in[doc] = misc2_out[...]

        @pl.when(t == first + 3)
        def _():
            for i in range(1, nd):
                misc2(i, lax.rem(doc + nd - i, nd)).wait_recv()
            total = misc2_in[0].astype(F32)
            for i in range(1, nd):
                total = total + misc2_in[i].astype(F32)
            gains_ref[...] = total[rq : rq + 8, :]
            gq_ref[own_rows, :] = total[0:rq].astype(BF16)
            for i in range(1, nb):
                misc3(i, own_rows).start()

    for i in range(1, nb):
        src = lax.rem(blk + nb - i, nb)
        misc3(i, pl.ds(pl.multiple_of(src * rq, rq), rq)).wait_recv()

    total = direct_out[...].astype(F32)
    for i in range(1, nd):
        direct_copy(i).wait_recv()
        total = total + dir_in[i - 1].astype(F32)
    dsum_ref[...] = total

    for n in range(D - 2, D):
        pltpu.make_async_copy(frames.at[n % 2, 0:kc, 0:din], bg_hbm.at[n], bg_s.at[n % 2]).wait()
    weights.drain()
    for g in range(2):
        values[g].drain()
        for s in range(pos):
            v_mate(g)(s).wait_send()
    for i in range(1, nb):
        delta_copy(i, own_rows).wait_send()
        misc1(i, blk).wait_send()
        misc3(i, own_rows).wait_send()
    for i in range(1, nd):
        direct_copy(i).wait_send()
        misc2(i, doc).wait_send()

    @pl.loop(0, parts)
    def _(e):
        mate_copy(e, p, c).wait_send()

        @pl.when(p < pos - 1)
        def _():
            right_copy(e, 0, p).wait_send()

        @pl.when(p > 0)
        def _():
            left_copy(e, 0, p).wait_send()

        for hop in range(pos - 1):
            j = p - 1 - hop

            @pl.when(j >= 0)
            def _():
                mate_copy(e, j, c).wait_send()
                if hop + 1 < pos - 1:
                    @pl.when(p < pos - 1)
                    def _():
                        right_copy(e, hop + 1, j).wait_send()

            i = p + 1 + hop

            @pl.when(i < pos)
            def _():
                mate_copy(e, i, c).wait_send()
                if hop + 1 < pos - 1:
                    @pl.when(p > 0)
                    def _():
                        left_copy(e, hop + 1, i).wait_send()


def backward(
    nb, nd, byte_embed, keys, values, w_out, w_up, w_down, w_key, w_value, cotangent,
    attended, latents, gain_mlp, bias, gain_bytes, queries, lse,
):
    D, kc, din = byte_embed.shape
    rq, dl = latents.shape
    pos = nb // 2
    rows = D * rq
    wunit, vunit = owner_rows(2 * dl // nb, nd), owner_rows(2 * din // nb, nd)
    whalf, vhalf = dl // 2, (DV + DQK) // 4
    vmem = pl.BlockSpec(memory_space=pltpu.VMEM)
    anywhere = pl.BlockSpec(memory_space=pl.ANY)
    dma = pltpu.SemaphoreType.DMA
    scratch = (
        shard_sum_scratch(nd, nb, 3 * pos, wunit, 2 * dl // nb, whalf)
        + shard_sum_scratch(nd, nb, pos, vunit, 2 * din // nb, vhalf)
        + shard_sum_scratch(nd, nb, pos, vunit, 2 * din // nb, vhalf)
        + [
            pltpu.VMEM((max(2 * dl, D * kc), dl), BF16),
            pltpu.VMEM((D, kc, din), BF16),
            pltpu.VMEM((D, kc, DQK), BF16),
            pltpu.VMEM((2 * D, LAT, DV // 2), BF16),
            pltpu.VMEM((LAT, 128), F32),
            pltpu.VMEM((D, HEADS, LAT), F32),
            pltpu.VMEM((HEADS, LAT, DQK // 2), BF16),
            pltpu.VMEM((2, din, (DV + DQK) // 2), BF16),
            pltpu.VMEM((kc, HEADS // 2 * LAT), BF16),
            pltpu.VMEM((kc, DV // 2), F32),
            pltpu.VMEM((DQK, LAT), F32),
            pltpu.VMEM((max(3 * rows, din), dl), F32),
            pltpu.VMEM((2, rows, dl), F32),
            pltpu.VMEM((dl, rows), BF16),
            pltpu.VMEM((rows, dl), BF16),
            pltpu.VMEM((rows, dl), BF16),
            pltpu.VMEM((rows, dl), BF16),
            pltpu.VMEM((rows, dl), BF16),
            pltpu.VMEM((rows, dl), BF16),
            pltpu.VMEM((max(2 * dl, D * kc), (DV + DQK) // 2), BF16),
            pltpu.VMEM((2, pos, 2 * din // nb, vhalf), BF16),
            pltpu.VMEM((1, din), F32),
            pltpu.VMEM((1, dl), F32),
            pltpu.VMEM((rq, dl), BF16),
            pltpu.VMEM((nd - 1, rq, dl), BF16),
            pltpu.VMEM((nb, rq + 16, 256), BF16),
            pltpu.VMEM((nb, rq + 16, 256), BF16),
            pltpu.VMEM((rq + 16, 256), BF16),
            pltpu.VMEM((nd, rq + 16, 256), BF16),
            dma((12,)), dma, dma((2,)),
            dma((2 * D, pos - 1)), dma((2 * D, pos - 1)),
            dma((2 * D, pos - 1)), dma((2 * D, pos - 1)),
            dma((2 * D, pos)), dma((2 * D, pos)),
            dma((nb - 1,)), dma((nb - 1,)), dma((nd - 1,)), dma((nd - 1,)),
            dma((nb - 1,)), dma((nb - 1,)), dma((nd - 1,)), dma((nd - 1,)),
            dma((nb - 1,)), dma((nb - 1,)),
        ]
    )
    return pl.pallas_call(
        functools.partial(backward_kernel, nb, nd, wunit, vunit),
        out_shape=(
            jax.ShapeDtypeStruct((rows, dl), F32),
            jax.ShapeDtypeStruct((D, kc, din), F32),
            jax.ShapeDtypeStruct((3, wunit * nd, whalf), BF16),
            jax.ShapeDtypeStruct((1, vunit * nd, vhalf), BF16),
            jax.ShapeDtypeStruct((1, vunit * nd, vhalf), BF16),
            jax.ShapeDtypeStruct((rq, dl), F32),
            jax.ShapeDtypeStruct((LAT, DQK), BF16),
            jax.ShapeDtypeStruct((8, 256), F32),
        ),
        in_specs=[anywhere] * 9 + [vmem] * 7,
        out_specs=(anywhere,) * 2 + (vmem,) * 6,
        scratch_shapes=scratch,
        compiler_params=pltpu.CompilerParams(
            collective_id=1, has_side_effects=True, vmem_limit_bytes=63 * 2**20
        ),
        name="backward",
    )(
        byte_embed, keys, values.reshape(D * kc, DV), w_out, w_up, w_down, w_key, w_value,
        cotangent.reshape(rows, dl), attended, latents, gain_mlp, bias,
        gain_bytes, queries, lse,
    )


def finish_kernel(
    nb, rows_hbm, bytes_hbm, wsum_hbm, vsum0_ref, vsum1_ref, dsum_ref, gq_ref, gains_ref, cols_ref,
    lat_ref, gain_ref, wq_ref, rows_out, bytes_out, lgrad_ref, gq_gain_ref, gb_gain_ref,
    gm_gain_ref, wq_out, wk_out, wv_out, wo_out, wu_out, wd_out, turned,
    wsum_ref, bytes_buf, rows_buf, take_s, move_s,
):
    D = bytes_hbm.shape[0]
    pairs = [(bytes_hbm.at[n], bytes_buf.at[n], bytes_out.at[n]) for n in range(D)]
    pairs.append((rows_hbm, rows_buf, rows_out))
    takes = [
        pltpu.make_async_copy(src, buf, take_s.at[i]) for i, (src, buf, _) in enumerate(pairs)
    ]
    takes.append(pltpu.make_async_copy(wsum_hbm, wsum_ref, take_s.at[D + 1]))
    moves = [
        pltpu.make_async_copy(buf, out, move_s.at[i]) for i, (_, buf, out) in enumerate(pairs)
    ]
    for take in takes:
        take.start()
    for take, move in zip(takes, moves):
        take.wait()
        move.start()
    takes[-1].wait()
    rq, dl = lat_ref.shape
    din, step, vstep = wk_out.shape[0] * nb, dl // nb, wk_out.shape[0]
    blk = lax.axis_index("blk")
    half = dl // 2
    for m, out in enumerate((wd_out, wu_out, wo_out)):
        for i in range(2):
            out[:, i * half : (i + 1) * half] = wsum_ref[
                m, i * step : (i + 1) * step, :
            ].astype(F32)
    width = (DV + DQK) // 4
    for g, ref in enumerate((vsum0_ref, vsum1_ref)):
        both = jnp.concatenate(
            [ref[0, i * vstep : (i + 1) * vstep, :].astype(F32) for i in range(2)], axis=1
        )
        at = DV // 2
        wv_out[:, g * at : (g + 1) * at] = both[:, :at]
        wk_out[:, g * DQK // 2 : (g + 1) * DQK // 2] = both[:, at : 2 * width]

    gq = gq_ref[...]
    cols = cols_ref[...]
    first = pl.multiple_of(jnp.minimum(blk * step // 128 * 128, dl - 256), 128)
    skip = blk * step - first
    turned[...] = dot_nn(jnp.transpose(cols), gq)
    wq_out[...] = turned[pl.ds(pl.multiple_of(skip, 16), step), :]
    dy = dot_nt(gq, wq_ref[pl.ds(first, 256), :])
    gain = jnp.sum(dy * cols.astype(F32), axis=0, keepdims=True) / gain_ref[pl.ds(first, 256)].reshape(1, -1)

    def cut(row, at, count):
        size = row.shape[1]
        return pltpu.roll(row, lax.rem(size - at, size), 1)[:, :count]

    gq_gain_ref[...] = cut(gain, skip, step)
    row = jnp.concatenate([gains_ref[i : i + 1, :] for i in range(8)], axis=1)
    gm_gain_ref[...] = cut(row[:, :dl], blk * step, step)
    gb_gain_ref[...] = cut(row[:, dl:], blk * vstep, vstep)

    own = gq_ref[pl.ds(pl.multiple_of(blk * rq, rq), rq), :]
    dxh = dot_nt(own, wq_ref[...]) * gain_ref[...].reshape(1, -1)
    xh, inv = norm_parts(lat_ref[...])
    lgrad_ref[...] = dsum_ref[...] + inv * (
        dxh
        - jnp.mean(dxh, axis=-1, keepdims=True)
        - xh * jnp.mean(dxh * xh, axis=-1, keepdims=True)
    )
    for move in moves:
        move.wait()


def finish(
    nb, latents_out, byte_grad, wsum, vsum0, vsum1, direct_sum, gq, gains, norm_cols, latents,
    gain_query, w_query,
):
    rq, dl = latents.shape
    din = gains.size - dl
    vmem = pl.BlockSpec(memory_space=pltpu.VMEM)
    anywhere = pl.BlockSpec(memory_space=pl.ANY)
    shapes = (
        latents_out.shape, byte_grad.shape, (rq, dl), (1, dl // nb), (1, din // nb), (1, dl // nb), (dl // nb, DQK),
        (din // nb, DQK), (din // nb, DV), (dl // nb, dl), (dl // nb, dl), (dl // nb, dl),
    )
    return pl.pallas_call(
        functools.partial(finish_kernel, nb),
        out_shape=tuple(jax.ShapeDtypeStruct(s, F32) for s in shapes),
        in_specs=[anywhere] * 3 + [vmem] * 9,
        out_specs=(anywhere,) * 2 + (vmem,) * 10,
        scratch_shapes=[
            pltpu.VMEM((256, DQK), F32),
            pltpu.VMEM(wsum.shape, BF16),
            pltpu.VMEM(byte_grad.shape, F32),
            pltpu.VMEM(latents_out.shape, F32),
            pltpu.SemaphoreType.DMA((byte_grad.shape[0] + 2,)),
            pltpu.SemaphoreType.DMA((byte_grad.shape[0] + 1,)),
        ],
        compiler_params=pltpu.CompilerParams(vmem_limit_bytes=60 * 2**20),
        name="finish",
    )(
        latents_out, byte_grad, wsum, vsum0, vsum1, direct_sum, gq, gains, norm_cols, latents,
        gain_query, w_query,
    )


def body(
    byte_embed,
    doc_lengths,
    key_mask,
    latents,
    gain_query,
    gain_bytes,
    gain_mlp,
    w_query,
    w_key,
    w_value,
    w_out,
    w_up,
    w_down,
    cotangent,
):
    nb, nd = lax.axis_size("blk"), lax.axis_size("doc")
    attended, lse, keys, values, norm_cols, queries, bias = forward(
        nb, byte_embed, doc_lengths, key_mask, latents, gain_query, gain_bytes, w_query, w_key,
        w_value,
    )
    latents_out, byte_grad, wsum, vsum0, vsum1, direct_sum, gq, gains = backward(
        nb, nd, byte_embed, keys, values, w_out, w_up, w_down, w_key, w_value, cotangent,
        attended, latents, gain_mlp, bias, gain_bytes, queries, lse,
    )
    (
        latents_out, byte_grad, latents_grad, gain_query_grad, gain_bytes_grad, gain_mlp_grad,
        grad_w_query, grad_w_key, grad_w_value, grad_w_out, grad_w_up, grad_w_down,
    ) = finish(
        nb, latents_out, byte_grad, wsum, vsum0, vsum1, direct_sum, gq, gains, norm_cols,
        latents, gain_query, w_query,
    )
    latents_out = latents_out.reshape(cotangent.shape)
    return (
        latents_out,
        byte_grad,
        latents_grad,
        gain_query_grad.reshape(-1),
        gain_bytes_grad.reshape(-1),
        gain_mlp_grad.reshape(-1),
        grad_w_query,
        grad_w_key,
        grad_w_value,
        grad_w_out,
        grad_w_up,
        grad_w_down,
    )


def solution(mesh):
    in_specs = (
        P("doc", "blk", None),
        P("doc"),
        P("doc", "blk"),
        P("blk", None),
        P(),
        P(),
        P(),
        P(),
        P(),
        P(),
        P(),
        P(),
        P(),
        P("doc", "blk", None),
    )
    out_specs = (
        P("doc", "blk", None),
        P("doc", "blk", None),
        P("blk", None),
        P("blk"),
        P("blk"),
        P("blk"),
        P("blk", None),
        P("blk", None),
        P("blk", None),
        P("blk", None),
        P("blk", None),
        P("blk", None),
    )
    return jax.shard_map(body, mesh=mesh, in_specs=in_specs, out_specs=out_specs, check_vma=False)
```

```python
import functools
import math

import jax
import jax.numpy as jnp
from jax import lax
from jax.experimental import pallas as pl
from jax.experimental.pallas import tpu as pltpu
from jax.sharding import PartitionSpec as P

LAT = 256
HEADS = 8
QK_HEAD = 32
V_HEAD = 160
DQK = HEADS * QK_HEAD
DV = HEADS * V_HEAD
MESH = pl.DeviceIdType.MESH
F32 = jnp.float32
BF16 = jnp.bfloat16

epsilon = 1e-05
masked_score = -1e30
LOG2E = math.log2(math.e)
SCORE2 = QK_HEAD ** (-0.5) * LOG2E
SCORE_SCALE = QK_HEAD ** (-0.5)


def dot_nn(a, b):
    return jnp.dot(a, b, preferred_element_type=F32)


def dot_nt(a, b):
    return lax.dot_general(a, b, (((1,), (1,)), ((), ())), preferred_element_type=F32)


def norm_parts(v):
    centered = v - jnp.mean(v, axis=-1, keepdims=True)
    spread = jnp.mean(centered * centered, axis=-1, keepdims=True)
    inv = lax.rsqrt(spread + epsilon)
    return centered * inv, inv


def window(h):
    return V_HEAD * h // 128 * 128


def value_mask(h, rows):
    lane = lax.broadcasted_iota(jnp.int32, (rows, 256), 1) + window(h)
    keep = (lane >= V_HEAD * h) & (lane < V_HEAD * (h + 1))
    return jnp.where(keep, 1.0, 0.0).astype(BF16)


def query_mask(h, rows):
    lane = lax.broadcasted_iota(jnp.int32, (rows, DQK), 1)
    keep = (lane >= QK_HEAD * h) & (lane < QK_HEAD * (h + 1))
    return jnp.where(keep, 1.0, 0.0).astype(BF16)


def row_to_lanes(row):
    return jnp.transpose(jnp.broadcast_to(row, (128, row.shape[1])))


def wide(col, n):
    return jnp.concatenate([col] * (n // 128), axis=1) if n > 128 else col


def remote(src, dst, send, recv, doc, blk):
    return pltpu.make_async_remote_copy(
        src_ref=src, dst_ref=dst, send_sem=send, recv_sem=recv,
        device_id=(doc, blk), device_id_type=MESH,
    )


def forward_kernel(
    nb,
    x_hbm, wq_hbm, wk_hbm, wv_hbm, len_ref, mask_ref, lat_ref, gq_ref, gb_ref,
    att_ref, lse_ref, k_hbm, v_hbm, nlw_ref, qall_ref, bias_ref,
    x_ref, wq_ref, wk_ref, wv_ref, k_ref, v_ref, nl_cols, normed, qm, lloc, lmate, lz, acc, part, mate_in, rin, lin,
    load_s, x_s, out_s, q_s, q_r, n_s, n_r, l_s, l_r, mate_s, mate_r, rs_s, rs_r, ls_s, ls_r,
):
    D, kc, din = x_hbm.shape
    rq = lat_ref.shape[0]
    pos = nb // 2
    doc, blk = lax.axis_index("doc"), lax.axis_index("blk")
    p, c = blk // 2, blk % 2
    mate = 2 * p + 1 - c
    loads = [
        pltpu.make_async_copy(src, dst, load_s.at[i])
        for i, (src, dst) in enumerate(((wq_hbm, wq_ref), (wk_hbm, wk_ref), (wv_hbm, wv_ref)))
    ]

    def x_load(n):
        return pltpu.make_async_copy(x_hbm.at[n], x_ref.at[n], x_s.at[n])

    stores = [
        pltpu.make_async_copy(src, dst, out_s.at[i])
        for i, (src, dst) in enumerate(((k_ref, k_hbm), (v_ref, v_hbm)))
    ]
    loads[0].start()
    x_load(0).start()
    loads[1].start()
    for n in range(1, D):
        x_load(n).start()
    loads[2].start()
    barrier = pltpu.get_barrier_semaphore()
    for i in range(1, nb):
        pl.semaphore_signal(
            barrier, inc=1, device_id=(doc, lax.rem(blk + i, nb)), device_id_type=MESH
        )

    slots = blk * kc + lax.broadcasted_iota(jnp.int32, (1, kc), 1)
    for n in range(D):
        usable = (slots < len_ref[n]) & (mask_ref[n : n + 1, :] == 1)
        bias_ref[n : n + 1, :] = jnp.where(usable, 0.0, masked_score)

    xhat, _ = norm_parts(lat_ref[...])
    nl = (xhat * gq_ref[...].reshape(1, -1)).astype(BF16)
    step = nl.shape[1] // nb
    for j in range(nb):
        at = min(j * step // 128 * 128, nl.shape[1] - 256)
        nl_cols[j] = nl[:, at : at + 256]
    own = pl.ds(pl.multiple_of(blk * rq, rq), rq)
    loads[0].wait()
    qall_ref[own, :] = dot_nn(nl, wq_ref[...]).astype(BF16)
    pl.semaphore_wait(barrier, nb - 1)

    def q_copy(i, slot):
        return remote(
            qall_ref.at[own, :], qall_ref.at[slot, :], q_s.at[i - 1], q_r.at[i - 1],
            doc, lax.rem(blk + i, nb),
        )

    def n_copy(i, slot):
        peer = lax.rem(blk + i, nb)
        return remote(
            nl_cols.at[peer], nlw_ref.at[slot, :], n_s.at[i - 1], n_r.at[i - 1], doc, peer
        )

    for i in range(1, nb):
        q_copy(i, own).start()
    for i in range(1, nb):
        n_copy(i, own).start()
    nlw_ref[own, :] = nl_cols[blk]

    loads[1].wait()

    @pl.loop(0, D)
    def _(n):
        x_load(n).wait()
        xh, _ = norm_parts(x_ref[n].astype(F32))
        normed[n] = (xh * gb_ref[...].reshape(1, -1)).astype(BF16)
        k_ref[n] = dot_nn(normed[n], wk_ref[...]).astype(BF16)

    for i in range(1, nb):
        src = lax.rem(blk + nb - i, nb)
        q_copy(i, pl.ds(pl.multiple_of(src * rq, rq), rq)).wait_recv()
    for h in range(HEADS):
        qm[h] = qall_ref[...] * query_mask(h, LAT)

    stores[0].start()

    def own_logs(lo, hi):
        @pl.loop(lo, hi)
        def _(n):
            bias = wide(row_to_lanes(bias_ref[pl.ds(n, 1), :]), LAT)
            kn = k_ref[n]
            rows = []
            for h in range(HEADS):
                s = dot_nt(kn, qm[h]) * SCORE2 + bias
                top = jnp.max(s, axis=0, keepdims=True)
                tot = jnp.sum(jnp.exp2(s - top), axis=0, keepdims=True)
                rows.append(top + jnp.log(tot) * LOG2E)
            lloc[n] = jnp.concatenate(rows, axis=0)

    half, quarter = D // 2, D // 4

    def mine(b):
        return pl.ds(b * half + c * quarter, quarter)

    def other(b):
        return pl.ds(b * half + (1 - c) * quarter, quarter)

    def merge(a, b):
        top = jnp.maximum(a, b)
        return top + jnp.log(jnp.exp2(a - top) + jnp.exp2(b - top)) * LOG2E

    def first(b):
        return remote(lloc.at[other(b)], lmate.at[b], l_s.at[b, 0], l_r.at[b, 0], doc, mate)

    def z_copy(b, i, slot):
        return remote(
            lz.at[b, p], lz.at[b, slot], l_s.at[b, i], l_r.at[b, i],
            doc, 2 * lax.rem(p + i, pos) + c,
        )

    def last(b, part):
        return remote(
            lse_ref.at[part], lse_ref.at[part], l_s.at[b, pos], l_r.at[b, pos], doc, mate
        )

    def along(b):
        first(b).wait_recv()
        lz[b, p] = merge(lloc[mine(b)], lmate[b])
        for i in range(1, pos):
            z_copy(b, i, p).start()

    def close(b):
        for i in range(1, pos):
            z_copy(b, i, lax.rem(p + pos - i, pos)).wait_recv()
        total = lz[b, 0]
        for i in range(1, pos):
            total = merge(total, lz[b, i])
        lse_ref[mine(b)] = total
        last(b, mine(b)).start()

    def values(lo, hi):
        @pl.loop(lo, hi)
        def _(n):
            v_ref[n] = dot_nn(normed[n], wv_ref[...]).astype(BF16)

    own_logs(0, half)
    first(0).start()
    own_logs(half, D)
    first(1).start()
    along(0)
    loads[2].wait()
    values(0, quarter)
    along(1)
    values(quarter, D)
    stores[1].start()
    close(0)
    close(1)
    last(0, other(0)).wait_recv()

    def mate_copy(n):
        return remote(
            part.at[n, 1 - c], mate_in.at[n], mate_s.at[n], mate_r.at[n], doc, mate
        )

    def right_copy(n, j, src):
        return remote(
            src, rin.at[n, j], rs_s.at[n, j], rs_r.at[n, j],
            doc, 2 * jnp.minimum(p + 1, pos - 1) + c,
        )

    def left_copy(n, j, src):
        return remote(
            src, lin.at[n, j], ls_s.at[n, j], ls_r.at[n, j],
            doc, 2 * jnp.maximum(p - 1, 0) + c,
        )

    def chip_sum(n):
        mate_copy(n).wait_recv()
        both = part[n, c].astype(F32) + mate_in[n].astype(F32)
        part[n, c] = both.astype(BF16)

        @pl.when(p == 0)
        def _():
            for j in range(pos - 1, 0, -1):
                right_copy(n, j, part.at[n, c, j]).start()

        @pl.when(p == pos - 1)
        def _():
            for j in range(pos - 1):
                left_copy(n, j, part.at[n, c, j]).start()

    @pl.loop(0, D)
    def _(n):
        @pl.when(n == half)
        def _():
            last(1, other(1)).wait_recv()

        logs = lse_ref[n]
        logs_t = jnp.transpose(jnp.concatenate([logs] * (128 // HEADS), axis=0))
        bias = bias_ref[pl.ds(n, 1), :]
        kn = k_ref[n]
        acc[...] = jnp.zeros_like(acc)
        for h in range(HEADS):
            s = dot_nt(qm[h], kn) * SCORE2 + bias
            prob = jnp.exp2(s - logs_t[:, h : h + 1]).astype(BF16)
            cols = slice(window(h), window(h) + 256)
            acc[:, cols] += dot_nn(prob, v_ref[n, :, cols] * value_mask(h, kc))
        for j in range(nb):
            part[n, j % 2, j // 2] = acc[rq * j : rq * (j + 1), :].astype(BF16)
        mate_copy(n).start()

        @pl.when(n > 0)
        def _():
            chip_sum(n - 1)

    chip_sum(D - 1)

    def from_left(n):
        for j in range(pos - 1, 0, -1):
            @pl.when(j >= p)
            def _():
                right_copy(n, j, part.at[n, c, j]).wait_recv()

            @pl.when(j > p)
            def _():
                both = rin[n, j].astype(F32) + part[n, c, j].astype(F32)
                part[n, c, j] = both.astype(BF16)
                right_copy(n, j, part.at[n, c, j]).start()

    def from_right(n):
        for j in range(pos - 1):
            @pl.when(j <= p)
            def _():
                left_copy(n, j, part.at[n, c, j]).wait_recv()

            @pl.when(j < p)
            def _():
                both = lin[n, j].astype(F32) + part[n, c, j].astype(F32)
                part[n, c, j] = both.astype(BF16)
                left_copy(n, j, part.at[n, c, j]).start()

    def finish(n):
        acc[0:rq, :] = part[n, c, p].astype(F32)

        @pl.when(p > 0)
        def _():
            acc[0:rq, :] += rin[n, p].astype(F32)

        @pl.when(p < pos - 1)
        def _():
            acc[0:rq, :] += lin[n, p].astype(F32)

        att_ref[n] = acc[0:rq, :].astype(BF16)

    @pl.loop(0, D + pos - 1)
    def _(t):
        right_n, left_n, done_n = t - p, t - (pos - 1 - p), t - (pos - 1)

        @pl.when((p > 0) & (right_n >= 0) & (right_n < D))
        def _():
            from_left(right_n)

        @pl.when((p < pos - 1) & (left_n >= 0) & (left_n < D))
        def _():
            from_right(left_n)

        @pl.when(done_n >= 0)
        def _():
            finish(done_n)

    for i in range(1, nb):
        src = lax.rem(blk + nb - i, nb)
        n_copy(i, pl.ds(pl.multiple_of(src * rq, rq), rq)).wait_recv()

    for i in range(1, nb):
        q_copy(i, own).wait_send()
        n_copy(i, own).wait_send()
    for b in range(2):
        first(b).wait_send()
        for i in range(1, pos):
            z_copy(b, i, p).wait_send()
        last(b, mine(b)).wait_send()
    for store in stores:
        store.wait()

    @pl.loop(0, D)
    def _(n):
        mate_copy(n).wait_send()
        for j in range(pos):
            @pl.when((j > p) & (p < pos - 1))
            def _():
                right_copy(n, j, part.at[n, c, j]).wait_send()

            @pl.when((j < p) & (p > 0))
            def _():
                left_copy(n, j, part.at[n, c, j]).wait_send()


def forward(
    nb, byte_embed, doc_lengths, key_mask, latents, gain_query, gain_bytes, w_query, w_key, w_value
):
    D, kc, din = byte_embed.shape
    rq, dl = latents.shape
    pos = nb // 2
    vmem = pl.BlockSpec(memory_space=pltpu.VMEM)
    anywhere = pl.BlockSpec(memory_space=pl.ANY)
    dma = pltpu.SemaphoreType.DMA
    return pl.pallas_call(
        functools.partial(forward_kernel, nb),
        out_shape=(
            jax.ShapeDtypeStruct((D, rq, DV), BF16),
            jax.ShapeDtypeStruct((D, HEADS, LAT), F32),
            jax.ShapeDtypeStruct((D, kc, DQK), BF16),
            jax.ShapeDtypeStruct((D, kc, DV), BF16),
            jax.ShapeDtypeStruct((LAT, 256), BF16),
            jax.ShapeDtypeStruct((LAT, DQK), BF16),
            jax.ShapeDtypeStruct((D, kc), F32),
        ),
        in_specs=[anywhere] * 4 + [pl.BlockSpec(memory_space=pltpu.SMEM)] + [vmem] * 4,
        out_specs=(vmem, vmem, anywhere, anywhere, vmem, vmem, vmem),
        scratch_shapes=[
            pltpu.VMEM((D, kc, din), BF16),
            pltpu.VMEM(w_query.shape, BF16),
            pltpu.VMEM(w_key.shape, BF16),
            pltpu.VMEM(w_value.shape, BF16),
            pltpu.VMEM((D, kc, DQK), BF16),
            pltpu.VMEM((D, kc, DV), BF16),
            pltpu.VMEM((nb, rq, 256), BF16),
            pltpu.VMEM((D, kc, din), BF16),
            pltpu.VMEM((HEADS, LAT, DQK), BF16),
            pltpu.VMEM((D, HEADS, LAT), F32),
            pltpu.VMEM((2, D // 4, HEADS, LAT), F32),
            pltpu.VMEM((2, pos, D // 4, HEADS, LAT), F32),
            pltpu.VMEM((LAT, DV), F32),
            pltpu.VMEM((D, 2, pos, rq, DV), BF16),
            pltpu.VMEM((D, pos, rq, DV), BF16),
            pltpu.VMEM((D, pos, rq, DV), BF16),
            pltpu.VMEM((D, pos, rq, DV), BF16),
            dma((3,)), dma((D,)), dma((2,)),
            dma((nb - 1,)), dma((nb - 1,)), dma((nb - 1,)), dma((nb - 1,)),
            dma((2, pos + 1)), dma((2, pos + 1)),
            dma((D,)), dma((D,)),
            dma((D, pos)), dma((D, pos)), dma((D, pos)), dma((D, pos)),
        ],
        compiler_params=pltpu.CompilerParams(
            collective_id=0, has_side_effects=True, vmem_limit_bytes=56 * 2**20
        ),
        name="forward",
    )(
        byte_embed, w_query, w_key, w_value, doc_lengths, key_mask, latents, gain_query,
        gain_bytes,
    )


def gelu_parts(u):
    k = math.sqrt(2.0 / math.pi)
    sq = u * u
    t = jnp.tanh(k * u * (1.0 + 0.044715 * sq))
    value = 0.5 * u * (1.0 + t)
    slope = 0.5 * (1.0 + t) + 0.5 * k * u * (1.0 - t * t) * (1.0 + 3 * 0.044715 * sq)
    return value, slope


def owner_rows(total, docs):
    return -(-total // (16 * docs)) * 16


class ShardSums:
    def __init__(
        self, doc, blk, nd, nb, count, unit, group, lags, direct,
        own, mate_in, inbox, rin, lin, out, sems,
    ):
        self.doc, self.p, self.c = doc, blk // 2, blk % 2
        self.nd, self.pos, self.count, self.unit = nd, nb // 2, count, unit
        self.bits = nd.bit_length() - 1
        self.own, self.mate_in, self.inbox = own, mate_in, inbox
        self.rin, self.lin, self.out = rin, lin, out
        (
            self.mate_s, self.mate_r, self.in_s, self.in_r,
            self.right_s, self.right_r, self.left_s, self.left_r, self.out_s, self.out_r,
        ) = sems
        self.group, self.lags, self.direct = group, lags, direct
        self.steps = count // group + lags[-1] + (1 if direct else self.pos - 1)

    def weight(self, s, k):
        b = (s + k) % self.bits
        return 1 + b * (b + 1) // 2

    def my_bit(self, w):
        return (self.doc // w) % 2

    def quarter(self, s, k, i, sent):
        q = 0
        for r in range(k):
            w = self.weight(s, r)
            q = q + self.my_bit(w) * w
        w = self.weight(s, k)
        mine = self.my_bit(w)
        q = q + ((1 - mine) if sent else mine) * w
        for r in range(k + 1, self.bits):
            q = q + ((i >> (r - k - 1)) & 1) * self.weight(s, r)
        return q

    def width(self, k):
        return 2 ** (self.bits - 1 - k)

    def slot(self, k, i):
        return sum(self.width(r) for r in range(k)) + i

    def rows(self, q):
        return pl.ds(pl.multiple_of(q * self.unit, self.unit), self.unit)

    def halving(self, s, k, i):
        w = self.weight(s, k)
        peer = self.doc + w * (1 - 2 * self.my_bit(w))
        slot = self.slot(k, i)
        return remote(
            self.own.at[s, self.rows(self.quarter(s, k, i, True)), :], self.inbox.at[s, slot],
            self.in_s.at[s, slot], self.in_r.at[s, slot], peer, 2 * self.p + self.c,
        )

    def right(self, s):
        return remote(
            self.own.at[s, self.rows(self.doc), :], self.rin.at[s],
            self.right_s.at[s], self.right_r.at[s],
            self.doc, 2 * jnp.minimum(self.p + 1, self.pos - 1) + self.c,
        )

    def left(self, s):
        return remote(
            self.own.at[s, self.rows(self.doc), :], self.lin.at[s],
            self.left_s.at[s], self.left_r.at[s],
            self.doc, 2 * jnp.maximum(self.p - 1, 0) + self.c,
        )

    def share(self, m, i):
        return remote(
            self.out.at[m, self.rows(self.doc), :], self.out.at[m, self.rows(self.doc), :],
            self.out_s.at[m, i - 1], self.out_r.at[m, i - 1],
            lax.rem(self.doc + i, self.nd), 2 * self.p + self.c,
        )

    def shared(self, m, i):
        src = lax.rem(self.doc + self.nd - i, self.nd)
        return remote(
            self.out.at[m, self.rows(src), :], self.out.at[m, self.rows(src), :],
            self.out_s.at[m, i - 1], self.out_r.at[m, i - 1], src, 2 * self.p + self.c,
        )

    def add(self, s, q, other):
        rows = self.rows(q)
        self.own[s, rows, :] = (
            self.own[s, rows, :].astype(F32) + other.astype(F32)
        ).astype(BF16)

    def begin(self, s, mate_copy):
        mate_copy(s).wait_recv()
        rows = self.mate_in.shape[1]
        self.own[s, 0:rows, :] = (
            self.own[s, 0:rows, :].astype(F32) + self.mate_in[s].astype(F32)
        ).astype(BF16)
        for i in range(self.width(0)):
            self.halving(s, 0, i).start()

    def halve(self, s, k):
        for i in range(self.width(k - 1)):
            self.halving(s, k - 1, i).wait_recv()
            self.add(s, self.quarter(s, k - 1, i, False), self.inbox[s, self.slot(k - 1, i)])
        if k < self.bits:
            for i in range(self.width(k)):
                self.halving(s, k, i).start()
            return
        if self.direct:
            return
        j = s % self.pos

        @pl.when((self.p == 0) & (j > 0))
        def _():
            self.right(s).start()

        @pl.when((self.p == self.pos - 1) & (j < self.pos - 1))
        def _():
            self.left(s).start()

    def from_left(self, s):
        j = s % self.pos

        @pl.when(j >= self.p)
        def _():
            self.right(s).wait_recv()

        @pl.when(j > self.p)
        def _():
            self.add(s, self.doc, self.rin[s])
            self.right(s).start()

    def from_right(self, s):
        j = s % self.pos

        @pl.when(j <= self.p)
        def _():
            self.left(s).wait_recv()

        @pl.when(j < self.p)
        def _():
            self.add(s, self.doc, self.lin[s])
            self.left(s).start()

    def finish(self, s):
        @pl.when(s % self.pos == self.p)
        def _():
            m = s // self.pos

            @pl.when(self.p > 0)
            def _():
                self.add(s, self.doc, self.rin[s])

            @pl.when(self.p < self.pos - 1)
            def _():
                self.add(s, self.doc, self.lin[s])

            self.out[m, self.rows(self.doc), :] = self.own[s, self.rows(self.doc), :]
            for i in range(1, self.nd):
                self.share(m, i).start()

    def spread(self, i, back):
        to = lax.rem(self.p + (self.pos - i if back else i), self.pos)
        return remote(
            self.own.at[to, self.rows(self.doc), :], self.rin.at[i - 1],
            self.right_s.at[i - 1], self.right_r.at[i - 1], self.doc, 2 * to + self.c,
        )

    def scatter(self):
        for i in range(1, self.pos):
            self.spread(i, False).start()

    def collect(self):
        rows = self.rows(self.doc)
        total = self.own[self.p, rows, :].astype(F32)
        for i in range(1, self.pos):
            self.spread(i, True).wait_recv()
            total = total + self.rin[i - 1].astype(F32)
        self.out[0, rows, :] = total.astype(BF16)
        for i in range(1, self.nd):
            self.share(0, i).start()

    def step(self, t, mate_copy, entered=0):
        def at(t, when, run, turned=False):
            @pl.when((t >= 0) & (t < self.count // self.group) & when)
            def _():
                for i in range(self.group):
                    run(t * self.group + (self.group - 1 - i if turned else i))

        at(t, t >= entered, lambda s: self.begin(s, mate_copy))
        for k in range(1, self.bits + 1):
            at(t - self.lags[k - 1], True, functools.partial(self.halve, k=k))
        base = t - self.lags[-1]
        if self.direct:
            pl.when(base == 0)(self.scatter)
            pl.when(base == 1)(self.collect)
            return
        at(base - self.p, self.p > 0, self.from_left, True)
        at(base - (self.pos - 1 - self.p), self.p < self.pos - 1, self.from_right)
        at(base - (self.pos - 1), True, self.finish)

    def drain(self):
        if self.direct:
            for i in range(1, self.pos):
                self.spread(i, False).wait_send()
        for m in range(self.count // self.pos):
            for i in range(1, self.nd):
                self.shared(m, i).wait_recv()
                self.share(m, i).wait_send()

        @pl.loop(0, self.count)
        def _(s):
            for k in range(self.bits):
                for i in range(self.width(k)):
                    self.halving(s, k, i).wait_send()
            if self.direct:
                return
            j = s % self.pos

            @pl.when((j > self.p) & (self.p < self.pos - 1))
            def _():
                self.right(s).wait_send()

            @pl.when((j < self.p) & (self.p > 0))
            def _():
                self.left(s).wait_send()


def shard_sum_scratch(nd, nb, count, unit, rows, width):
    dma = pltpu.SemaphoreType.DMA
    arrays = count // (nb // 2)
    return [
        pltpu.VMEM((count, unit * nd, width), BF16),
        pltpu.VMEM((count, rows, width), BF16),
        pltpu.VMEM((count, nd - 1, unit, width), BF16),
        pltpu.VMEM((count, unit, width), BF16),
        pltpu.VMEM((count, unit, width), BF16),
        dma((count,)), dma((count,)),
        dma((count, nd - 1)), dma((count, nd - 1)),
        dma((count,)), dma((count,)), dma((count,)), dma((count,)),
        dma((arrays, nd - 1)), dma((arrays, nd - 1)),
    ]


def backward_kernel(nb, nd, wunit, vunit, *refs):
    (
        x_hbm, k_hbm, v_hbm, wo_hbm, wu_hbm, wd_hbm, wk_hbm, wv_hbm, cot_hbm,
        att_ref, lat_ref, gm_ref, bias_ref, gb_ref, qall_ref, lse_ref,
    ) = refs[:16]
    out_hbm, bg_hbm, wsum_ref, vsum0_ref, vsum1_ref, dsum_ref, gq_ref, gains_ref = refs[16:24]
    wscr, vscr = refs[24:39], (refs[39:54], refs[54:69])
    (
        wpool, x_ref, k_ref, ga_all, delta_all, delta_t, qm, wkv, ds_all, gv_acc, gq_acc,
        fpool, frames, low_t, acts, gm, g_up, gb, stage, vstage, gain_acc, gmlp_acc, direct_out, dir_in,
        misc_out, misc_in, misc2_out, misc2_in,
        load_s, out_s, bg_s, ar_s, ar_r, al_s, al_r, am_s, am_r, d_s, d_r, dir_s, dir_r,
        m1_s, m1_r, m2_s, m2_r, m3_s, m3_r,
    ) = refs[69:]
    D, kc, din = x_ref.shape
    rq, dl = lat_ref.shape
    rows_all = D * rq
    pos = nb // 2
    hh, vh, qh = HEADS // 2, DV // 2, DQK // 2
    bits = nd.bit_length() - 1
    doc, blk = lax.axis_index("doc"), lax.axis_index("blk")
    p, c = blk // 2, blk % 2
    mate = 2 * p + 1 - c

    barrier = pltpu.get_barrier_semaphore()
    for i in range(1, nb):
        pl.semaphore_signal(
            barrier, inc=1, device_id=(doc, lax.rem(blk + i, nb)), device_id_type=MESH
        )
    for i in range(1, nd):
        pl.semaphore_signal(
            barrier, inc=1, device_id=(lax.rem(doc + i, nd), blk), device_id_type=MESH
        )

    def load(src, dst, i):
        return pltpu.make_async_copy(src, dst, load_s.at[i])

    slot0, slot1 = wpool.at[0:dl, :], wpool.at[dl : 2 * dl, :]
    load_out, load_up = load(wo_hbm, slot0, 0), load(wu_hbm, slot1, 1)
    load_down, load_out2 = load(wd_hbm, slot0, 2), load(wo_hbm, slot0, 3)
    load_v = load(v_hbm, wpool.at[0 : D * kc, :], 4)
    load_cot = load(cot_hbm, frames.at[1], 5)
    later = [load(k_hbm, k_ref, 6), load(x_hbm, x_ref, 7)]
    for g in range(2):
        later.append(load(wv_hbm.at[:, g * vh : (g + 1) * vh], wkv.at[g, :, 0:vh], 8 + g))
        later.append(
            load(wk_hbm.at[:, g * qh : (g + 1) * qh], wkv.at[g, :, vh : vh + qh], 10 + g)
        )
    load_out.start()
    load_up.start()
    load_cot.start()

    weights = ShardSums(
        doc, blk, nd, nb, 3 * pos, wunit, pos, [3 + 3 * k for k in range(bits)], False,
        *wscr[:5], wsum_ref, wscr[5:],
    )
    values = [
        ShardSums(
            doc, blk, nd, nb, pos, vunit, pos, lags, True, *vscr[g][:5], out, vscr[g][5:],
        )
        for g, (lags, out) in enumerate(
            (
                ([1 + k for k in range(bits)], vsum0_ref),
                ([1 + k for k in range(bits)], vsum1_ref),
            )
        )
    ]

    wrows, whalf = 2 * dl // nb, dl // 2
    vhalf = (vh + qh) // 2

    def w_mate(s):
        rows = pl.ds(pl.multiple_of(s % (2 * pos) * wrows, wrows), wrows)
        return remote(
            stage.at[rows, 0:whalf], weights.mate_in.at[s],
            weights.mate_s.at[s], weights.mate_r.at[s], doc, mate,
        )

    def v_mate(g):
        return lambda s: remote(
            vstage.at[g, s], values[g].mate_in.at[s],
            values[g].mate_s.at[s], values[g].mate_r.at[s], doc, mate,
        )

    parts, ahead = 2 * D, 4

    def chunk(j, core):
        return pl.ds(pl.multiple_of((2 * j + core) * rq, rq), rq)

    def right_copy(e, hop, j):
        rows = ga_all.at[e, chunk(j, c), :]
        return remote(
            rows, rows, ar_s.at[e, hop], ar_r.at[e, hop],
            doc, 2 * jnp.minimum(p + 1, pos - 1) + c,
        )

    def left_copy(e, hop, j):
        rows = ga_all.at[e, chunk(j, c), :]
        return remote(
            rows, rows, al_s.at[e, hop], al_r.at[e, hop],
            doc, 2 * jnp.maximum(p - 1, 0) + c,
        )

    def mate_copy(e, j, core):
        rows = ga_all.at[e, chunk(j, core), :]
        return remote(rows, rows, am_s.at[e, j], am_r.at[e, j], doc, mate)

    own_rows = pl.ds(pl.multiple_of(blk * rq, rq), rq)

    def delta_copy(i, rows):
        return remote(
            delta_all.at[rows, :], delta_all.at[rows, :], d_s.at[i - 1], d_r.at[i - 1],
            doc, lax.rem(blk + i, nb),
        )

    def direct_copy(i):
        return remote(
            direct_out, dir_in.at[i - 1], dir_s.at[i - 1], dir_r.at[i - 1],
            lax.rem(doc + i, nd), blk,
        )

    def send_own(e):
        @pl.when(p < pos - 1)
        def _():
            right_copy(e, 0, p).start()

        @pl.when(p > 0)
        def _():
            left_copy(e, 0, p).start()

        mate_copy(e, p, c).start()

    nm, act_low = acts.at[0], acts.at[1]
    mid = fpool.at[0:rows_all, :]
    xhat = fpool.at[rows_all : 2 * rows_all, :]
    slope = fpool.at[2 * rows_all : 3 * rows_all, :]
    kv_acc = fpool.at[0:din, 0 : vh + qh]
    step_w = dl // nb

    def weight_grad(m, left, right):
        low_t[...] = jnp.transpose(left[...])

        @pl.loop(0, pos)
        def _(j):
            s = m * pos + j
            for core in (1 - c, c):
                rows = pl.ds(pl.multiple_of((2 * j + core) * step_w, step_w), step_w)
                shard = dot_nn(low_t[rows, :], right[...]).astype(BF16)
                for i in range(2):
                    part = shard[:, i * whalf : (i + 1) * whalf]
                    if core is c:
                        weights.own[s, i * step_w : (i + 1) * step_w, :] = part
                    else:
                        at = pl.multiple_of(s % (2 * pos) * wrows, wrows) + i * step_w
                        stage[pl.ds(pl.multiple_of(at, 16), step_w), 0:whalf] = part
                if core is not c:
                    w_mate(s).start()

    att_low = att_ref[...].reshape(rows_all, DV)
    load_out.wait()
    mid[...] = dot_nn(att_low, slot0[...]) + jnp.concatenate([lat_ref[...]] * D, axis=0)
    load_down.start()
    xh, inv = norm_parts(mid[...])
    xhat[...] = xh
    nm[...] = (xh * gm_ref[...].reshape(1, -1)).astype(BF16)
    load_up.wait()
    act, sl = gelu_parts(dot_nn(nm[...], slot1[...]))
    slope[...] = sl
    act_low[...] = act.astype(BF16)
    load_cot.wait()
    gm[...] = frames[1].astype(BF16)
    pl.semaphore_wait(barrier, nb - 1 + nd - 1)
    weight_grad(0, act_low, gm)
    load_down.wait()
    frames[0] = mid[...] + dot_nn(act_low[...], slot0[...])
    store_out = pltpu.make_async_copy(frames.at[0], out_hbm, out_s)
    store_out.start()
    g_up[...] = (dot_nt(gm[...], slot0[...]) * slope[...]).astype(BF16)
    load_out2.start()
    for item in later:
        item.start()
    g_nm = dot_nt(g_up[...], slot1[...])
    gmlp_acc[...] = jnp.sum(g_nm * xhat[...], axis=0, keepdims=True)
    dxh = g_nm * gm_ref[...].reshape(1, -1)
    mid[...] = frames[1] + inv * (
        dxh
        - jnp.mean(dxh, axis=-1, keepdims=True)
        - xhat[...] * jnp.mean(dxh * xhat[...], axis=-1, keepdims=True)
    )
    gb[...] = mid[...].astype(BF16)
    for s in range(pos):
        weights.begin(s, w_mate)
    load_out2.wait()
    ga = dot_nt(gb[...], slot0[...])
    load_v.start()
    for g in range(2):
        for n in range(D):
            ga_all[g * D + n, own_rows, :] = ga[
                n * rq : (n + 1) * rq, g * vh : (g + 1) * vh
            ].astype(BF16)
    for e in range(ahead):
        send_own(e)
    lane = lax.broadcasted_iota(jnp.int32, (rq, 128), 1)
    delta = jnp.zeros((rq, 128), F32)
    for h in range(HEADS):
        cols = slice(window(h), window(h) + 256)
        prod = ga[:, cols] * (att_low[:, cols] * value_mask(h, rows_all)).astype(F32)
        one = jnp.sum(prod, axis=1, keepdims=True)
        for n in range(D):
            delta = delta + jnp.where(lane == n * HEADS + h, one[n * rq : (n + 1) * rq], 0.0)
    delta_all[own_rows, :] = delta
    for i in range(1, nb):
        delta_copy(i, own_rows).start()
    direct = mid[0:rq, :]
    for n in range(1, D):
        direct = direct + mid[n * rq : (n + 1) * rq, :]
    direct_out[...] = direct.astype(BF16)
    for i in range(1, nd):
        direct_copy(i).start()
    weight_grad(1, nm, g_up)
    for s in range(pos):
        w_mate(s).wait_send()
    weight_grad(2, att_low, gb)

    for h in range(HEADS):
        half = slice(h // hh * qh, h // hh * qh + qh)
        qm[h] = (qall_ref[...] * query_mask(h, LAT))[:, half]
    gq_acc[...] = jnp.zeros_like(gq_acc)
    kv_acc[...] = jnp.zeros((din, vh + qh), F32)
    gain_acc[...] = jnp.zeros_like(gain_acc)

    def forward_chunks(e, hop):
        j = p - 1 - hop

        @pl.when(j >= 0)
        def _():
            right_copy(e, hop, j).wait_recv()
            if hop + 1 < pos - 1:
                @pl.when(p < pos - 1)
                def _():
                    right_copy(e, hop + 1, j).start()

            mate_copy(e, j, c).start()

        i = p + 1 + hop

        @pl.when(i < pos)
        def _():
            left_copy(e, hop, i).wait_recv()
            if hop + 1 < pos - 1:
                @pl.when(p > 0)
                def _():
                    left_copy(e, hop + 1, i).start()

            mate_copy(e, i, c).start()

    def doc_rows(n):
        return pl.ds(pl.multiple_of(n * kc, kc), kc)

    def bytes_back(g, n):
        e = g * D + n
        for j in range(pos):
            mate_copy(e, j, 1 - c).wait_recv()
        bias = wide(row_to_lanes(bias_ref[pl.ds(n, 1), :]), LAT)
        logs, deltas = lse_ref[n], delta_t[n]
        kn = k_ref[n, :, g * qh : (g + 1) * qh]
        kt = jnp.transpose(kn)
        gv_acc[...] = jnp.zeros_like(gv_acc)
        for i in range(hh):
            h = g * hh + i
            cols = slice(window(i), window(i) + 256)
            vcols = slice(g * vh + window(i), g * vh + window(i) + 256)
            gah = ga_all[e, :, cols] * value_mask(i, LAT)
            s = dot_nt(kn, qm[h]) * SCORE2 + bias
            prob = jnp.exp2(s - logs[h : h + 1, :])
            dprob = dot_nt(wpool[doc_rows(n), vcols], gah)
            ds = (prob * (dprob - deltas[h : h + 1, :])).astype(BF16)
            ds_all[:, i * LAT : (i + 1) * LAT] = ds
            gv_acc[:, cols] += dot_nn(prob.astype(BF16), gah)
            head = slice(QK_HEAD * i, QK_HEAD * (i + 1))
            rows = slice(QK_HEAD * h, QK_HEAD * (h + 1))
            gq_acc[rows, :] += dot_nn(kt[head, :], ds)
        gk = dot_nn(ds_all[:, 0:LAT], qm[g * hh])
        for i in range(1, hh):
            gk = gk + dot_nn(ds_all[:, i * LAT : (i + 1) * LAT], qm[g * hh + i])
        grads_now = jnp.concatenate(
            [gv_acc[...].astype(BF16), (gk * SCORE_SCALE).astype(BF16)], axis=1
        )
        xh, inv = norm_parts(x_ref[n].astype(F32))
        kept = stage.at[doc_rows(n), 0:din]
        if g == 0:
            kept[...] = dot_nt(grads_now, wkv[0]).astype(BF16)
        else:
            gx = kept[...].astype(F32) + dot_nt(grads_now, wkv[1])
            gain_acc[...] += jnp.sum(gx * xh, axis=0, keepdims=True)
            dxh = gx * gb_ref[...].reshape(1, -1)
            slot = lax.rem(n, 2)

            @pl.when(n >= 2)
            def _():
                pltpu.make_async_copy(acts.at[slot, 0:kc, 0:din], bg_hbm.at[n - 2], bg_s.at[slot]).wait()

            dx = inv * (
                dxh
                - jnp.mean(dxh, axis=-1, keepdims=True)
                - xh * jnp.mean(dxh * xh, axis=-1, keepdims=True)
            )
            acts[slot, 0:kc, 0:din] = dx.astype(BF16)
            pltpu.make_async_copy(acts.at[slot, 0:kc, 0:din], bg_hbm.at[n], bg_s.at[slot]).start()
        normed_t = jnp.transpose((xh * gb_ref[...].reshape(1, -1)).astype(BF16))
        kv_acc[...] += dot_nn(normed_t, grads_now)

    def cut_values(g):
        step = din // nb
        for s in range(pos):
            for core in (1 - c, c):
                rows = pl.ds(pl.multiple_of((2 * s + core) * step, step), step)
                to = values[g].own if core is c else vstage.at[g]
                for i in range(2):
                    to[s, i * step : (i + 1) * step, :] = fpool[
                        rows, i * vhalf : (i + 1) * vhalf
                    ].astype(BF16)
            v_mate(g)(s).start()
        if g == 0:
            kv_acc[...] = jnp.zeros((din, vh + qh), F32)

    start0 = (pos + D + 2) // 2

    @pl.loop(0, parts + pos)
    def _(t):
        @pl.when(t < parts - ahead)
        def _():
            send_own(t + ahead)

        for hop in range(pos - 1):
            @pl.when((t >= hop) & (t - hop < parts))
            def _():
                forward_chunks(t - hop, hop)

        @pl.when(t % 2 == 0)
        def _():
            weights.step(t // 2 + 1, w_mate, 1)
            values[0].step(t // 2 - start0, v_mate(0))

        @pl.when(t == pos)
        def _():
            for i in range(1, nb):
                src = lax.rem(blk + nb - i, nb)
                delta_copy(i, pl.ds(pl.multiple_of(src * rq, rq), rq)).wait_recv()
            turned = jnp.transpose(delta_all[...])
            for n in range(D):
                delta_t[n] = turned[n * HEADS : (n + 1) * HEADS, :]
            for item in later:
                item.wait()
            load_v.wait()
            store_out.wait()
            for s in range(pos, 3 * pos):
                w_mate(s).wait_send()

        @pl.when((t >= pos) & (t < pos + D))
        def _():
            bytes_back(0, t - pos)

        @pl.when(t == pos + D)
        def _():
            cut_values(0)

        @pl.when(t >= pos + D)
        def _():
            bytes_back(1, t - pos - D)

    cut_values(1)

    gq_rows = (jnp.transpose(gq_acc[...]) * SCORE_SCALE).astype(BF16)
    gains = jnp.concatenate([gmlp_acc[...], gain_acc[...]], axis=1)
    rows8 = [gains[:, 256 * i : 256 * (i + 1)] for i in range(8)]
    gains8 = jnp.concatenate(rows8 + [jnp.zeros((8, 256), F32)], axis=0).astype(BF16)
    for j in range(nb):
        misc_out[j, 0:rq] = gq_rows[j * rq : (j + 1) * rq, :]
        misc_out[j, rq : rq + 16] = gains8

    def misc1(i, slot):
        peer = lax.rem(blk + i, nb)
        return remote(
            misc_out.at[peer], misc_in.at[slot], m1_s.at[i - 1], m1_r.at[i - 1], doc, peer
        )

    def misc2(i, slot):
        return remote(
            misc2_out, misc2_in.at[slot], m2_s.at[i - 1], m2_r.at[i - 1],
            lax.rem(doc + i, nd), blk,
        )

    def misc3(i, rows):
        return remote(
            gq_ref.at[rows, :], gq_ref.at[rows, :], m3_s.at[i - 1], m3_r.at[i - 1],
            doc, lax.rem(blk + i, nb),
        )

    for i in range(1, nb):
        misc1(i, blk).start()
    misc_in[blk] = misc_out[blk]

    first = (parts + pos + 1) // 2
    last = max(weights.steps - 1, start0 + values[0].steps, first + values[1].steps)

    @pl.loop(first, last)
    def _(t):
        values[1].step(t - first, v_mate(1))
        values[0].step(t - start0, v_mate(0))
        weights.step(t + 1, w_mate, 1)

        @pl.when(t == first + 1)
        def _():
            for i in range(1, nb):
                misc1(i, lax.rem(blk + nb - i, nb)).wait_recv()
            total = misc_in[0].astype(F32)
            for i in range(1, nb):
                total = total + misc_in[i].astype(F32)
            misc2_out[...] = total.astype(BF16)
            for i in range(1, nd):
                misc2(i, doc).start()
            misc2_in[doc] = misc2_out[...]

        @pl.when(t == first + 3)
        def _():
            for i in range(1, nd):
                misc2(i, lax.rem(doc + nd - i, nd)).wait_recv()
            total = misc2_in[0].astype(F32)
            for i in range(1, nd):
                total = total + misc2_in[i].astype(F32)
            gains_ref[...] = total[rq : rq + 8, :]
            gq_ref[own_rows, :] = total[0:rq].astype(BF16)
            for i in range(1, nb):
                misc3(i, own_rows).start()

    for i in range(1, nb):
        src = lax.rem(blk + nb - i, nb)
        misc3(i, pl.ds(pl.multiple_of(src * rq, rq), rq)).wait_recv()

    total = direct_out[...].astype(F32)
    for i in range(1, nd):
        direct_copy(i).wait_recv()
        total = total + dir_in[i - 1].astype(F32)
    dsum_ref[...] = total

    for n in range(D - 2, D):
        pltpu.make_async_copy(acts.at[n % 2, 0:kc, 0:din], bg_hbm.at[n], bg_s.at[n % 2]).wait()
    weights.drain()
    for g in range(2):
        values[g].drain()
        for s in range(pos):
            v_mate(g)(s).wait_send()
    for i in range(1, nb):
        delta_copy(i, own_rows).wait_send()
        misc1(i, blk).wait_send()
        misc3(i, own_rows).wait_send()
    for i in range(1, nd):
        direct_copy(i).wait_send()
        misc2(i, doc).wait_send()

    @pl.loop(0, parts)
    def _(e):
        mate_copy(e, p, c).wait_send()

        @pl.when(p < pos - 1)
        def _():
            right_copy(e, 0, p).wait_send()

        @pl.when(p > 0)
        def _():
            left_copy(e, 0, p).wait_send()

        for hop in range(pos - 1):
            j = p - 1 - hop

            @pl.when(j >= 0)
            def _():
                mate_copy(e, j, c).wait_send()
                if hop + 1 < pos - 1:
                    @pl.when(p < pos - 1)
                    def _():
                        right_copy(e, hop + 1, j).wait_send()

            i = p + 1 + hop

            @pl.when(i < pos)
            def _():
                mate_copy(e, i, c).wait_send()
                if hop + 1 < pos - 1:
                    @pl.when(p > 0)
                    def _():
                        left_copy(e, hop + 1, i).wait_send()


def backward(
    nb, nd, byte_embed, keys, values, w_out, w_up, w_down, w_key, w_value, cotangent,
    attended, latents, gain_mlp, bias, gain_bytes, queries, lse,
):
    D, kc, din = byte_embed.shape
    rq, dl = latents.shape
    pos = nb // 2
    rows = D * rq
    wunit, vunit = owner_rows(2 * dl // nb, nd), owner_rows(2 * din // nb, nd)
    whalf, vhalf = dl // 2, (DV + DQK) // 4
    vmem = pl.BlockSpec(memory_space=pltpu.VMEM)
    anywhere = pl.BlockSpec(memory_space=pl.ANY)
    dma = pltpu.SemaphoreType.DMA
    scratch = (
        shard_sum_scratch(nd, nb, 3 * pos, wunit, 2 * dl // nb, whalf)
        + shard_sum_scratch(nd, nb, pos, vunit, 2 * din // nb, vhalf)
        + shard_sum_scratch(nd, nb, pos, vunit, 2 * din // nb, vhalf)
        + [
            pltpu.VMEM((max(2 * dl, D * kc), dl), BF16),
            pltpu.VMEM((D, kc, din), BF16),
            pltpu.VMEM((D, kc, DQK), BF16),
            pltpu.VMEM((2 * D, LAT, DV // 2), BF16),
            pltpu.VMEM((LAT, 128), F32),
            pltpu.VMEM((D, HEADS, LAT), F32),
            pltpu.VMEM((HEADS, LAT, DQK // 2), BF16),
            pltpu.VMEM((2, din, (DV + DQK) // 2), BF16),
            pltpu.VMEM((kc, HEADS // 2 * LAT), BF16),
            pltpu.VMEM((kc, DV // 2), F32),
            pltpu.VMEM((DQK, LAT), F32),
            pltpu.VMEM((max(3 * rows, din), dl), F32),
            pltpu.VMEM((2, rows, dl), F32),
            pltpu.VMEM((dl, rows), BF16),
            pltpu.VMEM((2, rows, dl), BF16),
            pltpu.VMEM((rows, dl), BF16),
            pltpu.VMEM((rows, dl), BF16),
            pltpu.VMEM((rows, dl), BF16),
            pltpu.VMEM((max(2 * dl, D * kc), (DV + DQK) // 2), BF16),
            pltpu.VMEM((2, pos, 2 * din // nb, vhalf), BF16),
            pltpu.VMEM((1, din), F32),
            pltpu.VMEM((1, dl), F32),
            pltpu.VMEM((rq, dl), BF16),
            pltpu.VMEM((nd - 1, rq, dl), BF16),
            pltpu.VMEM((nb, rq + 16, 256), BF16),
            pltpu.VMEM((nb, rq + 16, 256), BF16),
            pltpu.VMEM((rq + 16, 256), BF16),
            pltpu.VMEM((nd, rq + 16, 256), BF16),
            dma((12,)), dma, dma((2,)),
            dma((2 * D, pos - 1)), dma((2 * D, pos - 1)),
            dma((2 * D, pos - 1)), dma((2 * D, pos - 1)),
            dma((2 * D, pos)), dma((2 * D, pos)),
            dma((nb - 1,)), dma((nb - 1,)), dma((nd - 1,)), dma((nd - 1,)),
            dma((nb - 1,)), dma((nb - 1,)), dma((nd - 1,)), dma((nd - 1,)),
            dma((nb - 1,)), dma((nb - 1,)),
        ]
    )
    return pl.pallas_call(
        functools.partial(backward_kernel, nb, nd, wunit, vunit),
        out_shape=(
            jax.ShapeDtypeStruct((rows, dl), F32),
            jax.ShapeDtypeStruct((D, kc, din), BF16),
            jax.ShapeDtypeStruct((3, wunit * nd, whalf), BF16),
            jax.ShapeDtypeStruct((1, vunit * nd, vhalf), BF16),
            jax.ShapeDtypeStruct((1, vunit * nd, vhalf), BF16),
            jax.ShapeDtypeStruct((rq, dl), F32),
            jax.ShapeDtypeStruct((LAT, DQK), BF16),
            jax.ShapeDtypeStruct((8, 256), F32),
        ),
        in_specs=[anywhere] * 9 + [vmem] * 7,
        out_specs=(anywhere,) * 2 + (vmem,) * 6,
        scratch_shapes=scratch,
        compiler_params=pltpu.CompilerParams(
            collective_id=1, has_side_effects=True, vmem_limit_bytes=63 * 2**20
        ),
        name="backward",
    )(
        byte_embed, keys, values.reshape(D * kc, DV), w_out, w_up, w_down, w_key, w_value,
        cotangent.reshape(rows, dl), attended, latents, gain_mlp, bias,
        gain_bytes, queries, lse,
    )


def finish_kernel(
    nb, rows_hbm, bytes_hbm, wsum_hbm, vsum0_ref, vsum1_ref, dsum_ref, gq_ref, gains_ref, cols_ref,
    lat_ref, gain_ref, wq_ref, rows_out, bytes_out, lgrad_ref, gq_gain_ref, gb_gain_ref,
    gm_gain_ref, wq_out, wk_out, wv_out, wo_out, wu_out, wd_out, turned,
    wsum_ref, bytes_in, bytes_buf, rows_buf, take_s, move_s,
):
    D = bytes_hbm.shape[0]
    pairs = [(bytes_hbm.at[n], bytes_in.at[n], bytes_buf.at[n], bytes_out.at[n]) for n in range(D)]
    pairs.append((rows_hbm, rows_buf, rows_buf, rows_out))
    takes = [
        pltpu.make_async_copy(src, buf, take_s.at[i]) for i, (src, buf, _, _) in enumerate(pairs)
    ]
    takes.append(pltpu.make_async_copy(wsum_hbm, wsum_ref, take_s.at[D + 1]))
    moves = [
        pltpu.make_async_copy(buf, out, move_s.at[i]) for i, (_, _, buf, out) in enumerate(pairs)
    ]
    for take in takes:
        take.start()
    for n in range(D + 1):
        takes[n].wait()
        if n < D:
            bytes_buf[n] = bytes_in[n].astype(F32)
        moves[n].start()
    takes[-1].wait()
    rq, dl = lat_ref.shape
    din, step, vstep = wk_out.shape[0] * nb, dl // nb, wk_out.shape[0]
    blk = lax.axis_index("blk")
    half = dl // 2
    for m, out in enumerate((wd_out, wu_out, wo_out)):
        for i in range(2):
            out[:, i * half : (i + 1) * half] = wsum_ref[
                m, i * step : (i + 1) * step, :
            ].astype(F32)
    width = (DV + DQK) // 4
    for g, ref in enumerate((vsum0_ref, vsum1_ref)):
        both = jnp.concatenate(
            [ref[0, i * vstep : (i + 1) * vstep, :].astype(F32) for i in range(2)], axis=1
        )
        at = DV // 2
        wv_out[:, g * at : (g + 1) * at] = both[:, :at]
        wk_out[:, g * DQK // 2 : (g + 1) * DQK // 2] = both[:, at : 2 * width]

    gq = gq_ref[...]
    cols = cols_ref[...]
    first = pl.multiple_of(jnp.minimum(blk * step // 128 * 128, dl - 256), 128)
    skip = blk * step - first
    turned[...] = dot_nn(jnp.transpose(cols), gq)
    wq_out[...] = turned[pl.ds(pl.multiple_of(skip, 16), step), :]
    dy = dot_nt(gq, wq_ref[pl.ds(first, 256), :])
    gain = jnp.sum(dy * cols.astype(F32), axis=0, keepdims=True) / gain_ref[pl.ds(first, 256)].reshape(1, -1)

    def cut(row, at, count):
        size = row.shape[1]
        return pltpu.roll(row, lax.rem(size - at, size), 1)[:, :count]

    gq_gain_ref[...] = cut(gain, skip, step)
    row = jnp.concatenate([gains_ref[i : i + 1, :] for i in range(8)], axis=1)
    gm_gain_ref[...] = cut(row[:, :dl], blk * step, step)
    gb_gain_ref[...] = cut(row[:, dl:], blk * vstep, vstep)

    own = gq_ref[pl.ds(pl.multiple_of(blk * rq, rq), rq), :]
    dxh = dot_nt(own, wq_ref[...]) * gain_ref[...].reshape(1, -1)
    xh, inv = norm_parts(lat_ref[...])
    lgrad_ref[...] = dsum_ref[...] + inv * (
        dxh
        - jnp.mean(dxh, axis=-1, keepdims=True)
        - xh * jnp.mean(dxh * xh, axis=-1, keepdims=True)
    )
    for move in moves:
        move.wait()


def finish(
    nb, latents_out, byte_grad, wsum, vsum0, vsum1, direct_sum, gq, gains, norm_cols, latents,
    gain_query, w_query,
):
    rq, dl = latents.shape
    din = gains.size - dl
    vmem = pl.BlockSpec(memory_space=pltpu.VMEM)
    anywhere = pl.BlockSpec(memory_space=pl.ANY)
    shapes = (
        latents_out.shape, byte_grad.shape, (rq, dl), (1, dl // nb), (1, din // nb), (1, dl // nb), (dl // nb, DQK),
        (din // nb, DQK), (din // nb, DV), (dl // nb, dl), (dl // nb, dl), (dl // nb, dl),
    )
    return pl.pallas_call(
        functools.partial(finish_kernel, nb),
        out_shape=tuple(jax.ShapeDtypeStruct(s, F32) for s in shapes),
        in_specs=[anywhere] * 3 + [vmem] * 9,
        out_specs=(anywhere,) * 2 + (vmem,) * 10,
        scratch_shapes=[
            pltpu.VMEM((256, DQK), F32),
            pltpu.VMEM(wsum.shape, BF16),
            pltpu.VMEM(byte_grad.shape, BF16),
            pltpu.VMEM(byte_grad.shape, F32),
            pltpu.VMEM(latents_out.shape, F32),
            pltpu.SemaphoreType.DMA((byte_grad.shape[0] + 2,)),
            pltpu.SemaphoreType.DMA((byte_grad.shape[0] + 1,)),
        ],
        compiler_params=pltpu.CompilerParams(vmem_limit_bytes=60 * 2**20),
        name="finish",
    )(
        latents_out, byte_grad, wsum, vsum0, vsum1, direct_sum, gq, gains, norm_cols, latents,
        gain_query, w_query,
    )


def body(
    byte_embed,
    doc_lengths,
    key_mask,
    latents,
    gain_query,
    gain_bytes,
    gain_mlp,
    w_query,
    w_key,
    w_value,
    w_out,
    w_up,
    w_down,
    cotangent,
):
    nb, nd = lax.axis_size("blk"), lax.axis_size("doc")
    attended, lse, keys, values, norm_cols, queries, bias = forward(
        nb, byte_embed, doc_lengths, key_mask, latents, gain_query, gain_bytes, w_query, w_key,
        w_value,
    )
    latents_out, byte_grad, wsum, vsum0, vsum1, direct_sum, gq, gains = backward(
        nb, nd, byte_embed, keys, values, w_out, w_up, w_down, w_key, w_value, cotangent,
        attended, latents, gain_mlp, bias, gain_bytes, queries, lse,
    )
    (
        latents_out, byte_grad, latents_grad, gain_query_grad, gain_bytes_grad, gain_mlp_grad,
        grad_w_query, grad_w_key, grad_w_value, grad_w_out, grad_w_up, grad_w_down,
    ) = finish(
        nb, latents_out, byte_grad, wsum, vsum0, vsum1, direct_sum, gq, gains, norm_cols,
        latents, gain_query, w_query,
    )
    latents_out = latents_out.reshape(cotangent.shape)
    return (
        latents_out,
        byte_grad,
        latents_grad,
        gain_query_grad.reshape(-1),
        gain_bytes_grad.reshape(-1),
        gain_mlp_grad.reshape(-1),
        grad_w_query,
        grad_w_key,
        grad_w_value,
        grad_w_out,
        grad_w_up,
        grad_w_down,
    )


def solution(mesh):
    in_specs = (
        P("doc", "blk", None),
        P("doc"),
        P("doc", "blk"),
        P("blk", None),
        P(),
        P(),
        P(),
        P(),
        P(),
        P(),
        P(),
        P(),
        P(),
        P("doc", "blk", None),
    )
    out_specs = (
        P("doc", "blk", None),
        P("doc", "blk", None),
        P("blk", None),
        P("blk"),
        P("blk"),
        P("blk"),
        P("blk", None),
        P("blk", None),
        P("blk", None),
        P("blk", None),
        P("blk", None),
        P("blk", None),
    )
    return jax.shard_map(body, mesh=mesh, in_specs=in_specs, out_specs=out_specs, check_vma=False)
```

```python
import functools
import math

import jax
import jax.numpy as jnp
from jax import lax
from jax.experimental import pallas as pl
from jax.experimental.pallas import tpu as pltpu
from jax.sharding import PartitionSpec as P

LAT = 256
HEADS = 8
QK_HEAD = 32
V_HEAD = 160
DQK = HEADS * QK_HEAD
DV = HEADS * V_HEAD
MESH = pl.DeviceIdType.MESH
F32 = jnp.float32
BF16 = jnp.bfloat16

epsilon = 1e-05
masked_score = -1e30
LOG2E = math.log2(math.e)
SCORE2 = QK_HEAD ** (-0.5) * LOG2E
SCORE_SCALE = QK_HEAD ** (-0.5)


def dot_nn(a, b):
    return jnp.dot(a, b, preferred_element_type=F32)


def dot_nt(a, b):
    return lax.dot_general(a, b, (((1,), (1,)), ((), ())), preferred_element_type=F32)


def norm_parts(v):
    centered = v - jnp.mean(v, axis=-1, keepdims=True)
    spread = jnp.mean(centered * centered, axis=-1, keepdims=True)
    inv = lax.rsqrt(spread + epsilon)
    return centered * inv, inv


def window(h):
    return V_HEAD * h // 128 * 128


def value_mask(h, rows):
    lane = lax.broadcasted_iota(jnp.int32, (rows, 256), 1) + window(h)
    keep = (lane >= V_HEAD * h) & (lane < V_HEAD * (h + 1))
    return jnp.where(keep, 1.0, 0.0).astype(BF16)


def query_mask(h, rows):
    lane = lax.broadcasted_iota(jnp.int32, (rows, DQK), 1)
    keep = (lane >= QK_HEAD * h) & (lane < QK_HEAD * (h + 1))
    return jnp.where(keep, 1.0, 0.0).astype(BF16)


def row_to_lanes(row):
    return jnp.transpose(jnp.broadcast_to(row, (128, row.shape[1])))


def wide(col, n):
    return jnp.concatenate([col] * (n // 128), axis=1) if n > 128 else col


def remote(src, dst, send, recv, doc, blk):
    return pltpu.make_async_remote_copy(
        src_ref=src, dst_ref=dst, send_sem=send, recv_sem=recv,
        device_id=(doc, blk), device_id_type=MESH,
    )


def forward_kernel(
    nb,
    x_hbm, wq_hbm, wk_hbm, wv_hbm, len_ref, mask_ref, lat_ref, gq_ref, gb_ref,
    att_ref, lse_ref, k_hbm, v_hbm, nlw_ref, qall_ref, bias_ref,
    x_ref, wq_ref, wk_ref, wv_ref, k_ref, v_ref, nl_cols, normed, qm, lloc, lmate, lz, acc, part, mate_in, rin, lin,
    load_s, x_s, out_s, q_s, q_r, n_s, n_r, l_s, l_r, mate_s, mate_r, rs_s, rs_r, ls_s, ls_r,
):
    D, kc, din = x_hbm.shape
    rq = lat_ref.shape[0]
    pos = nb // 2
    doc, blk = lax.axis_index("doc"), lax.axis_index("blk")
    p, c = blk // 2, blk % 2
    mate = 2 * p + 1 - c
    loads = [
        pltpu.make_async_copy(src, dst, load_s.at[i])
        for i, (src, dst) in enumerate(((wq_hbm, wq_ref), (wk_hbm, wk_ref), (wv_hbm, wv_ref)))
    ]

    def x_load(n):
        return pltpu.make_async_copy(x_hbm.at[n], x_ref.at[n], x_s.at[n])

    stores = [
        pltpu.make_async_copy(src, dst, out_s.at[i])
        for i, (src, dst) in enumerate(((k_ref, k_hbm), (v_ref, v_hbm)))
    ]
    loads[0].start()
    x_load(0).start()
    loads[1].start()
    for n in range(1, D):
        x_load(n).start()
    loads[2].start()
    barrier = pltpu.get_barrier_semaphore()
    for i in range(1, nb):
        pl.semaphore_signal(
            barrier, inc=1, device_id=(doc, lax.rem(blk + i, nb)), device_id_type=MESH
        )

    slots = blk * kc + lax.broadcasted_iota(jnp.int32, (1, kc), 1)
    for n in range(D):
        usable = (slots < len_ref[n]) & (mask_ref[n : n + 1, :] == 1)
        bias_ref[n : n + 1, :] = jnp.where(usable, 0.0, masked_score)

    xhat, _ = norm_parts(lat_ref[...])
    nl = (xhat * gq_ref[...].reshape(1, -1)).astype(BF16)
    step = nl.shape[1] // nb
    for j in range(nb):
        at = min(j * step // 128 * 128, nl.shape[1] - 256)
        nl_cols[j] = nl[:, at : at + 256]
    own = pl.ds(pl.multiple_of(blk * rq, rq), rq)
    loads[0].wait()
    qall_ref[own, :] = dot_nn(nl, wq_ref[...]).astype(BF16)
    pl.semaphore_wait(barrier, nb - 1)

    def q_copy(i, slot):
        return remote(
            qall_ref.at[own, :], qall_ref.at[slot, :], q_s.at[i - 1], q_r.at[i - 1],
            doc, lax.rem(blk + i, nb),
        )

    def n_copy(i, slot):
        peer = lax.rem(blk + i, nb)
        return remote(
            nl_cols.at[peer], nlw_ref.at[slot, :], n_s.at[i - 1], n_r.at[i - 1], doc, peer
        )

    for i in range(1, nb):
        q_copy(i, own).start()
    for i in range(1, nb):
        n_copy(i, own).start()
    nlw_ref[own, :] = nl_cols[blk]

    loads[1].wait()

    @pl.loop(0, D)
    def _(n):
        x_load(n).wait()
        xh, _ = norm_parts(x_ref[n].astype(F32))
        normed[n] = (xh * gb_ref[...].reshape(1, -1)).astype(BF16)
        k_ref[n] = dot_nn(normed[n], wk_ref[...]).astype(BF16)

    for i in range(1, nb):
        src = lax.rem(blk + nb - i, nb)
        q_copy(i, pl.ds(pl.multiple_of(src * rq, rq), rq)).wait_recv()
    for h in range(HEADS):
        qm[h] = qall_ref[...] * query_mask(h, LAT)

    stores[0].start()

    def own_logs(lo, hi):
        @pl.loop(lo, hi)
        def _(n):
            bias = wide(row_to_lanes(bias_ref[pl.ds(n, 1), :]), LAT)
            kn = k_ref[n]
            rows = []
            for h in range(HEADS):
                s = dot_nt(kn, qm[h]) * SCORE2 + bias
                top = jnp.max(s, axis=0, keepdims=True)
                tot = jnp.sum(jnp.exp2(s - top), axis=0, keepdims=True)
                rows.append(top + jnp.log(tot) * LOG2E)
            lloc[n] = jnp.concatenate(rows, axis=0)

    half, quarter = D // 2, D // 4

    def mine(b):
        return pl.ds(b * half + c * quarter, quarter)

    def other(b):
        return pl.ds(b * half + (1 - c) * quarter, quarter)

    def merge(a, b):
        top = jnp.maximum(a, b)
        return top + jnp.log(jnp.exp2(a - top) + jnp.exp2(b - top)) * LOG2E

    def first(b):
        return remote(lloc.at[other(b)], lmate.at[b], l_s.at[b, 0], l_r.at[b, 0], doc, mate)

    def z_copy(b, i, slot):
        return remote(
            lz.at[b, p], lz.at[b, slot], l_s.at[b, i], l_r.at[b, i],
            doc, 2 * lax.rem(p + i, pos) + c,
        )

    def last(b, part):
        return remote(
            lse_ref.at[part], lse_ref.at[part], l_s.at[b, pos], l_r.at[b, pos], doc, mate
        )

    def along(b):
        first(b).wait_recv()
        lz[b, p] = merge(lloc[mine(b)], lmate[b])
        for i in range(1, pos):
            z_copy(b, i, p).start()

    def close(b):
        for i in range(1, pos):
            z_copy(b, i, lax.rem(p + pos - i, pos)).wait_recv()
        total = lz[b, 0]
        for i in range(1, pos):
            total = merge(total, lz[b, i])
        lse_ref[mine(b)] = total
        last(b, mine(b)).start()

    def values(lo, hi):
        @pl.loop(lo, hi)
        def _(n):
            v_ref[n] = dot_nn(normed[n], wv_ref[...]).astype(BF16)

    own_logs(0, half)
    first(0).start()
    own_logs(half, D)
    first(1).start()
    along(0)
    loads[2].wait()
    values(0, quarter)
    along(1)
    values(quarter, D)
    stores[1].start()
    close(0)
    close(1)
    last(0, other(0)).wait_recv()

    def mate_copy(n):
        return remote(
            part.at[n, 1 - c], mate_in.at[n], mate_s.at[n], mate_r.at[n], doc, mate
        )

    def right_copy(n, j, src):
        return remote(
            src, rin.at[n, j], rs_s.at[n, j], rs_r.at[n, j],
            doc, 2 * jnp.minimum(p + 1, pos - 1) + c,
        )

    def left_copy(n, j, src):
        return remote(
            src, lin.at[n, j], ls_s.at[n, j], ls_r.at[n, j],
            doc, 2 * jnp.maximum(p - 1, 0) + c,
        )

    def chip_sum(n):
        mate_copy(n).wait_recv()
        both = part[n, c].astype(F32) + mate_in[n].astype(F32)
        part[n, c] = both.astype(BF16)

        @pl.when(p == 0)
        def _():
            for j in range(pos - 1, 0, -1):
                right_copy(n, j, part.at[n, c, j]).start()

        @pl.when(p == pos - 1)
        def _():
            for j in range(pos - 1):
                left_copy(n, j, part.at[n, c, j]).start()

    @pl.loop(0, D)
    def _(n):
        @pl.when(n == half)
        def _():
            last(1, other(1)).wait_recv()

        logs = lse_ref[n]
        logs_t = jnp.transpose(jnp.concatenate([logs] * (128 // HEADS), axis=0))
        bias = bias_ref[pl.ds(n, 1), :]
        kn = k_ref[n]
        acc[...] = jnp.zeros_like(acc)
        for h in range(HEADS):
            s = dot_nt(qm[h], kn) * SCORE2 + bias
            prob = jnp.exp2(s - logs_t[:, h : h + 1]).astype(BF16)
            cols = slice(window(h), window(h) + 256)
            acc[:, cols] += dot_nn(prob, v_ref[n, :, cols] * value_mask(h, kc))
        for j in range(nb):
            part[n, j % 2, j // 2] = acc[rq * j : rq * (j + 1), :].astype(BF16)
        mate_copy(n).start()

        @pl.when(n > 0)
        def _():
            chip_sum(n - 1)

    chip_sum(D - 1)

    def from_left(n):
        for j in range(pos - 1, 0, -1):
            @pl.when(j >= p)
            def _():
                right_copy(n, j, part.at[n, c, j]).wait_recv()

            @pl.when(j > p)
            def _():
                both = rin[n, j].astype(F32) + part[n, c, j].astype(F32)
                part[n, c, j] = both.astype(BF16)
                right_copy(n, j, part.at[n, c, j]).start()

    def from_right(n):
        for j in range(pos - 1):
            @pl.when(j <= p)
            def _():
                left_copy(n, j, part.at[n, c, j]).wait_recv()

            @pl.when(j < p)
            def _():
                both = lin[n, j].astype(F32) + part[n, c, j].astype(F32)
                part[n, c, j] = both.astype(BF16)
                left_copy(n, j, part.at[n, c, j]).start()

    def finish(n):
        acc[0:rq, :] = part[n, c, p].astype(F32)

        @pl.when(p > 0)
        def _():
            acc[0:rq, :] += rin[n, p].astype(F32)

        @pl.when(p < pos - 1)
        def _():
            acc[0:rq, :] += lin[n, p].astype(F32)

        att_ref[n] = acc[0:rq, :].astype(BF16)

    @pl.loop(0, D + pos - 1)
    def _(t):
        right_n, left_n, done_n = t - p, t - (pos - 1 - p), t - (pos - 1)

        @pl.when((p > 0) & (right_n >= 0) & (right_n < D))
        def _():
            from_left(right_n)

        @pl.when((p < pos - 1) & (left_n >= 0) & (left_n < D))
        def _():
            from_right(left_n)

        @pl.when(done_n >= 0)
        def _():
            finish(done_n)

    for i in range(1, nb):
        src = lax.rem(blk + nb - i, nb)
        n_copy(i, pl.ds(pl.multiple_of(src * rq, rq), rq)).wait_recv()

    for i in range(1, nb):
        q_copy(i, own).wait_send()
        n_copy(i, own).wait_send()
    for b in range(2):
        first(b).wait_send()
        for i in range(1, pos):
            z_copy(b, i, p).wait_send()
        last(b, mine(b)).wait_send()
    for store in stores:
        store.wait()

    @pl.loop(0, D)
    def _(n):
        mate_copy(n).wait_send()
        for j in range(pos):
            @pl.when((j > p) & (p < pos - 1))
            def _():
                right_copy(n, j, part.at[n, c, j]).wait_send()

            @pl.when((j < p) & (p > 0))
            def _():
                left_copy(n, j, part.at[n, c, j]).wait_send()


def forward(
    nb, byte_embed, doc_lengths, key_mask, latents, gain_query, gain_bytes, w_query, w_key, w_value
):
    D, kc, din = byte_embed.shape
    rq, dl = latents.shape
    pos = nb // 2
    vmem = pl.BlockSpec(memory_space=pltpu.VMEM)
    anywhere = pl.BlockSpec(memory_space=pl.ANY)
    dma = pltpu.SemaphoreType.DMA
    return pl.pallas_call(
        functools.partial(forward_kernel, nb),
        out_shape=(
            jax.ShapeDtypeStruct((D, rq, DV), BF16),
            jax.ShapeDtypeStruct((D, HEADS, LAT), F32),
            jax.ShapeDtypeStruct((D, kc, DQK), BF16),
            jax.ShapeDtypeStruct((D, kc, DV), BF16),
            jax.ShapeDtypeStruct((LAT, 256), BF16),
            jax.ShapeDtypeStruct((LAT, DQK), BF16),
            jax.ShapeDtypeStruct((D, kc), F32),
        ),
        in_specs=[anywhere] * 4 + [pl.BlockSpec(memory_space=pltpu.SMEM)] + [vmem] * 4,
        out_specs=(vmem, vmem, anywhere, anywhere, vmem, vmem, vmem),
        scratch_shapes=[
            pltpu.VMEM((D, kc, din), BF16),
            pltpu.VMEM(w_query.shape, BF16),
            pltpu.VMEM(w_key.shape, BF16),
            pltpu.VMEM(w_value.shape, BF16),
            pltpu.VMEM((D, kc, DQK), BF16),
            pltpu.VMEM((D, kc, DV), BF16),
            pltpu.VMEM((nb, rq, 256), BF16),
            pltpu.VMEM((D, kc, din), BF16),
            pltpu.VMEM((HEADS, LAT, DQK), BF16),
            pltpu.VMEM((D, HEADS, LAT), F32),
            pltpu.VMEM((2, D // 4, HEADS, LAT), F32),
            pltpu.VMEM((2, pos, D // 4, HEADS, LAT), F32),
            pltpu.VMEM((LAT, DV), F32),
            pltpu.VMEM((D, 2, pos, rq, DV), BF16),
            pltpu.VMEM((D, pos, rq, DV), BF16),
            pltpu.VMEM((D, pos, rq, DV), BF16),
            pltpu.VMEM((D, pos, rq, DV), BF16),
            dma((3,)), dma((D,)), dma((2,)),
            dma((nb - 1,)), dma((nb - 1,)), dma((nb - 1,)), dma((nb - 1,)),
            dma((2, pos + 1)), dma((2, pos + 1)),
            dma((D,)), dma((D,)),
            dma((D, pos)), dma((D, pos)), dma((D, pos)), dma((D, pos)),
        ],
        compiler_params=pltpu.CompilerParams(
            collective_id=0, has_side_effects=True, vmem_limit_bytes=56 * 2**20
        ),
        name="forward",
    )(
        byte_embed, w_query, w_key, w_value, doc_lengths, key_mask, latents, gain_query,
        gain_bytes,
    )


def gelu_parts(u):
    k = math.sqrt(2.0 / math.pi)
    sq = u * u
    t = jnp.tanh(k * u * (1.0 + 0.044715 * sq))
    value = 0.5 * u * (1.0 + t)
    slope = 0.5 * (1.0 + t) + 0.5 * k * u * (1.0 - t * t) * (1.0 + 3 * 0.044715 * sq)
    return value, slope


def owner_rows(total, docs):
    return -(-total // (16 * docs)) * 16


class ShardSums:
    def __init__(
        self, doc, blk, nd, nb, count, unit, group, lags, direct,
        own, mate_in, inbox, rin, lin, out, sems,
    ):
        self.doc, self.p, self.c = doc, blk // 2, blk % 2
        self.nd, self.pos, self.count, self.unit = nd, nb // 2, count, unit
        self.bits = nd.bit_length() - 1
        self.own, self.mate_in, self.inbox = own, mate_in, inbox
        self.rin, self.lin, self.out = rin, lin, out
        (
            self.mate_s, self.mate_r, self.in_s, self.in_r,
            self.right_s, self.right_r, self.left_s, self.left_r, self.out_s, self.out_r,
        ) = sems
        self.group, self.lags, self.direct = group, lags, direct
        self.steps = count // group + lags[-1] + (1 if direct else self.pos - 1)

    def weight(self, s, k):
        b = (s + k) % self.bits
        return 1 + b * (b + 1) // 2

    def my_bit(self, w):
        return (self.doc // w) % 2

    def quarter(self, s, k, i, sent):
        q = 0
        for r in range(k):
            w = self.weight(s, r)
            q = q + self.my_bit(w) * w
        w = self.weight(s, k)
        mine = self.my_bit(w)
        q = q + ((1 - mine) if sent else mine) * w
        for r in range(k + 1, self.bits):
            q = q + ((i >> (r - k - 1)) & 1) * self.weight(s, r)
        return q

    def width(self, k):
        return 2 ** (self.bits - 1 - k)

    def slot(self, k, i):
        return sum(self.width(r) for r in range(k)) + i

    def rows(self, q):
        return pl.ds(pl.multiple_of(q * self.unit, self.unit), self.unit)

    def halving(self, s, k, i):
        w = self.weight(s, k)
        peer = self.doc + w * (1 - 2 * self.my_bit(w))
        slot = self.slot(k, i)
        return remote(
            self.own.at[s, self.rows(self.quarter(s, k, i, True)), :], self.inbox.at[s, slot],
            self.in_s.at[s, slot], self.in_r.at[s, slot], peer, 2 * self.p + self.c,
        )

    def right(self, s):
        return remote(
            self.own.at[s, self.rows(self.doc), :], self.rin.at[s],
            self.right_s.at[s], self.right_r.at[s],
            self.doc, 2 * jnp.minimum(self.p + 1, self.pos - 1) + self.c,
        )

    def left(self, s):
        return remote(
            self.own.at[s, self.rows(self.doc), :], self.lin.at[s],
            self.left_s.at[s], self.left_r.at[s],
            self.doc, 2 * jnp.maximum(self.p - 1, 0) + self.c,
        )

    def share(self, m, i):
        return remote(
            self.out.at[m, self.rows(self.doc), :], self.out.at[m, self.rows(self.doc), :],
            self.out_s.at[m, i - 1], self.out_r.at[m, i - 1],
            lax.rem(self.doc + i, self.nd), 2 * self.p + self.c,
        )

    def shared(self, m, i):
        src = lax.rem(self.doc + self.nd - i, self.nd)
        return remote(
            self.out.at[m, self.rows(src), :], self.out.at[m, self.rows(src), :],
            self.out_s.at[m, i - 1], self.out_r.at[m, i - 1], src, 2 * self.p + self.c,
        )

    def add(self, s, q, other):
        rows = self.rows(q)
        self.own[s, rows, :] = (
            self.own[s, rows, :].astype(F32) + other.astype(F32)
        ).astype(BF16)

    def begin(self, s, mate_copy):
        mate_copy(s).wait_recv()
        rows = self.mate_in.shape[1]
        self.own[s, 0:rows, :] = (
            self.own[s, 0:rows, :].astype(F32) + self.mate_in[s].astype(F32)
        ).astype(BF16)
        for i in range(self.width(0)):
            self.halving(s, 0, i).start()

    def halve(self, s, k):
        for i in range(self.width(k - 1)):
            self.halving(s, k - 1, i).wait_recv()
            self.add(s, self.quarter(s, k - 1, i, False), self.inbox[s, self.slot(k - 1, i)])
        if k < self.bits:
            for i in range(self.width(k)):
                self.halving(s, k, i).start()
            return
        if self.direct:
            return
        j = s % self.pos

        @pl.when((self.p == 0) & (j > 0))
        def _():
            self.right(s).start()

        @pl.when((self.p == self.pos - 1) & (j < self.pos - 1))
        def _():
            self.left(s).start()

    def from_left(self, s):
        j = s % self.pos

        @pl.when(j >= self.p)
        def _():
            self.right(s).wait_recv()

        @pl.when(j > self.p)
        def _():
            self.add(s, self.doc, self.rin[s])
            self.right(s).start()

    def from_right(self, s):
        j = s % self.pos

        @pl.when(j <= self.p)
        def _():
            self.left(s).wait_recv()

        @pl.when(j < self.p)
        def _():
            self.add(s, self.doc, self.lin[s])
            self.left(s).start()

    def finish(self, s):
        @pl.when(s % self.pos == self.p)
        def _():
            m = s // self.pos

            @pl.when(self.p > 0)
            def _():
                self.add(s, self.doc, self.rin[s])

            @pl.when(self.p < self.pos - 1)
            def _():
                self.add(s, self.doc, self.lin[s])

            self.out[m, self.rows(self.doc), :] = self.own[s, self.rows(self.doc), :]
            for i in range(1, self.nd):
                self.share(m, i).start()

    def spread(self, i, back):
        to = lax.rem(self.p + (self.pos - i if back else i), self.pos)
        return remote(
            self.own.at[to, self.rows(self.doc), :], self.rin.at[i - 1],
            self.right_s.at[i - 1], self.right_r.at[i - 1], self.doc, 2 * to + self.c,
        )

    def scatter(self):
        for i in range(1, self.pos):
            self.spread(i, False).start()

    def collect(self):
        rows = self.rows(self.doc)
        total = self.own[self.p, rows, :].astype(F32)
        for i in range(1, self.pos):
            self.spread(i, True).wait_recv()
            total = total + self.rin[i - 1].astype(F32)
        self.out[0, rows, :] = total.astype(BF16)
        for i in range(1, self.nd):
            self.share(0, i).start()

    def step(self, t, mate_copy, entered=0):
        def at(t, when, run, turned=False):
            @pl.when((t >= 0) & (t < self.count // self.group) & when)
            def _():
                for i in range(self.group):
                    run(t * self.group + (self.group - 1 - i if turned else i))

        at(t, t >= entered, lambda s: self.begin(s, mate_copy))
        for k in range(1, self.bits + 1):
            at(t - self.lags[k - 1], True, functools.partial(self.halve, k=k))
        base = t - self.lags[-1]
        if self.direct:
            pl.when(base == 0)(self.scatter)
            pl.when(base == 1)(self.collect)
            return
        at(base - self.p, self.p > 0, self.from_left, True)
        at(base - (self.pos - 1 - self.p), self.p < self.pos - 1, self.from_right)
        at(base - (self.pos - 1), True, self.finish)

    def halved(self):
        @pl.loop(0, self.count)
        def _(s):
            for k in range(self.bits):
                for i in range(self.width(k)):
                    self.halving(s, k, i).wait_send()

    def drain(self):
        if self.direct:
            for i in range(1, self.pos):
                self.spread(i, False).wait_send()
        for m in range(self.count // self.pos):
            for i in range(1, self.nd):
                self.shared(m, i).wait_recv()
                self.share(m, i).wait_send()

        if self.direct:
            return

        @pl.loop(0, self.count)
        def _(s):
            j = s % self.pos

            @pl.when((j > self.p) & (self.p < self.pos - 1))
            def _():
                self.right(s).wait_send()

            @pl.when((j < self.p) & (self.p > 0))
            def _():
                self.left(s).wait_send()


def shard_sum_scratch(nd, nb, count, unit, rows, width, direct):
    dma = pltpu.SemaphoreType.DMA
    arrays = count // (nb // 2)
    return [
        pltpu.VMEM((count, unit * nd, width), BF16),
        pltpu.VMEM((count, rows, width), BF16),
        pltpu.VMEM((count, nd - 1, unit, width), BF16),
        pltpu.VMEM((count, unit, width), BF16),
        pltpu.VMEM((1, 16, 128) if direct else (count, unit, width), BF16),
        dma((count,)), dma((count,)),
        dma((count, nd - 1)), dma((count, nd - 1)),
        dma((count,)), dma((count,)), dma((count,)), dma((count,)),
        dma((arrays, nd - 1)), dma((arrays, nd - 1)),
    ]


def backward_kernel(nb, nd, wunit, vunit, *refs):
    (
        x_hbm, k_hbm, v_hbm, wo_hbm, wu_hbm, wd_hbm, wk_hbm, wv_hbm, cot_hbm,
        att_ref, lat_ref, gm_ref, bias_ref, gb_ref, qall_ref, lse_ref,
    ) = refs[:16]
    out_hbm, bg_hbm, wsum_ref, vsum0_ref, vsum1_ref, dsum_ref, gq_ref, gains_ref = refs[16:24]
    wscr, vscr = refs[24:39], (refs[39:54], refs[54:69])
    (
        wpool, x_ref, k_ref, ga_all, delta_all, delta_t, qm, wkv, gq_acc,
        fpool, frames, low_t, acts, gm, g_up, gb, stage, vstage, gain_acc, gmlp_acc, direct_out, dir_in,
        misc_out, misc_in, misc2_out, misc2_in,
        load_s, out_s, bg_s, ar_s, ar_r, al_s, al_r, am_s, am_r, d_s, d_r, dir_s, dir_r,
        m1_s, m1_r, m2_s, m2_r, m3_s, m3_r,
    ) = refs[69:]
    D, kc, din = x_ref.shape
    rq, dl = lat_ref.shape
    rows_all = D * rq
    pos = nb // 2
    hh, vh, qh = HEADS // 2, DV // 2, DQK // 2
    bits = nd.bit_length() - 1
    doc, blk = lax.axis_index("doc"), lax.axis_index("blk")
    p, c = blk // 2, blk % 2
    mate = 2 * p + 1 - c

    barrier = pltpu.get_barrier_semaphore()
    for i in range(1, nb):
        pl.semaphore_signal(
            barrier, inc=1, device_id=(doc, lax.rem(blk + i, nb)), device_id_type=MESH
        )
    for i in range(1, nd):
        pl.semaphore_signal(
            barrier, inc=1, device_id=(lax.rem(doc + i, nd), blk), device_id_type=MESH
        )

    def load(src, dst, i):
        return pltpu.make_async_copy(src, dst, load_s.at[i])

    slot0, slot1 = wpool.at[0:dl, :], wpool.at[dl : 2 * dl, :]
    load_out, load_up = load(wo_hbm, slot0, 0), load(wu_hbm, slot1, 1)
    load_down, load_out2 = load(wd_hbm, slot0, 2), load(wo_hbm, slot0, 3)
    load_v = load(v_hbm, wpool.at[0 : D * kc, :], 4)
    load_cot = load(cot_hbm, frames.at[1], 5)
    later = [load(k_hbm, k_ref, 6), load(x_hbm, x_ref, 7)]
    for g in range(2):
        later.append(load(wv_hbm.at[:, g * vh : (g + 1) * vh], wkv.at[g, :, 0:vh], 8 + g))
        later.append(
            load(wk_hbm.at[:, g * qh : (g + 1) * qh], wkv.at[g, :, vh : vh + qh], 10 + g)
        )
    load_out.start()
    load_up.start()
    load_cot.start()

    weights = ShardSums(
        doc, blk, nd, nb, 3 * pos, wunit, pos, [5 + 3 * k for k in range(bits)], False,
        *wscr[:5], wsum_ref, wscr[5:],
    )
    values = [
        ShardSums(
            doc, blk, nd, nb, pos, vunit, pos, lags, True, *vscr[g][:5], out, vscr[g][5:],
        )
        for g, (lags, out) in enumerate(
            (
                ([1 + k for k in range(bits)], vsum0_ref),
                ([1 + k for k in range(bits)], vsum1_ref),
            )
        )
    ]

    wrows, whalf = 2 * dl // nb, dl // 2
    vhalf = (vh + qh) // 2

    def w_mate(s):
        rows = pl.ds(pl.multiple_of(s % (2 * pos) * wrows, wrows), wrows)
        return remote(
            stage.at[rows, 0:whalf], weights.mate_in.at[s],
            weights.mate_s.at[s], weights.mate_r.at[s], doc, mate,
        )

    def v_mate(g):
        return lambda s: remote(
            vstage.at[s], values[g].mate_in.at[s],
            values[g].mate_s.at[s], values[g].mate_r.at[s], doc, mate,
        )

    parts, ahead = 2 * D, 4

    def chunk(j, core):
        return pl.ds(pl.multiple_of((2 * j + core) * rq, rq), rq)

    def right_copy(e, hop, j):
        rows = ga_all.at[e, chunk(j, c), :]
        return remote(
            rows, rows, ar_s.at[e, hop], ar_r.at[e, hop],
            doc, 2 * jnp.minimum(p + 1, pos - 1) + c,
        )

    def left_copy(e, hop, j):
        rows = ga_all.at[e, chunk(j, c), :]
        return remote(
            rows, rows, al_s.at[e, hop], al_r.at[e, hop],
            doc, 2 * jnp.maximum(p - 1, 0) + c,
        )

    def mate_copy(e, j, core):
        rows = ga_all.at[e, chunk(j, core), :]
        return remote(rows, rows, am_s.at[e, j], am_r.at[e, j], doc, mate)

    own_rows = pl.ds(pl.multiple_of(blk * rq, rq), rq)

    def delta_copy(i, rows):
        return remote(
            delta_all.at[rows, :], delta_all.at[rows, :], d_s.at[i - 1], d_r.at[i - 1],
            doc, lax.rem(blk + i, nb),
        )

    def direct_copy(i):
        return remote(
            direct_out, dir_in.at[i - 1], dir_s.at[i - 1], dir_r.at[i - 1],
            lax.rem(doc + i, nd), blk,
        )

    def send_own(e):
        @pl.when(p < pos - 1)
        def _():
            right_copy(e, 0, p).start()

        @pl.when(p > 0)
        def _():
            left_copy(e, 0, p).start()

        mate_copy(e, p, c).start()

    nm, act_low = acts.at[0], acts.at[1]
    mid = fpool.at[0:rows_all, :]
    xhat = fpool.at[rows_all : 2 * rows_all, :]
    slope = fpool.at[2 * rows_all : 3 * rows_all, :]
    kv_acc = fpool.at[0:din, 0 : vh + qh]
    step_w = dl // nb

    def weight_grad(m, left, right):
        low_t[...] = jnp.transpose(left[...])

        @pl.loop(0, pos)
        def _(j):
            s = m * pos + j
            for core in (1 - c, c):
                rows = pl.ds(pl.multiple_of((2 * j + core) * step_w, step_w), step_w)
                shard = dot_nn(low_t[rows, :], right[...]).astype(BF16)
                for i in range(2):
                    part = shard[:, i * whalf : (i + 1) * whalf]
                    if core is c:
                        weights.own[s, i * step_w : (i + 1) * step_w, :] = part
                    else:
                        at = pl.multiple_of(s % (2 * pos) * wrows, wrows) + i * step_w
                        stage[pl.ds(pl.multiple_of(at, 16), step_w), 0:whalf] = part
                if core is not c:
                    w_mate(s).start()

    att_low = att_ref[...].reshape(rows_all, DV)
    load_out.wait()
    mid[...] = dot_nn(att_low, slot0[...]) + jnp.concatenate([lat_ref[...]] * D, axis=0)
    load_down.start()
    xh, inv = norm_parts(mid[...])
    xhat[...] = xh
    nm[...] = (xh * gm_ref[...].reshape(1, -1)).astype(BF16)
    load_up.wait()
    act, sl = gelu_parts(dot_nn(nm[...], slot1[...]))
    slope[...] = sl
    act_low[...] = act.astype(BF16)
    load_cot.wait()
    gm[...] = frames[1].astype(BF16)
    pl.semaphore_wait(barrier, nb - 1 + nd - 1)
    weight_grad(0, act_low, gm)
    load_down.wait()
    frames[0] = mid[...] + dot_nn(act_low[...], slot0[...])
    store_out = pltpu.make_async_copy(frames.at[0], out_hbm, out_s)
    store_out.start()
    g_up[...] = (dot_nt(gm[...], slot0[...]) * slope[...]).astype(BF16)
    load_out2.start()
    for item in later:
        item.start()
    g_nm = dot_nt(g_up[...], slot1[...])
    gmlp_acc[...] = jnp.sum(g_nm * xhat[...], axis=0, keepdims=True)
    dxh = g_nm * gm_ref[...].reshape(1, -1)
    mid[...] = frames[1] + inv * (
        dxh
        - jnp.mean(dxh, axis=-1, keepdims=True)
        - xhat[...] * jnp.mean(dxh * xhat[...], axis=-1, keepdims=True)
    )
    gb[...] = mid[...].astype(BF16)
    for s in range(pos):
        weights.begin(s, w_mate)
    load_out2.wait()
    ga = dot_nt(gb[...], slot0[...])
    load_v.start()
    for g in range(2):
        for n in range(D):
            ga_all[g * D + n, own_rows, :] = ga[
                n * rq : (n + 1) * rq, g * vh : (g + 1) * vh
            ].astype(BF16)
    for e in range(ahead):
        send_own(e)
    lane = lax.broadcasted_iota(jnp.int32, (rq, 128), 1)
    delta = jnp.zeros((rq, 128), F32)
    for h in range(HEADS):
        cols = slice(window(h), window(h) + 256)
        prod = ga[:, cols] * (att_low[:, cols] * value_mask(h, rows_all)).astype(F32)
        one = jnp.sum(prod, axis=1, keepdims=True)
        for n in range(D):
            delta = delta + jnp.where(lane == n * HEADS + h, one[n * rq : (n + 1) * rq], 0.0)
    delta_all[own_rows, :] = delta
    for i in range(1, nb):
        delta_copy(i, own_rows).start()
    direct = mid[0:rq, :]
    for n in range(1, D):
        direct = direct + mid[n * rq : (n + 1) * rq, :]
    direct_out[...] = direct.astype(BF16)
    for i in range(1, nd):
        direct_copy(i).start()
    weight_grad(1, nm, g_up)
    for s in range(pos):
        w_mate(s).wait_send()
    weight_grad(2, att_low, gb)

    for h in range(HEADS):
        half = slice(h // hh * qh, h // hh * qh + qh)
        qm[h] = (qall_ref[...] * query_mask(h, LAT))[:, half]
    gq_acc[...] = jnp.zeros_like(gq_acc)
    kv_acc[...] = jnp.zeros((din, vh + qh), F32)
    gain_acc[...] = jnp.zeros_like(gain_acc)

    def forward_chunks(e, hop):
        j = p - 1 - hop

        @pl.when(j >= 0)
        def _():
            right_copy(e, hop, j).wait_recv()
            if hop + 1 < pos - 1:
                @pl.when(p < pos - 1)
                def _():
                    right_copy(e, hop + 1, j).start()

            mate_copy(e, j, c).start()

        i = p + 1 + hop

        @pl.when(i < pos)
        def _():
            left_copy(e, hop, i).wait_recv()
            if hop + 1 < pos - 1:
                @pl.when(p > 0)
                def _():
                    left_copy(e, hop + 1, i).start()

            mate_copy(e, i, c).start()

    def doc_rows(n):
        return pl.ds(pl.multiple_of(n * kc, kc), kc)

    def scores_back(g, n, i):
        e = g * D + n
        bias = wide(row_to_lanes(bias_ref[pl.ds(n, 1), :]), LAT)
        logs, deltas = lse_ref[n], delta_t[n]
        kn = k_ref[n, :, g * qh : (g + 1) * qh]
        kt = jnp.transpose(kn)
        gk = None
        for k in range(hh):
            h, at = g * hh + k, window(k)
            vcols = slice(g * vh + at, g * vh + at + 256)
            gah = ga_all[e, :, at : at + 256] * value_mask(k, LAT)
            s = dot_nt(kn, qm[h]) * SCORE2 + bias
            prob = jnp.exp2(s - logs[h : h + 1, :])
            dprob = dot_nt(wpool[doc_rows(n), vcols], gah)
            ds = (prob * (dprob - deltas[h : h + 1, :])).astype(BF16)
            gv = dot_nn(prob.astype(BF16), gah)
            if k == 0:
                frames[i, 0:kc, 0:128] = gv[:, 0:128]
            else:
                frames[i, 0:kc, at : at + 128] += gv[:, 0:128]
            frames[i, 0:kc, at + 128 : at + 256] = gv[:, 128:256]
            part = dot_nn(ds, qm[h])
            gk = part if k == 0 else gk + part
            rows = slice(QK_HEAD * h, QK_HEAD * (h + 1))
            gq_acc[rows, :] += dot_nn(kt[QK_HEAD * k : QK_HEAD * (k + 1), :], ds)
        return jnp.concatenate(
            [frames[i, 0:kc, 0:vh].astype(BF16), (gk * SCORE_SCALE).astype(BF16)], axis=1
        )

    def wave(w):
        @pl.when(w < parts - ahead)
        def _():
            send_own(w + ahead)

        for hop in range(pos - 1):
            @pl.when((w >= hop) & (w - hop < parts))
            def _():
                forward_chunks(w - hop, hop)

    def bytes_back(g, m, w):
        n0 = 2 * m
        both = []
        for i in range(2):
            if i == 1:
                wave(w)
            for j in range(pos):
                mate_copy(g * D + n0 + i, j, 1 - c).wait_recv()
            both.append(scores_back(g, n0 + i, i))
        grads = jnp.concatenate(both, axis=0)
        xh, inv = norm_parts(x_ref[pl.ds(n0, 2)].reshape(2 * kc, din).astype(F32))
        kept = stage.at[pl.ds(pl.multiple_of(n0 * kc, 2 * kc), 2 * kc), 0:din]
        if g == 0:
            kept[...] = dot_nt(grads, wkv[0]).astype(BF16)
        else:
            gx = kept[...].astype(F32) + dot_nt(grads, wkv[1])
            gain_acc[...] += jnp.sum(gx * xh, axis=0, keepdims=True)
            dxh = gx * gb_ref[...].reshape(1, -1)
            dx = inv * (
                dxh
                - jnp.mean(dxh, axis=-1, keepdims=True)
                - xh * jnp.mean(dxh * xh, axis=-1, keepdims=True)
            )
            for i in range(2):
                @pl.when(m >= 1)
                def _():
                    pltpu.make_async_copy(
                        acts.at[i, 0:kc, 0:din], bg_hbm.at[n0 + i - 2], bg_s.at[i]
                    ).wait()

                acts[i, 0:kc, 0:din] = dx[i * kc : (i + 1) * kc, :].astype(BF16)
                pltpu.make_async_copy(
                    acts.at[i, 0:kc, 0:din], bg_hbm.at[n0 + i], bg_s.at[i]
                ).start()
        normed_t = jnp.transpose((xh * gb_ref[...].reshape(1, -1)).astype(BF16))
        kv_acc[...] += dot_nn(normed_t, grads)

    def cut_values(g):
        step = din // nb
        if g == 1:
            for s in range(pos):
                v_mate(0)(s).wait_send()
        for s in range(pos):
            for core in (1 - c, c):
                rows = pl.ds(pl.multiple_of((2 * s + core) * step, step), step)
                to = values[g].own if core is c else vstage
                for i in range(2):
                    to[s, i * step : (i + 1) * step, :] = fpool[
                        rows, i * vhalf : (i + 1) * vhalf
                    ].astype(BF16)
            v_mate(g)(s).start()
        if g == 0:
            kv_acc[...] = jnp.zeros((din, vh + qh), F32)

    pairs, fill = D // 2, pos // 2
    start0 = fill + pairs + 1

    @pl.loop(0, 2 * pairs + fill)
    def _(t):
        wave(2 * t)

        @pl.when(t < fill)
        def _():
            wave(2 * t + 1)

        weights.step(t + 1, w_mate, 1)
        values[0].step(t - start0, v_mate(0))

        @pl.when(t == fill)
        def _():
            for i in range(1, nb):
                src = lax.rem(blk + nb - i, nb)
                delta_copy(i, pl.ds(pl.multiple_of(src * rq, rq), rq)).wait_recv()
            turned = jnp.transpose(delta_all[...])
            for n in range(D):
                delta_t[n] = turned[n * HEADS : (n + 1) * HEADS, :]
            for item in later:
                item.wait()
            load_v.wait()
            store_out.wait()
            for s in range(pos, 3 * pos):
                w_mate(s).wait_send()

        @pl.when((t >= fill) & (t < fill + pairs))
        def _():
            bytes_back(0, t - fill, 2 * t + 1)

        @pl.when(t == fill + pairs)
        def _():
            cut_values(0)

        @pl.when(t >= fill + pairs)
        def _():
            bytes_back(1, t - fill - pairs, 2 * t + 1)

    cut_values(1)

    gq_rows = (jnp.transpose(gq_acc[...]) * SCORE_SCALE).astype(BF16)
    gains = jnp.concatenate([gmlp_acc[...], gain_acc[...]], axis=1)
    rows8 = [gains[:, 256 * i : 256 * (i + 1)] for i in range(8)]
    gains8 = jnp.concatenate(rows8 + [jnp.zeros((8, 256), F32)], axis=0).astype(BF16)
    for j in range(nb):
        misc_out[j, 0:rq] = gq_rows[j * rq : (j + 1) * rq, :]
        misc_out[j, rq : rq + 16] = gains8

    def misc1(i, slot):
        peer = lax.rem(blk + i, nb)
        return remote(
            misc_out.at[peer], misc_in.at[slot], m1_s.at[i - 1], m1_r.at[i - 1], doc, peer
        )

    def misc2(i, slot):
        return remote(
            misc2_out, misc2_in.at[slot], m2_s.at[i - 1], m2_r.at[i - 1],
            lax.rem(doc + i, nd), blk,
        )

    def misc3(i, rows):
        return remote(
            gq_ref.at[rows, :], gq_ref.at[rows, :], m3_s.at[i - 1], m3_r.at[i - 1],
            doc, lax.rem(blk + i, nb),
        )

    for i in range(1, nb):
        misc1(i, blk).start()
    misc_in[blk] = misc_out[blk]

    @pl.loop(0, parts)
    def _(e):
        mate_copy(e, p, c).wait_send()

        @pl.when(p < pos - 1)
        def _():
            right_copy(e, 0, p).wait_send()

        @pl.when(p > 0)
        def _():
            left_copy(e, 0, p).wait_send()

        for hop in range(pos - 1):
            j = p - 1 - hop

            @pl.when(j >= 0)
            def _():
                mate_copy(e, j, c).wait_send()
                if hop + 1 < pos - 1:
                    @pl.when(p < pos - 1)
                    def _():
                        right_copy(e, hop + 1, j).wait_send()

            i = p + 1 + hop

            @pl.when(i < pos)
            def _():
                mate_copy(e, i, c).wait_send()
                if hop + 1 < pos - 1:
                    @pl.when(p > 0)
                    def _():
                        left_copy(e, hop + 1, i).wait_send()

    total = direct_out[...].astype(F32)
    for i in range(1, nd):
        direct_copy(i).wait_recv()
        total = total + dir_in[i - 1].astype(F32)
    dsum_ref[...] = total

    for n in range(D - 2, D):
        pltpu.make_async_copy(acts.at[n % 2, 0:kc, 0:din], bg_hbm.at[n], bg_s.at[n % 2]).wait()
    first = 2 * pairs + fill
    last = max(weights.steps - 1, start0 + values[0].steps, first + values[1].steps)

    @pl.loop(first, last)
    def _(t):
        values[1].step(t - first, v_mate(1))
        values[0].step(t - start0, v_mate(0))
        weights.step(t + 1, w_mate, 1)

        @pl.when(t == first)
        def _():
            for i in range(1, nb):
                misc1(i, lax.rem(blk + nb - i, nb)).wait_recv()
            total = misc_in[0].astype(F32)
            for i in range(1, nb):
                total = total + misc_in[i].astype(F32)
            misc2_out[...] = total.astype(BF16)
            for i in range(1, nd):
                misc2(i, doc).start()
            misc2_in[doc] = misc2_out[...]

        @pl.when(t == first + 1)
        def _():
            for i in range(1, nd):
                misc2(i, lax.rem(doc + nd - i, nd)).wait_recv()
            total = misc2_in[0].astype(F32)
            for i in range(1, nd):
                total = total + misc2_in[i].astype(F32)
            weights.halved()
            values[0].halved()
            gains_ref[...] = total[rq : rq + 8, :]
            gq_ref[own_rows, :] = total[0:rq].astype(BF16)
            for i in range(1, nb):
                misc3(i, own_rows).start()

    for i in range(1, nb):
        src = lax.rem(blk + nb - i, nb)
        misc3(i, pl.ds(pl.multiple_of(src * rq, rq), rq)).wait_recv()

    values[1].halved()
    weights.drain()
    for g in range(2):
        values[g].drain()
    for s in range(pos):
        v_mate(1)(s).wait_send()
    for i in range(1, nb):
        delta_copy(i, own_rows).wait_send()
        misc1(i, blk).wait_send()
        misc3(i, own_rows).wait_send()
    for i in range(1, nd):
        direct_copy(i).wait_send()
        misc2(i, doc).wait_send()


def backward(
    nb, nd, byte_embed, keys, values, w_out, w_up, w_down, w_key, w_value, cotangent,
    attended, latents, gain_mlp, bias, gain_bytes, queries, lse,
):
    D, kc, din = byte_embed.shape
    rq, dl = latents.shape
    pos = nb // 2
    rows = D * rq
    wunit, vunit = owner_rows(2 * dl // nb, nd), owner_rows(2 * din // nb, nd)
    whalf, vhalf = dl // 2, (DV + DQK) // 4
    vmem = pl.BlockSpec(memory_space=pltpu.VMEM)
    anywhere = pl.BlockSpec(memory_space=pl.ANY)
    dma = pltpu.SemaphoreType.DMA
    scratch = (
        shard_sum_scratch(nd, nb, 3 * pos, wunit, 2 * dl // nb, whalf, False)
        + shard_sum_scratch(nd, nb, pos, vunit, 2 * din // nb, vhalf, True)
        + shard_sum_scratch(nd, nb, pos, vunit, 2 * din // nb, vhalf, True)
        + [
            pltpu.VMEM((max(2 * dl, D * kc), dl), BF16),
            pltpu.VMEM((D, kc, din), BF16),
            pltpu.VMEM((D, kc, DQK), BF16),
            pltpu.VMEM((2 * D, LAT, DV // 2), BF16),
            pltpu.VMEM((LAT, 128), F32),
            pltpu.VMEM((D, HEADS, LAT), F32),
            pltpu.VMEM((HEADS, LAT, DQK // 2), BF16),
            pltpu.VMEM((2, din, (DV + DQK) // 2), BF16),
            pltpu.VMEM((DQK, LAT), F32),
            pltpu.VMEM((max(3 * rows, din), dl), F32),
            pltpu.VMEM((2, rows, dl), F32),
            pltpu.VMEM((dl, rows), BF16),
            pltpu.VMEM((2, rows, dl), BF16),
            pltpu.VMEM((rows, dl), BF16),
            pltpu.VMEM((rows, dl), BF16),
            pltpu.VMEM((rows, dl), BF16),
            pltpu.VMEM((max(2 * dl, D * kc), (DV + DQK) // 2), BF16),
            pltpu.VMEM((pos, 2 * din // nb, vhalf), BF16),
            pltpu.VMEM((1, din), F32),
            pltpu.VMEM((1, dl), F32),
            pltpu.VMEM((rq, dl), BF16),
            pltpu.VMEM((nd - 1, rq, dl), BF16),
            pltpu.VMEM((nb, rq + 16, 256), BF16),
            pltpu.VMEM((nb, rq + 16, 256), BF16),
            pltpu.VMEM((rq + 16, 256), BF16),
            pltpu.VMEM((nd, rq + 16, 256), BF16),
            dma((12,)), dma, dma((2,)),
            dma((2 * D, pos - 1)), dma((2 * D, pos - 1)),
            dma((2 * D, pos - 1)), dma((2 * D, pos - 1)),
            dma((2 * D, pos)), dma((2 * D, pos)),
            dma((nb - 1,)), dma((nb - 1,)), dma((nd - 1,)), dma((nd - 1,)),
            dma((nb - 1,)), dma((nb - 1,)), dma((nd - 1,)), dma((nd - 1,)),
            dma((nb - 1,)), dma((nb - 1,)),
        ]
    )
    return pl.pallas_call(
        functools.partial(backward_kernel, nb, nd, wunit, vunit),
        out_shape=(
            jax.ShapeDtypeStruct((rows, dl), F32),
            jax.ShapeDtypeStruct((D, kc, din), BF16),
            jax.ShapeDtypeStruct((3, wunit * nd, whalf), BF16),
            jax.ShapeDtypeStruct((1, vunit * nd, vhalf), BF16),
            jax.ShapeDtypeStruct((1, vunit * nd, vhalf), BF16),
            jax.ShapeDtypeStruct((rq, dl), F32),
            jax.ShapeDtypeStruct((LAT, DQK), BF16),
            jax.ShapeDtypeStruct((8, 256), F32),
        ),
        in_specs=[anywhere] * 9 + [vmem] * 7,
        out_specs=(anywhere,) * 2 + (vmem,) * 6,
        scratch_shapes=scratch,
        compiler_params=pltpu.CompilerParams(
            collective_id=1, has_side_effects=True, vmem_limit_bytes=63 * 2**20
        ),
        name="backward",
    )(
        byte_embed, keys, values.reshape(D * kc, DV), w_out, w_up, w_down, w_key, w_value,
        cotangent.reshape(rows, dl), attended, latents, gain_mlp, bias,
        gain_bytes, queries, lse,
    )


def finish_kernel(
    nb, rows_hbm, bytes_hbm, wsum_hbm, vsum0_ref, vsum1_ref, dsum_ref, gq_ref, gains_ref, cols_ref,
    lat_ref, gain_ref, wq_ref, rows_out, bytes_out, lgrad_ref, gq_gain_ref, gb_gain_ref,
    gm_gain_ref, wq_out, wk_out, wv_out, wo_out, wu_out, wd_out, turned,
    wsum_ref, bytes_in, bytes_buf, rows_buf, take_s, move_s,
):
    D = bytes_hbm.shape[0]
    pairs = [(bytes_hbm.at[n], bytes_in.at[n], bytes_buf.at[n], bytes_out.at[n]) for n in range(D)]
    pairs.append((rows_hbm, rows_buf, rows_buf, rows_out))
    takes = [
        pltpu.make_async_copy(src, buf, take_s.at[i]) for i, (src, buf, _, _) in enumerate(pairs)
    ]
    takes.append(pltpu.make_async_copy(wsum_hbm, wsum_ref, take_s.at[D + 1]))
    moves = [
        pltpu.make_async_copy(buf, out, move_s.at[i]) for i, (_, _, buf, out) in enumerate(pairs)
    ]
    for take in takes:
        take.start()
    for n in range(D + 1):
        takes[n].wait()
        if n < D:
            bytes_buf[n] = bytes_in[n].astype(F32)
        moves[n].start()
    takes[-1].wait()
    rq, dl = lat_ref.shape
    din, step, vstep = wk_out.shape[0] * nb, dl // nb, wk_out.shape[0]
    blk = lax.axis_index("blk")
    half = dl // 2
    for m, out in enumerate((wd_out, wu_out, wo_out)):
        for i in range(2):
            out[:, i * half : (i + 1) * half] = wsum_ref[
                m, i * step : (i + 1) * step, :
            ].astype(F32)
    width = (DV + DQK) // 4
    for g, ref in enumerate((vsum0_ref, vsum1_ref)):
        both = jnp.concatenate(
            [ref[0, i * vstep : (i + 1) * vstep, :].astype(F32) for i in range(2)], axis=1
        )
        at = DV // 2
        wv_out[:, g * at : (g + 1) * at] = both[:, :at]
        wk_out[:, g * DQK // 2 : (g + 1) * DQK // 2] = both[:, at : 2 * width]

    gq = gq_ref[...]
    cols = cols_ref[...]
    first = pl.multiple_of(jnp.minimum(blk * step // 128 * 128, dl - 256), 128)
    skip = blk * step - first
    turned[...] = dot_nn(jnp.transpose(cols), gq)
    wq_out[...] = turned[pl.ds(pl.multiple_of(skip, 16), step), :]
    dy = dot_nt(gq, wq_ref[pl.ds(first, 256), :])
    gain = jnp.sum(dy * cols.astype(F32), axis=0, keepdims=True) / gain_ref[pl.ds(first, 256)].reshape(1, -1)

    def cut(row, at, count):
        size = row.shape[1]
        return pltpu.roll(row, lax.rem(size - at, size), 1)[:, :count]

    gq_gain_ref[...] = cut(gain, skip, step)
    row = jnp.concatenate([gains_ref[i : i + 1, :] for i in range(8)], axis=1)
    gm_gain_ref[...] = cut(row[:, :dl], blk * step, step)
    gb_gain_ref[...] = cut(row[:, dl:], blk * vstep, vstep)

    own = gq_ref[pl.ds(pl.multiple_of(blk * rq, rq), rq), :]
    dxh = dot_nt(own, wq_ref[...]) * gain_ref[...].reshape(1, -1)
    xh, inv = norm_parts(lat_ref[...])
    lgrad_ref[...] = dsum_ref[...] + inv * (
        dxh
        - jnp.mean(dxh, axis=-1, keepdims=True)
        - xh * jnp.mean(dxh * xh, axis=-1, keepdims=True)
    )
    for move in moves:
        move.wait()


def finish(
    nb, latents_out, byte_grad, wsum, vsum0, vsum1, direct_sum, gq, gains, norm_cols, latents,
    gain_query, w_query,
):
    rq, dl = latents.shape
    din = gains.size - dl
    vmem = pl.BlockSpec(memory_space=pltpu.VMEM)
    anywhere = pl.BlockSpec(memory_space=pl.ANY)
    shapes = (
        latents_out.shape, byte_grad.shape, (rq, dl), (1, dl // nb), (1, din // nb), (1, dl // nb), (dl // nb, DQK),
        (din // nb, DQK), (din // nb, DV), (dl // nb, dl), (dl // nb, dl), (dl // nb, dl),
    )
    return pl.pallas_call(
        functools.partial(finish_kernel, nb),
        out_shape=tuple(jax.ShapeDtypeStruct(s, F32) for s in shapes),
        in_specs=[anywhere] * 3 + [vmem] * 9,
        out_specs=(anywhere,) * 2 + (vmem,) * 10,
        scratch_shapes=[
            pltpu.VMEM((256, DQK), F32),
            pltpu.VMEM(wsum.shape, BF16),
            pltpu.VMEM(byte_grad.shape, BF16),
            pltpu.VMEM(byte_grad.shape, F32),
            pltpu.VMEM(latents_out.shape, F32),
            pltpu.SemaphoreType.DMA((byte_grad.shape[0] + 2,)),
            pltpu.SemaphoreType.DMA((byte_grad.shape[0] + 1,)),
        ],
        compiler_params=pltpu.CompilerParams(vmem_limit_bytes=60 * 2**20),
        name="finish",
    )(
        latents_out, byte_grad, wsum, vsum0, vsum1, direct_sum, gq, gains, norm_cols, latents,
        gain_query, w_query,
    )


def body(
    byte_embed,
    doc_lengths,
    key_mask,
    latents,
    gain_query,
    gain_bytes,
    gain_mlp,
    w_query,
    w_key,
    w_value,
    w_out,
    w_up,
    w_down,
    cotangent,
):
    nb, nd = lax.axis_size("blk"), lax.axis_size("doc")
    attended, lse, keys, values, norm_cols, queries, bias = forward(
        nb, byte_embed, doc_lengths, key_mask, latents, gain_query, gain_bytes, w_query, w_key,
        w_value,
    )
    latents_out, byte_grad, wsum, vsum0, vsum1, direct_sum, gq, gains = backward(
        nb, nd, byte_embed, keys, values, w_out, w_up, w_down, w_key, w_value, cotangent,
        attended, latents, gain_mlp, bias, gain_bytes, queries, lse,
    )
    (
        latents_out, byte_grad, latents_grad, gain_query_grad, gain_bytes_grad, gain_mlp_grad,
        grad_w_query, grad_w_key, grad_w_value, grad_w_out, grad_w_up, grad_w_down,
    ) = finish(
        nb, latents_out, byte_grad, wsum, vsum0, vsum1, direct_sum, gq, gains, norm_cols,
        latents, gain_query, w_query,
    )
    latents_out = latents_out.reshape(cotangent.shape)
    return (
        latents_out,
        byte_grad,
        latents_grad,
        gain_query_grad.reshape(-1),
        gain_bytes_grad.reshape(-1),
        gain_mlp_grad.reshape(-1),
        grad_w_query,
        grad_w_key,
        grad_w_value,
        grad_w_out,
        grad_w_up,
        grad_w_down,
    )


def solution(mesh):
    in_specs = (
        P("doc", "blk", None),
        P("doc"),
        P("doc", "blk"),
        P("blk", None),
        P(),
        P(),
        P(),
        P(),
        P(),
        P(),
        P(),
        P(),
        P(),
        P("doc", "blk", None),
    )
    out_specs = (
        P("doc", "blk", None),
        P("doc", "blk", None),
        P("blk", None),
        P("blk"),
        P("blk"),
        P("blk"),
        P("blk", None),
        P("blk", None),
        P("blk", None),
        P("blk", None),
        P("blk", None),
        P("blk", None),
    )
    return jax.shard_map(body, mesh=mesh, in_specs=in_specs, out_specs=out_specs, check_vma=False)
```

```python
import functools
import math

import jax
import jax.numpy as jnp
from jax import lax
from jax.experimental import pallas as pl
from jax.experimental.pallas import tpu as pltpu
from jax.sharding import PartitionSpec as P

LAT = 256
HEADS = 8
QK_HEAD = 32
V_HEAD = 160
DQK = HEADS * QK_HEAD
DV = HEADS * V_HEAD
MESH = pl.DeviceIdType.MESH
F32 = jnp.float32
BF16 = jnp.bfloat16

epsilon = 1e-05
masked_score = -1e30
LOG2E = math.log2(math.e)
SCORE2 = QK_HEAD ** (-0.5) * LOG2E
SCORE_SCALE = QK_HEAD ** (-0.5)


def dot_nn(a, b):
    return jnp.dot(a, b, preferred_element_type=F32)


def dot_nt(a, b):
    return lax.dot_general(a, b, (((1,), (1,)), ((), ())), preferred_element_type=F32)


def norm_parts(v):
    centered = v - jnp.mean(v, axis=-1, keepdims=True)
    spread = jnp.mean(centered * centered, axis=-1, keepdims=True)
    inv = lax.rsqrt(spread + epsilon)
    return centered * inv, inv


def window(h):
    return V_HEAD * h // 128 * 128


def value_mask(h, rows):
    lane = lax.broadcasted_iota(jnp.int32, (rows, 256), 1) + window(h)
    keep = (lane >= V_HEAD * h) & (lane < V_HEAD * (h + 1))
    return jnp.where(keep, 1.0, 0.0).astype(BF16)


def query_mask(h, rows):
    lane = lax.broadcasted_iota(jnp.int32, (rows, DQK), 1)
    keep = (lane >= QK_HEAD * h) & (lane < QK_HEAD * (h + 1))
    return jnp.where(keep, 1.0, 0.0).astype(BF16)


def row_to_lanes(row):
    return jnp.transpose(jnp.broadcast_to(row, (128, row.shape[1])))


def wide(col, n):
    return jnp.concatenate([col] * (n // 128), axis=1) if n > 128 else col


def remote(src, dst, send, recv, doc, blk):
    return pltpu.make_async_remote_copy(
        src_ref=src, dst_ref=dst, send_sem=send, recv_sem=recv,
        device_id=(doc, blk), device_id_type=MESH,
    )


def forward_kernel(
    nb,
    x_hbm, wq_hbm, wk_hbm, wv_hbm, len_ref, mask_ref, lat_ref, gq_ref, gb_ref,
    att_ref, lse_ref, k_hbm, v_hbm, nlw_ref, qall_ref, bias_ref,
    x_ref, wq_ref, wk_ref, wv_ref, k_ref, v_ref, nl_cols, normed, qm, lloc, lmate, lz, acc, part, mate_in, rin, lin,
    load_s, x_s, out_s, q_s, q_r, n_s, n_r, l_s, l_r, mate_s, mate_r, rs_s, rs_r, ls_s, ls_r,
):
    D, kc, din = x_hbm.shape
    rq = lat_ref.shape[0]
    pos = nb // 2
    doc, blk = lax.axis_index("doc"), lax.axis_index("blk")
    p, c = blk // 2, blk % 2
    mate = 2 * p + 1 - c
    loads = [
        pltpu.make_async_copy(src, dst, load_s.at[i])
        for i, (src, dst) in enumerate(((wq_hbm, wq_ref), (wk_hbm, wk_ref), (wv_hbm, wv_ref)))
    ]

    def x_load(n):
        return pltpu.make_async_copy(x_hbm.at[n], x_ref.at[n], x_s.at[n])

    stores = [
        pltpu.make_async_copy(src, dst, out_s.at[i])
        for i, (src, dst) in enumerate(((k_ref, k_hbm), (v_ref, v_hbm)))
    ]
    loads[0].start()
    x_load(0).start()
    loads[1].start()
    for n in range(1, D):
        x_load(n).start()
    loads[2].start()
    barrier = pltpu.get_barrier_semaphore()
    for i in range(1, nb):
        pl.semaphore_signal(
            barrier, inc=1, device_id=(doc, lax.rem(blk + i, nb)), device_id_type=MESH
        )

    slots = blk * kc + lax.broadcasted_iota(jnp.int32, (1, kc), 1)
    for n in range(D):
        usable = (slots < len_ref[n]) & (mask_ref[n : n + 1, :] == 1)
        bias_ref[n : n + 1, :] = jnp.where(usable, 0.0, masked_score)

    xhat, _ = norm_parts(lat_ref[...])
    nl = (xhat * gq_ref[...].reshape(1, -1)).astype(BF16)
    step = nl.shape[1] // nb
    for j in range(nb):
        at = min(j * step // 128 * 128, nl.shape[1] - 256)
        nl_cols[j] = nl[:, at : at + 256]
    own = pl.ds(pl.multiple_of(blk * rq, rq), rq)
    loads[0].wait()
    qall_ref[own, :] = dot_nn(nl, wq_ref[...]).astype(BF16)
    pl.semaphore_wait(barrier, nb - 1)

    def q_copy(i, slot):
        return remote(
            qall_ref.at[own, :], qall_ref.at[slot, :], q_s.at[i - 1], q_r.at[i - 1],
            doc, lax.rem(blk + i, nb),
        )

    def n_copy(i, slot):
        peer = lax.rem(blk + i, nb)
        return remote(
            nl_cols.at[peer], nlw_ref.at[slot, :], n_s.at[i - 1], n_r.at[i - 1], doc, peer
        )

    for i in range(1, nb):
        q_copy(i, own).start()
    for i in range(1, nb):
        n_copy(i, own).start()
    nlw_ref[own, :] = nl_cols[blk]

    loads[1].wait()

    @pl.loop(0, D)
    def _(n):
        x_load(n).wait()
        xh, _ = norm_parts(x_ref[n].astype(F32))
        normed[n] = (xh * gb_ref[...].reshape(1, -1)).astype(BF16)
        k_ref[n] = dot_nn(normed[n], wk_ref[...]).astype(BF16)

    for i in range(1, nb):
        src = lax.rem(blk + nb - i, nb)
        q_copy(i, pl.ds(pl.multiple_of(src * rq, rq), rq)).wait_recv()
    for h in range(HEADS):
        qm[h] = qall_ref[...] * query_mask(h, LAT)

    stores[0].start()

    def own_logs(lo, hi):
        @pl.loop(lo, hi)
        def _(n):
            bias = wide(row_to_lanes(bias_ref[pl.ds(n, 1), :]), LAT)
            kn = k_ref[n]
            rows = []
            for h in range(HEADS):
                s = dot_nt(kn, qm[h]) * SCORE2 + bias
                top = jnp.max(s, axis=0, keepdims=True)
                tot = jnp.sum(jnp.exp2(s - top), axis=0, keepdims=True)
                rows.append(top + jnp.log(tot) * LOG2E)
            lloc[n] = jnp.concatenate(rows, axis=0)

    half, quarter = D // 2, D // 4

    def mine(b):
        return pl.ds(b * half + c * quarter, quarter)

    def other(b):
        return pl.ds(b * half + (1 - c) * quarter, quarter)

    def merge(a, b):
        top = jnp.maximum(a, b)
        return top + jnp.log(jnp.exp2(a - top) + jnp.exp2(b - top)) * LOG2E

    def first(b):
        return remote(lloc.at[other(b)], lmate.at[b], l_s.at[b, 0], l_r.at[b, 0], doc, mate)

    def z_copy(b, i, slot):
        return remote(
            lz.at[b, p], lz.at[b, slot], l_s.at[b, i], l_r.at[b, i],
            doc, 2 * lax.rem(p + i, pos) + c,
        )

    def last(b, part):
        return remote(
            lse_ref.at[part], lse_ref.at[part], l_s.at[b, pos], l_r.at[b, pos], doc, mate
        )

    def along(b):
        first(b).wait_recv()
        lz[b, p] = merge(lloc[mine(b)], lmate[b])
        for i in range(1, pos):
            z_copy(b, i, p).start()

    def close(b):
        for i in range(1, pos):
            z_copy(b, i, lax.rem(p + pos - i, pos)).wait_recv()
        total = lz[b, 0]
        for i in range(1, pos):
            total = merge(total, lz[b, i])
        lse_ref[mine(b)] = total
        last(b, mine(b)).start()

    def values(lo, hi):
        @pl.loop(lo, hi)
        def _(n):
            v_ref[n] = dot_nn(normed[n], wv_ref[...]).astype(BF16)

    own_logs(0, half)
    first(0).start()
    own_logs(half, D)
    first(1).start()
    along(0)
    loads[2].wait()
    values(0, quarter)
    along(1)
    values(quarter, D)
    stores[1].start()
    close(0)
    close(1)
    last(0, other(0)).wait_recv()

    def mate_copy(n):
        return remote(
            part.at[n, 1 - c], mate_in.at[n], mate_s.at[n], mate_r.at[n], doc, mate
        )

    def right_copy(n, j, src):
        return remote(
            src, rin.at[n, j], rs_s.at[n, j], rs_r.at[n, j],
            doc, 2 * jnp.minimum(p + 1, pos - 1) + c,
        )

    def left_copy(n, j, src):
        return remote(
            src, lin.at[n, j], ls_s.at[n, j], ls_r.at[n, j],
            doc, 2 * jnp.maximum(p - 1, 0) + c,
        )

    def chip_sum(n):
        mate_copy(n).wait_recv()
        both = part[n, c].astype(F32) + mate_in[n].astype(F32)
        part[n, c] = both.astype(BF16)

        @pl.when(p == 0)
        def _():
            for j in range(pos - 1, 0, -1):
                right_copy(n, j, part.at[n, c, j]).start()

        @pl.when(p == pos - 1)
        def _():
            for j in range(pos - 1):
                left_copy(n, j, part.at[n, c, j]).start()

    @pl.loop(0, D)
    def _(n):
        @pl.when(n == half)
        def _():
            last(1, other(1)).wait_recv()

        logs = lse_ref[n]
        logs_t = jnp.transpose(jnp.concatenate([logs] * (128 // HEADS), axis=0))
        bias = bias_ref[pl.ds(n, 1), :]
        kn = k_ref[n]
        for h in range(HEADS):
            s = dot_nt(qm[h], kn) * SCORE2 + bias
            prob = jnp.exp2(s - logs_t[:, h : h + 1]).astype(BF16)
            cols = slice(window(h), window(h) + 256)
            out = dot_nn(prob, v_ref[n, :, cols] * value_mask(h, kc))
            at = window(h)
            if h % (HEADS // 2) == 0:
                acc[:, at : at + 128] = out[:, 0:128]
            else:
                acc[:, at : at + 128] += out[:, 0:128]
            acc[:, at + 128 : at + 256] = out[:, 128:256]
        for j in range(nb):
            part[n, j % 2, j // 2] = acc[rq * j : rq * (j + 1), :].astype(BF16)
        mate_copy(n).start()

        @pl.when(n > 0)
        def _():
            chip_sum(n - 1)

    chip_sum(D - 1)

    def from_left(n):
        for j in range(pos - 1, 0, -1):
            @pl.when(j >= p)
            def _():
                right_copy(n, j, part.at[n, c, j]).wait_recv()

            @pl.when(j > p)
            def _():
                both = rin[n, j].astype(F32) + part[n, c, j].astype(F32)
                part[n, c, j] = both.astype(BF16)
                right_copy(n, j, part.at[n, c, j]).start()

    def from_right(n):
        for j in range(pos - 1):
            @pl.when(j <= p)
            def _():
                left_copy(n, j, part.at[n, c, j]).wait_recv()

            @pl.when(j < p)
            def _():
                both = lin[n, j].astype(F32) + part[n, c, j].astype(F32)
                part[n, c, j] = both.astype(BF16)
                left_copy(n, j, part.at[n, c, j]).start()

    def finish(n):
        acc[0:rq, :] = part[n, c, p].astype(F32)

        @pl.when(p > 0)
        def _():
            acc[0:rq, :] += rin[n, p].astype(F32)

        @pl.when(p < pos - 1)
        def _():
            acc[0:rq, :] += lin[n, p].astype(F32)

        att_ref[n] = acc[0:rq, :].astype(BF16)

    @pl.loop(0, D + pos - 1)
    def _(t):
        right_n, left_n, done_n = t - p, t - (pos - 1 - p), t - (pos - 1)

        @pl.when((p > 0) & (right_n >= 0) & (right_n < D))
        def _():
            from_left(right_n)

        @pl.when((p < pos - 1) & (left_n >= 0) & (left_n < D))
        def _():
            from_right(left_n)

        @pl.when(done_n >= 0)
        def _():
            finish(done_n)

    for i in range(1, nb):
        src = lax.rem(blk + nb - i, nb)
        n_copy(i, pl.ds(pl.multiple_of(src * rq, rq), rq)).wait_recv()

    for i in range(1, nb):
        q_copy(i, own).wait_send()
        n_copy(i, own).wait_send()
    for b in range(2):
        first(b).wait_send()
        for i in range(1, pos):
            z_copy(b, i, p).wait_send()
        last(b, mine(b)).wait_send()
    for store in stores:
        store.wait()

    @pl.loop(0, D)
    def _(n):
        mate_copy(n).wait_send()
        for j in range(pos):
            @pl.when((j > p) & (p < pos - 1))
            def _():
                right_copy(n, j, part.at[n, c, j]).wait_send()

            @pl.when((j < p) & (p > 0))
            def _():
                left_copy(n, j, part.at[n, c, j]).wait_send()


def forward(
    nb, byte_embed, doc_lengths, key_mask, latents, gain_query, gain_bytes, w_query, w_key, w_value
):
    D, kc, din = byte_embed.shape
    rq, dl = latents.shape
    pos = nb // 2
    vmem = pl.BlockSpec(memory_space=pltpu.VMEM)
    anywhere = pl.BlockSpec(memory_space=pl.ANY)
    dma = pltpu.SemaphoreType.DMA
    return pl.pallas_call(
        functools.partial(forward_kernel, nb),
        out_shape=(
            jax.ShapeDtypeStruct((D, rq, DV), BF16),
            jax.ShapeDtypeStruct((D, HEADS, LAT), F32),
            jax.ShapeDtypeStruct((D, kc, DQK), BF16),
            jax.ShapeDtypeStruct((D, kc, DV), BF16),
            jax.ShapeDtypeStruct((LAT, 256), BF16),
            jax.ShapeDtypeStruct((LAT, DQK), BF16),
            jax.ShapeDtypeStruct((D, kc), F32),
        ),
        in_specs=[anywhere] * 4 + [pl.BlockSpec(memory_space=pltpu.SMEM)] + [vmem] * 4,
        out_specs=(vmem, vmem, anywhere, anywhere, vmem, vmem, vmem),
        scratch_shapes=[
            pltpu.VMEM((D, kc, din), BF16),
            pltpu.VMEM(w_query.shape, BF16),
            pltpu.VMEM(w_key.shape, BF16),
            pltpu.VMEM(w_value.shape, BF16),
            pltpu.VMEM((D, kc, DQK), BF16),
            pltpu.VMEM((D, kc, DV), BF16),
            pltpu.VMEM((nb, rq, 256), BF16),
            pltpu.VMEM((D, kc, din), BF16),
            pltpu.VMEM((HEADS, LAT, DQK), BF16),
            pltpu.VMEM((D, HEADS, LAT), F32),
            pltpu.VMEM((2, D // 4, HEADS, LAT), F32),
            pltpu.VMEM((2, pos, D // 4, HEADS, LAT), F32),
            pltpu.VMEM((LAT, DV), F32),
            pltpu.VMEM((D, 2, pos, rq, DV), BF16),
            pltpu.VMEM((D, pos, rq, DV), BF16),
            pltpu.VMEM((D, pos, rq, DV), BF16),
            pltpu.VMEM((D, pos, rq, DV), BF16),
            dma((3,)), dma((D,)), dma((2,)),
            dma((nb - 1,)), dma((nb - 1,)), dma((nb - 1,)), dma((nb - 1,)),
            dma((2, pos + 1)), dma((2, pos + 1)),
            dma((D,)), dma((D,)),
            dma((D, pos)), dma((D, pos)), dma((D, pos)), dma((D, pos)),
        ],
        compiler_params=pltpu.CompilerParams(
            collective_id=0, has_side_effects=True, vmem_limit_bytes=56 * 2**20
        ),
        name="forward",
    )(
        byte_embed, w_query, w_key, w_value, doc_lengths, key_mask, latents, gain_query,
        gain_bytes,
    )


def gelu_parts(u):
    k = math.sqrt(2.0 / math.pi)
    sq = u * u
    t = jnp.tanh(k * u * (1.0 + 0.044715 * sq))
    value = 0.5 * u * (1.0 + t)
    slope = 0.5 * (1.0 + t) + 0.5 * k * u * (1.0 - t * t) * (1.0 + 3 * 0.044715 * sq)
    return value, slope


def owner_rows(total, docs):
    return -(-total // (16 * docs)) * 16


class ShardSums:
    def __init__(
        self, doc, blk, nd, nb, count, unit, group, lags, direct,
        own, mate_in, inbox, rin, lin, out, sems,
    ):
        self.doc, self.p, self.c = doc, blk // 2, blk % 2
        self.nd, self.pos, self.count, self.unit = nd, nb // 2, count, unit
        self.bits = nd.bit_length() - 1
        self.own, self.mate_in, self.inbox = own, mate_in, inbox
        self.rin, self.lin, self.out = rin, lin, out
        (
            self.mate_s, self.mate_r, self.in_s, self.in_r,
            self.right_s, self.right_r, self.left_s, self.left_r, self.out_s, self.out_r,
        ) = sems
        self.group, self.lags, self.direct = group, lags, direct
        self.steps = count // group + lags[-1] + (1 if direct else self.pos - 1)

    def weight(self, s, k):
        b = (s + k) % self.bits
        return 1 + b * (b + 1) // 2

    def my_bit(self, w):
        return (self.doc // w) % 2

    def quarter(self, s, k, i, sent):
        q = 0
        for r in range(k):
            w = self.weight(s, r)
            q = q + self.my_bit(w) * w
        w = self.weight(s, k)
        mine = self.my_bit(w)
        q = q + ((1 - mine) if sent else mine) * w
        for r in range(k + 1, self.bits):
            q = q + ((i >> (r - k - 1)) & 1) * self.weight(s, r)
        return q

    def width(self, k):
        return 2 ** (self.bits - 1 - k)

    def slot(self, k, i):
        return sum(self.width(r) for r in range(k)) + i

    def rows(self, q):
        return pl.ds(pl.multiple_of(q * self.unit, self.unit), self.unit)

    def halving(self, s, k, i):
        w = self.weight(s, k)
        peer = self.doc + w * (1 - 2 * self.my_bit(w))
        slot = self.slot(k, i)
        return remote(
            self.own.at[s, self.rows(self.quarter(s, k, i, True)), :], self.inbox.at[s, slot],
            self.in_s.at[s, slot], self.in_r.at[s, slot], peer, 2 * self.p + self.c,
        )

    def right(self, s):
        return remote(
            self.own.at[s, self.rows(self.doc), :], self.rin.at[s],
            self.right_s.at[s], self.right_r.at[s],
            self.doc, 2 * jnp.minimum(self.p + 1, self.pos - 1) + self.c,
        )

    def left(self, s):
        return remote(
            self.own.at[s, self.rows(self.doc), :], self.lin.at[s],
            self.left_s.at[s], self.left_r.at[s],
            self.doc, 2 * jnp.maximum(self.p - 1, 0) + self.c,
        )

    def share(self, m, i):
        return remote(
            self.out.at[m, self.rows(self.doc), :], self.out.at[m, self.rows(self.doc), :],
            self.out_s.at[m, i - 1], self.out_r.at[m, i - 1],
            lax.rem(self.doc + i, self.nd), 2 * self.p + self.c,
        )

    def shared(self, m, i):
        src = lax.rem(self.doc + self.nd - i, self.nd)
        return remote(
            self.out.at[m, self.rows(src), :], self.out.at[m, self.rows(src), :],
            self.out_s.at[m, i - 1], self.out_r.at[m, i - 1], src, 2 * self.p + self.c,
        )

    def add(self, s, q, other):
        rows = self.rows(q)
        self.own[s, rows, :] = (
            self.own[s, rows, :].astype(F32) + other.astype(F32)
        ).astype(BF16)

    def begin(self, s, mate_copy):
        mate_copy(s).wait_recv()
        rows = self.mate_in.shape[1]
        self.own[s, 0:rows, :] = (
            self.own[s, 0:rows, :].astype(F32) + self.mate_in[s].astype(F32)
        ).astype(BF16)
        for i in range(self.width(0)):
            self.halving(s, 0, i).start()

    def halve(self, s, k):
        for i in range(self.width(k - 1)):
            self.halving(s, k - 1, i).wait_recv()
            self.add(s, self.quarter(s, k - 1, i, False), self.inbox[s, self.slot(k - 1, i)])
        if k < self.bits:
            for i in range(self.width(k)):
                self.halving(s, k, i).start()
            return
        if self.direct:
            return
        j = s % self.pos

        @pl.when((self.p == 0) & (j > 0))
        def _():
            self.right(s).start()

        @pl.when((self.p == self.pos - 1) & (j < self.pos - 1))
        def _():
            self.left(s).start()

    def from_left(self, s):
        j = s % self.pos

        @pl.when(j >= self.p)
        def _():
            self.right(s).wait_recv()

        @pl.when(j > self.p)
        def _():
            self.add(s, self.doc, self.rin[s])
            self.right(s).start()

    def from_right(self, s):
        j = s % self.pos

        @pl.when(j <= self.p)
        def _():
            self.left(s).wait_recv()

        @pl.when(j < self.p)
        def _():
            self.add(s, self.doc, self.lin[s])
            self.left(s).start()

    def finish(self, s):
        @pl.when(s % self.pos == self.p)
        def _():
            m = s // self.pos

            @pl.when(self.p > 0)
            def _():
                self.add(s, self.doc, self.rin[s])

            @pl.when(self.p < self.pos - 1)
            def _():
                self.add(s, self.doc, self.lin[s])

            self.out[m, self.rows(self.doc), :] = self.own[s, self.rows(self.doc), :]
            for i in range(1, self.nd):
                self.share(m, i).start()

    def spread(self, i, back):
        to = lax.rem(self.p + (self.pos - i if back else i), self.pos)
        return remote(
            self.own.at[to, self.rows(self.doc), :], self.rin.at[i - 1],
            self.right_s.at[i - 1], self.right_r.at[i - 1], self.doc, 2 * to + self.c,
        )

    def scatter(self):
        for i in range(1, self.pos):
            self.spread(i, False).start()

    def collect(self):
        rows = self.rows(self.doc)
        total = self.own[self.p, rows, :].astype(F32)
        for i in range(1, self.pos):
            self.spread(i, True).wait_recv()
            total = total + self.rin[i - 1].astype(F32)
        self.out[0, rows, :] = total.astype(BF16)
        for i in range(1, self.nd):
            self.share(0, i).start()

    def step(self, t, mate_copy, entered=0):
        def at(t, when, run, turned=False):
            @pl.when((t >= 0) & (t < self.count // self.group) & when)
            def _():
                for i in range(self.group):
                    run(t * self.group + (self.group - 1 - i if turned else i))

        at(t, t >= entered, lambda s: self.begin(s, mate_copy))
        for k in range(1, self.bits + 1):
            at(t - self.lags[k - 1], True, functools.partial(self.halve, k=k))
        base = t - self.lags[-1]
        if self.direct:
            pl.when(base == 0)(self.scatter)
            pl.when(base == 1)(self.collect)
            return
        at(base - self.p, self.p > 0, self.from_left, True)
        at(base - (self.pos - 1 - self.p), self.p < self.pos - 1, self.from_right)
        at(base - (self.pos - 1), True, self.finish)

    def halved(self):
        @pl.loop(0, self.count)
        def _(s):
            for k in range(self.bits):
                for i in range(self.width(k)):
                    self.halving(s, k, i).wait_send()

    def drain(self):
        if self.direct:
            for i in range(1, self.pos):
                self.spread(i, False).wait_send()
        for m in range(self.count // self.pos):
            for i in range(1, self.nd):
                self.shared(m, i).wait_recv()
                self.share(m, i).wait_send()

        if self.direct:
            return

        @pl.loop(0, self.count)
        def _(s):
            j = s % self.pos

            @pl.when((j > self.p) & (self.p < self.pos - 1))
            def _():
                self.right(s).wait_send()

            @pl.when((j < self.p) & (self.p > 0))
            def _():
                self.left(s).wait_send()


def shard_sum_scratch(nd, nb, count, unit, rows, width, direct):
    dma = pltpu.SemaphoreType.DMA
    arrays = count // (nb // 2)
    return [
        pltpu.VMEM((count, unit * nd, width), BF16),
        pltpu.VMEM((count, rows, width), BF16),
        pltpu.VMEM((count, nd - 1, unit, width), BF16),
        pltpu.VMEM((count, unit, width), BF16),
        pltpu.VMEM((1, 16, 128) if direct else (count, unit, width), BF16),
        dma((count,)), dma((count,)),
        dma((count, nd - 1)), dma((count, nd - 1)),
        dma((count,)), dma((count,)), dma((count,)), dma((count,)),
        dma((arrays, nd - 1)), dma((arrays, nd - 1)),
    ]


def backward_kernel(nb, nd, wunit, vunit, *refs):
    (
        x_hbm, k_hbm, v_hbm, wo_hbm, wu_hbm, wd_hbm, wk_hbm, wv_hbm, cot_hbm,
        att_ref, lat_ref, gm_ref, bias_ref, gb_ref, qall_ref, lse_ref,
    ) = refs[:16]
    out_hbm, bg_hbm, wsum_ref, vsum0_ref, vsum1_ref, dsum_ref, gq_ref, gains_ref = refs[16:24]
    wscr, vscr = refs[24:39], (refs[39:54], refs[54:69])
    (
        wpool, x_ref, k_ref, ga_all, delta_all, delta_t, qm, wkv, gq_acc,
        fpool, frames, low_t, acts, gm, g_up, gb, stage, vstage, gain_acc, gmlp_acc, direct_out, dir_in,
        misc_out, misc_in, misc2_out, misc2_in,
        load_s, out_s, bg_s, ar_s, ar_r, al_s, al_r, am_s, am_r, d_s, d_r, dir_s, dir_r,
        m1_s, m1_r, m2_s, m2_r, m3_s, m3_r,
    ) = refs[69:]
    D, kc, din = x_ref.shape
    rq, dl = lat_ref.shape
    rows_all = D * rq
    pos = nb // 2
    hh, vh, qh = HEADS // 2, DV // 2, DQK // 2
    bits = nd.bit_length() - 1
    doc, blk = lax.axis_index("doc"), lax.axis_index("blk")
    p, c = blk // 2, blk % 2
    mate = 2 * p + 1 - c

    barrier = pltpu.get_barrier_semaphore()
    for i in range(1, nb):
        pl.semaphore_signal(
            barrier, inc=1, device_id=(doc, lax.rem(blk + i, nb)), device_id_type=MESH
        )
    for i in range(1, nd):
        pl.semaphore_signal(
            barrier, inc=1, device_id=(lax.rem(doc + i, nd), blk), device_id_type=MESH
        )

    def load(src, dst, i):
        return pltpu.make_async_copy(src, dst, load_s.at[i])

    slot0, slot1 = wpool.at[0:dl, :], wpool.at[dl : 2 * dl, :]
    load_out, load_up = load(wo_hbm, slot0, 0), load(wu_hbm, slot1, 1)
    load_down, load_out2 = load(wd_hbm, slot0, 2), load(wo_hbm, slot0, 3)
    load_v = load(v_hbm, wpool.at[0 : D * kc, :], 4)
    load_cot = load(cot_hbm, frames.at[1], 5)
    later = [load(k_hbm, k_ref, 6), load(x_hbm, x_ref, 7)]
    for g in range(2):
        later.append(load(wv_hbm.at[:, g * vh : (g + 1) * vh], wkv.at[g, :, 0:vh], 8 + g))
        later.append(
            load(wk_hbm.at[:, g * qh : (g + 1) * qh], wkv.at[g, :, vh : vh + qh], 10 + g)
        )
    load_out.start()
    load_up.start()
    load_cot.start()

    weights = ShardSums(
        doc, blk, nd, nb, 3 * pos, wunit, pos, [5 + 3 * k for k in range(bits)], False,
        *wscr[:5], wsum_ref, wscr[5:],
    )
    values = [
        ShardSums(
            doc, blk, nd, nb, pos, vunit, pos, lags, True, *vscr[g][:5], out, vscr[g][5:],
        )
        for g, (lags, out) in enumerate(
            (
                ([1 + k for k in range(bits)], vsum0_ref),
                ([1 + k for k in range(bits)], vsum1_ref),
            )
        )
    ]

    wrows, whalf = 2 * dl // nb, dl // 2
    vhalf = (vh + qh) // 2

    def w_mate(s):
        rows = pl.ds(pl.multiple_of(s % (2 * pos) * wrows, wrows), wrows)
        return remote(
            stage.at[rows, 0:whalf], weights.mate_in.at[s],
            weights.mate_s.at[s], weights.mate_r.at[s], doc, mate,
        )

    def v_mate(g):
        return lambda s: remote(
            vstage.at[s], values[g].mate_in.at[s],
            values[g].mate_s.at[s], values[g].mate_r.at[s], doc, mate,
        )

    parts, ahead = 2 * D, 4

    def chunk(j, core):
        return pl.ds(pl.multiple_of((2 * j + core) * rq, rq), rq)

    def right_copy(e, hop, j):
        rows = ga_all.at[e, chunk(j, c), :]
        return remote(
            rows, rows, ar_s.at[e, hop], ar_r.at[e, hop],
            doc, 2 * jnp.minimum(p + 1, pos - 1) + c,
        )

    def left_copy(e, hop, j):
        rows = ga_all.at[e, chunk(j, c), :]
        return remote(
            rows, rows, al_s.at[e, hop], al_r.at[e, hop],
            doc, 2 * jnp.maximum(p - 1, 0) + c,
        )

    def mate_copy(e, j, core):
        rows = ga_all.at[e, chunk(j, core), :]
        return remote(rows, rows, am_s.at[e, j], am_r.at[e, j], doc, mate)

    own_rows = pl.ds(pl.multiple_of(blk * rq, rq), rq)

    def delta_copy(i, rows):
        return remote(
            delta_all.at[rows, :], delta_all.at[rows, :], d_s.at[i - 1], d_r.at[i - 1],
            doc, lax.rem(blk + i, nb),
        )

    def direct_copy(i):
        return remote(
            direct_out, dir_in.at[i - 1], dir_s.at[i - 1], dir_r.at[i - 1],
            lax.rem(doc + i, nd), blk,
        )

    def send_own(e):
        @pl.when(p < pos - 1)
        def _():
            right_copy(e, 0, p).start()

        @pl.when(p > 0)
        def _():
            left_copy(e, 0, p).start()

        mate_copy(e, p, c).start()

    nm, act_low = acts.at[0], acts.at[1]
    mid = fpool.at[0:rows_all, :]
    xhat = fpool.at[rows_all : 2 * rows_all, :]
    slope = fpool.at[2 * rows_all : 3 * rows_all, :]
    kv_acc = fpool.at[0:din, 0 : vh + qh]
    step_w = dl // nb

    def weight_grad(m, left, right):
        low_t[...] = jnp.transpose(left[...])

        @pl.loop(0, pos)
        def _(j):
            s = m * pos + j
            for core in (1 - c, c):
                rows = pl.ds(pl.multiple_of((2 * j + core) * step_w, step_w), step_w)
                shard = dot_nn(low_t[rows, :], right[...]).astype(BF16)
                for i in range(2):
                    part = shard[:, i * whalf : (i + 1) * whalf]
                    if core is c:
                        weights.own[s, i * step_w : (i + 1) * step_w, :] = part
                    else:
                        at = pl.multiple_of(s % (2 * pos) * wrows, wrows) + i * step_w
                        stage[pl.ds(pl.multiple_of(at, 16), step_w), 0:whalf] = part
                if core is not c:
                    w_mate(s).start()

    att_low = att_ref[...].reshape(rows_all, DV)
    load_out.wait()
    mid[...] = dot_nn(att_low, slot0[...]) + jnp.concatenate([lat_ref[...]] * D, axis=0)
    load_down.start()
    xh, inv = norm_parts(mid[...])
    xhat[...] = xh
    nm[...] = (xh * gm_ref[...].reshape(1, -1)).astype(BF16)
    load_up.wait()
    act, sl = gelu_parts(dot_nn(nm[...], slot1[...]))
    slope[...] = sl
    act_low[...] = act.astype(BF16)
    load_cot.wait()
    gm[...] = frames[1].astype(BF16)
    pl.semaphore_wait(barrier, nb - 1 + nd - 1)
    weight_grad(0, act_low, gm)
    load_down.wait()
    frames[0] = mid[...] + dot_nn(act_low[...], slot0[...])
    store_out = pltpu.make_async_copy(frames.at[0], out_hbm, out_s)
    store_out.start()
    g_up[...] = (dot_nt(gm[...], slot0[...]) * slope[...]).astype(BF16)
    load_out2.start()
    for item in later:
        item.start()
    g_nm = dot_nt(g_up[...], slot1[...])
    gmlp_acc[...] = jnp.sum(g_nm * xhat[...], axis=0, keepdims=True)
    dxh = g_nm * gm_ref[...].reshape(1, -1)
    mid[...] = frames[1] + inv * (
        dxh
        - jnp.mean(dxh, axis=-1, keepdims=True)
        - xhat[...] * jnp.mean(dxh * xhat[...], axis=-1, keepdims=True)
    )
    gb[...] = mid[...].astype(BF16)
    for s in range(pos):
        weights.begin(s, w_mate)
    load_out2.wait()
    ga = dot_nt(gb[...], slot0[...])
    load_v.start()
    for g in range(2):
        for n in range(D):
            ga_all[g * D + n, own_rows, :] = ga[
                n * rq : (n + 1) * rq, g * vh : (g + 1) * vh
            ].astype(BF16)
    for e in range(ahead):
        send_own(e)
    lane = lax.broadcasted_iota(jnp.int32, (rq, 128), 1)
    delta = jnp.zeros((rq, 128), F32)
    for h in range(HEADS):
        cols = slice(window(h), window(h) + 256)
        prod = ga[:, cols] * (att_low[:, cols] * value_mask(h, rows_all)).astype(F32)
        one = jnp.sum(prod, axis=1, keepdims=True)
        for n in range(D):
            delta = delta + jnp.where(lane == n * HEADS + h, one[n * rq : (n + 1) * rq], 0.0)
    delta_all[own_rows, :] = delta
    for i in range(1, nb):
        delta_copy(i, own_rows).start()
    direct = mid[0:rq, :]
    for n in range(1, D):
        direct = direct + mid[n * rq : (n + 1) * rq, :]
    direct_out[...] = direct.astype(BF16)
    for i in range(1, nd):
        direct_copy(i).start()
    weight_grad(1, nm, g_up)
    for s in range(pos):
        w_mate(s).wait_send()
    weight_grad(2, att_low, gb)

    for h in range(HEADS):
        half = slice(h // hh * qh, h // hh * qh + qh)
        qm[h] = (qall_ref[...] * query_mask(h, LAT))[:, half]
    gq_acc[...] = jnp.zeros_like(gq_acc)
    kv_acc[...] = jnp.zeros((din, vh + qh), F32)
    gain_acc[...] = jnp.zeros_like(gain_acc)

    def forward_chunks(e, hop):
        j = p - 1 - hop

        @pl.when(j >= 0)
        def _():
            right_copy(e, hop, j).wait_recv()
            if hop + 1 < pos - 1:
                @pl.when(p < pos - 1)
                def _():
                    right_copy(e, hop + 1, j).start()

            mate_copy(e, j, c).start()

        i = p + 1 + hop

        @pl.when(i < pos)
        def _():
            left_copy(e, hop, i).wait_recv()
            if hop + 1 < pos - 1:
                @pl.when(p > 0)
                def _():
                    left_copy(e, hop + 1, i).start()

            mate_copy(e, i, c).start()

    def doc_rows(n):
        return pl.ds(pl.multiple_of(n * kc, kc), kc)

    def scores_back(g, n, i):
        e = g * D + n
        bias = wide(row_to_lanes(bias_ref[pl.ds(n, 1), :]), LAT)
        logs, deltas = lse_ref[n], delta_t[n]
        kn = k_ref[n, :, g * qh : (g + 1) * qh]
        kt = jnp.transpose(kn)
        gk = None
        for k in range(hh):
            h, at = g * hh + k, window(k)
            vcols = slice(g * vh + at, g * vh + at + 256)
            gah = ga_all[e, :, at : at + 256] * value_mask(k, LAT)
            s = dot_nt(kn, qm[h]) * SCORE2 + bias
            prob = jnp.exp2(s - logs[h : h + 1, :])
            dprob = dot_nt(wpool[doc_rows(n), vcols], gah)
            ds = (prob * (dprob - deltas[h : h + 1, :])).astype(BF16)
            gv = dot_nn(prob.astype(BF16), gah)
            if k == 0:
                frames[i, 0:kc, 0:128] = gv[:, 0:128]
            else:
                frames[i, 0:kc, at : at + 128] += gv[:, 0:128]
            frames[i, 0:kc, at + 128 : at + 256] = gv[:, 128:256]
            part = dot_nn(ds, qm[h])
            gk = part if k == 0 else gk + part
            rows = slice(QK_HEAD * h, QK_HEAD * (h + 1))
            gq_acc[rows, :] += dot_nn(kt[QK_HEAD * k : QK_HEAD * (k + 1), :], ds)
        return jnp.concatenate(
            [frames[i, 0:kc, 0:vh].astype(BF16), (gk * SCORE_SCALE).astype(BF16)], axis=1
        )

    def wave(w):
        @pl.when(w < parts - ahead)
        def _():
            send_own(w + ahead)

        for hop in range(pos - 1):
            @pl.when((w >= hop) & (w - hop < parts))
            def _():
                forward_chunks(w - hop, hop)

    def bytes_back(g, m, w):
        n0 = 2 * m
        both = []
        for i in range(2):
            if i == 1:
                wave(w)
            for j in range(pos):
                mate_copy(g * D + n0 + i, j, 1 - c).wait_recv()
            both.append(scores_back(g, n0 + i, i))
        grads = jnp.concatenate(both, axis=0)
        xh, inv = norm_parts(x_ref[pl.ds(n0, 2)].reshape(2 * kc, din).astype(F32))
        kept = stage.at[pl.ds(pl.multiple_of(n0 * kc, 2 * kc), 2 * kc), 0:din]
        if g == 0:
            kept[...] = dot_nt(grads, wkv[0]).astype(BF16)
        else:
            gx = kept[...].astype(F32) + dot_nt(grads, wkv[1])
            gain_acc[...] += jnp.sum(gx * xh, axis=0, keepdims=True)
            dxh = gx * gb_ref[...].reshape(1, -1)
            dx = inv * (
                dxh
                - jnp.mean(dxh, axis=-1, keepdims=True)
                - xh * jnp.mean(dxh * xh, axis=-1, keepdims=True)
            )
            for i in range(2):
                @pl.when(m >= 1)
                def _():
                    pltpu.make_async_copy(
                        acts.at[i, 0:kc, 0:din], bg_hbm.at[n0 + i - 2], bg_s.at[i]
                    ).wait()

                acts[i, 0:kc, 0:din] = dx[i * kc : (i + 1) * kc, :].astype(BF16)
                pltpu.make_async_copy(
                    acts.at[i, 0:kc, 0:din], bg_hbm.at[n0 + i], bg_s.at[i]
                ).start()
        normed_t = jnp.transpose((xh * gb_ref[...].reshape(1, -1)).astype(BF16))
        kv_acc[...] += dot_nn(normed_t, grads)

    def cut_values(g):
        step = din // nb
        if g == 1:
            for s in range(pos):
                v_mate(0)(s).wait_send()
        for s in range(pos):
            for core in (1 - c, c):
                rows = pl.ds(pl.multiple_of((2 * s + core) * step, step), step)
                to = values[g].own if core is c else vstage
                for i in range(2):
                    to[s, i * step : (i + 1) * step, :] = fpool[
                        rows, i * vhalf : (i + 1) * vhalf
                    ].astype(BF16)
            v_mate(g)(s).start()
        if g == 0:
            kv_acc[...] = jnp.zeros((din, vh + qh), F32)

    pairs, fill = D // 2, pos // 2
    start0 = fill + pairs + 1

    @pl.loop(0, 2 * pairs + fill)
    def _(t):
        wave(2 * t)

        @pl.when(t < fill)
        def _():
            wave(2 * t + 1)

        weights.step(t + 1, w_mate, 1)
        values[0].step(t - start0, v_mate(0))

        @pl.when(t == fill)
        def _():
            for i in range(1, nb):
                src = lax.rem(blk + nb - i, nb)
                delta_copy(i, pl.ds(pl.multiple_of(src * rq, rq), rq)).wait_recv()
            turned = jnp.transpose(delta_all[...])
            for n in range(D):
                delta_t[n] = turned[n * HEADS : (n + 1) * HEADS, :]
            for item in later:
                item.wait()
            load_v.wait()
            store_out.wait()
            for s in range(pos, 3 * pos):
                w_mate(s).wait_send()

        @pl.when((t >= fill) & (t < fill + pairs))
        def _():
            bytes_back(0, t - fill, 2 * t + 1)

        @pl.when(t == fill + pairs)
        def _():
            cut_values(0)

        @pl.when(t >= fill + pairs)
        def _():
            bytes_back(1, t - fill - pairs, 2 * t + 1)

    cut_values(1)

    gq_rows = (jnp.transpose(gq_acc[...]) * SCORE_SCALE).astype(BF16)
    gains = jnp.concatenate([gmlp_acc[...], gain_acc[...]], axis=1)
    rows8 = [gains[:, 256 * i : 256 * (i + 1)] for i in range(8)]
    gains8 = jnp.concatenate(rows8 + [jnp.zeros((8, 256), F32)], axis=0).astype(BF16)
    for j in range(nb):
        misc_out[j, 0:rq] = gq_rows[j * rq : (j + 1) * rq, :]
        misc_out[j, rq : rq + 16] = gains8

    def misc1(i, slot):
        peer = lax.rem(blk + i, nb)
        return remote(
            misc_out.at[peer], misc_in.at[slot], m1_s.at[i - 1], m1_r.at[i - 1], doc, peer
        )

    def misc2(i, slot):
        return remote(
            misc2_out, misc2_in.at[slot], m2_s.at[i - 1], m2_r.at[i - 1],
            lax.rem(doc + i, nd), blk,
        )

    def misc3(i, rows):
        return remote(
            gq_ref.at[rows, :], gq_ref.at[rows, :], m3_s.at[i - 1], m3_r.at[i - 1],
            doc, lax.rem(blk + i, nb),
        )

    for i in range(1, nb):
        misc1(i, blk).start()
    misc_in[blk] = misc_out[blk]

    @pl.loop(0, parts)
    def _(e):
        mate_copy(e, p, c).wait_send()

        @pl.when(p < pos - 1)
        def _():
            right_copy(e, 0, p).wait_send()

        @pl.when(p > 0)
        def _():
            left_copy(e, 0, p).wait_send()

        for hop in range(pos - 1):
            j = p - 1 - hop

            @pl.when(j >= 0)
            def _():
                mate_copy(e, j, c).wait_send()
                if hop + 1 < pos - 1:
                    @pl.when(p < pos - 1)
                    def _():
                        right_copy(e, hop + 1, j).wait_send()

            i = p + 1 + hop

            @pl.when(i < pos)
            def _():
                mate_copy(e, i, c).wait_send()
                if hop + 1 < pos - 1:
                    @pl.when(p > 0)
                    def _():
                        left_copy(e, hop + 1, i).wait_send()

    total = direct_out[...].astype(F32)
    for i in range(1, nd):
        direct_copy(i).wait_recv()
        total = total + dir_in[i - 1].astype(F32)
    dsum_ref[...] = total

    for n in range(D - 2, D):
        pltpu.make_async_copy(acts.at[n % 2, 0:kc, 0:din], bg_hbm.at[n], bg_s.at[n % 2]).wait()
    first = 2 * pairs + fill
    last = max(weights.steps - 1, start0 + values[0].steps, first + values[1].steps)

    @pl.loop(first, last)
    def _(t):
        values[1].step(t - first, v_mate(1))
        values[0].step(t - start0, v_mate(0))
        weights.step(t + 1, w_mate, 1)

        @pl.when(t == first)
        def _():
            for i in range(1, nb):
                misc1(i, lax.rem(blk + nb - i, nb)).wait_recv()
            total = misc_in[0].astype(F32)
            for i in range(1, nb):
                total = total + misc_in[i].astype(F32)
            misc2_out[...] = total.astype(BF16)
            for i in range(1, nd):
                misc2(i, doc).start()
            misc2_in[doc] = misc2_out[...]

        @pl.when(t == first + 1)
        def _():
            for i in range(1, nd):
                misc2(i, lax.rem(doc + nd - i, nd)).wait_recv()
            total = misc2_in[0].astype(F32)
            for i in range(1, nd):
                total = total + misc2_in[i].astype(F32)
            weights.halved()
            values[0].halved()
            gains_ref[...] = total[rq : rq + 8, :]
            gq_ref[own_rows, :] = total[0:rq].astype(BF16)
            for i in range(1, nb):
                misc3(i, own_rows).start()

    for i in range(1, nb):
        src = lax.rem(blk + nb - i, nb)
        misc3(i, pl.ds(pl.multiple_of(src * rq, rq), rq)).wait_recv()

    values[1].halved()
    weights.drain()
    for g in range(2):
        values[g].drain()
    for s in range(pos):
        v_mate(1)(s).wait_send()
    for i in range(1, nb):
        delta_copy(i, own_rows).wait_send()
        misc1(i, blk).wait_send()
        misc3(i, own_rows).wait_send()
    for i in range(1, nd):
        direct_copy(i).wait_send()
        misc2(i, doc).wait_send()


def backward(
    nb, nd, byte_embed, keys, values, w_out, w_up, w_down, w_key, w_value, cotangent,
    attended, latents, gain_mlp, bias, gain_bytes, queries, lse,
):
    D, kc, din = byte_embed.shape
    rq, dl = latents.shape
    pos = nb // 2
    rows = D * rq
    wunit, vunit = owner_rows(2 * dl // nb, nd), owner_rows(2 * din // nb, nd)
    whalf, vhalf = dl // 2, (DV + DQK) // 4
    vmem = pl.BlockSpec(memory_space=pltpu.VMEM)
    anywhere = pl.BlockSpec(memory_space=pl.ANY)
    dma = pltpu.SemaphoreType.DMA
    scratch = (
        shard_sum_scratch(nd, nb, 3 * pos, wunit, 2 * dl // nb, whalf, False)
        + shard_sum_scratch(nd, nb, pos, vunit, 2 * din // nb, vhalf, True)
        + shard_sum_scratch(nd, nb, pos, vunit, 2 * din // nb, vhalf, True)
        + [
            pltpu.VMEM((max(2 * dl, D * kc), dl), BF16),
            pltpu.VMEM((D, kc, din), BF16),
            pltpu.VMEM((D, kc, DQK), BF16),
            pltpu.VMEM((2 * D, LAT, DV // 2), BF16),
            pltpu.VMEM((LAT, 128), F32),
            pltpu.VMEM((D, HEADS, LAT), F32),
            pltpu.VMEM((HEADS, LAT, DQK // 2), BF16),
            pltpu.VMEM((2, din, (DV + DQK) // 2), BF16),
            pltpu.VMEM((DQK, LAT), F32),
            pltpu.VMEM((max(3 * rows, din), dl), F32),
            pltpu.VMEM((2, rows, dl), F32),
            pltpu.VMEM((dl, rows), BF16),
            pltpu.VMEM((2, rows, dl), BF16),
            pltpu.VMEM((rows, dl), BF16),
            pltpu.VMEM((rows, dl), BF16),
            pltpu.VMEM((rows, dl), BF16),
            pltpu.VMEM((max(2 * dl, D * kc), (DV + DQK) // 2), BF16),
            pltpu.VMEM((pos, 2 * din // nb, vhalf), BF16),
            pltpu.VMEM((1, din), F32),
            pltpu.VMEM((1, dl), F32),
            pltpu.VMEM((rq, dl), BF16),
            pltpu.VMEM((nd - 1, rq, dl), BF16),
            pltpu.VMEM((nb, rq + 16, 256), BF16),
            pltpu.VMEM((nb, rq + 16, 256), BF16),
            pltpu.VMEM((rq + 16, 256), BF16),
            pltpu.VMEM((nd, rq + 16, 256), BF16),
            dma((12,)), dma, dma((2,)),
            dma((2 * D, pos - 1)), dma((2 * D, pos - 1)),
            dma((2 * D, pos - 1)), dma((2 * D, pos - 1)),
            dma((2 * D, pos)), dma((2 * D, pos)),
            dma((nb - 1,)), dma((nb - 1,)), dma((nd - 1,)), dma((nd - 1,)),
            dma((nb - 1,)), dma((nb - 1,)), dma((nd - 1,)), dma((nd - 1,)),
            dma((nb - 1,)), dma((nb - 1,)),
        ]
    )
    return pl.pallas_call(
        functools.partial(backward_kernel, nb, nd, wunit, vunit),
        out_shape=(
            jax.ShapeDtypeStruct((rows, dl), F32),
            jax.ShapeDtypeStruct((D, kc, din), BF16),
            jax.ShapeDtypeStruct((3, wunit * nd, whalf), BF16),
            jax.ShapeDtypeStruct((1, vunit * nd, vhalf), BF16),
            jax.ShapeDtypeStruct((1, vunit * nd, vhalf), BF16),
            jax.ShapeDtypeStruct((rq, dl), F32),
            jax.ShapeDtypeStruct((LAT, DQK), BF16),
            jax.ShapeDtypeStruct((8, 256), F32),
        ),
        in_specs=[anywhere] * 9 + [vmem] * 7,
        out_specs=(anywhere,) * 2 + (vmem,) * 6,
        scratch_shapes=scratch,
        compiler_params=pltpu.CompilerParams(
            collective_id=1, has_side_effects=True, vmem_limit_bytes=63 * 2**20
        ),
        name="backward",
    )(
        byte_embed, keys, values.reshape(D * kc, DV), w_out, w_up, w_down, w_key, w_value,
        cotangent.reshape(rows, dl), attended, latents, gain_mlp, bias,
        gain_bytes, queries, lse,
    )


def finish_kernel(
    nb, rows_hbm, bytes_hbm, wsum_hbm, vsum0_ref, vsum1_ref, dsum_ref, gq_ref, gains_ref, cols_ref,
    lat_ref, gain_ref, wq_ref, rows_out, bytes_out, lgrad_ref, gq_gain_ref, gb_gain_ref,
    gm_gain_ref, wq_out, wk_out, wv_out, wo_out, wu_out, wd_out, turned,
    wsum_ref, bytes_in, bytes_buf, rows_buf, take_s, move_s,
):
    D = bytes_hbm.shape[0]
    pairs = [(bytes_hbm.at[n], bytes_in.at[n], bytes_buf.at[n], bytes_out.at[n]) for n in range(D)]
    pairs.append((rows_hbm, rows_buf, rows_buf, rows_out))
    takes = [
        pltpu.make_async_copy(src, buf, take_s.at[i]) for i, (src, buf, _, _) in enumerate(pairs)
    ]
    takes.append(pltpu.make_async_copy(wsum_hbm, wsum_ref, take_s.at[D + 1]))
    moves = [
        pltpu.make_async_copy(buf, out, move_s.at[i]) for i, (_, _, buf, out) in enumerate(pairs)
    ]
    for take in takes:
        take.start()
    for n in range(D + 1):
        takes[n].wait()
        if n < D:
            bytes_buf[n] = bytes_in[n].astype(F32)
        moves[n].start()
    takes[-1].wait()
    rq, dl = lat_ref.shape
    din, step, vstep = wk_out.shape[0] * nb, dl // nb, wk_out.shape[0]
    blk = lax.axis_index("blk")
    half = dl // 2
    for m, out in enumerate((wd_out, wu_out, wo_out)):
        for i in range(2):
            out[:, i * half : (i + 1) * half] = wsum_ref[
                m, i * step : (i + 1) * step, :
            ].astype(F32)
    width = (DV + DQK) // 4
    for g, ref in enumerate((vsum0_ref, vsum1_ref)):
        both = jnp.concatenate(
            [ref[0, i * vstep : (i + 1) * vstep, :].astype(F32) for i in range(2)], axis=1
        )
        at = DV // 2
        wv_out[:, g * at : (g + 1) * at] = both[:, :at]
        wk_out[:, g * DQK // 2 : (g + 1) * DQK // 2] = both[:, at : 2 * width]

    gq = gq_ref[...]
    cols = cols_ref[...]
    first = pl.multiple_of(jnp.minimum(blk * step // 128 * 128, dl - 256), 128)
    skip = blk * step - first
    turned[...] = dot_nn(jnp.transpose(cols), gq)
    wq_out[...] = turned[pl.ds(pl.multiple_of(skip, 16), step), :]
    dy = dot_nt(gq, wq_ref[pl.ds(first, 256), :])
    gain = jnp.sum(dy * cols.astype(F32), axis=0, keepdims=True) / gain_ref[pl.ds(first, 256)].reshape(1, -1)

    def cut(row, at, count):
        size = row.shape[1]
        return pltpu.roll(row, lax.rem(size - at, size), 1)[:, :count]

    gq_gain_ref[...] = cut(gain, skip, step)
    row = jnp.concatenate([gains_ref[i : i + 1, :] for i in range(8)], axis=1)
    gm_gain_ref[...] = cut(row[:, :dl], blk * step, step)
    gb_gain_ref[...] = cut(row[:, dl:], blk * vstep, vstep)

    own = gq_ref[pl.ds(pl.multiple_of(blk * rq, rq), rq), :]
    dxh = dot_nt(own, wq_ref[...]) * gain_ref[...].reshape(1, -1)
    xh, inv = norm_parts(lat_ref[...])
    lgrad_ref[...] = dsum_ref[...] + inv * (
        dxh
        - jnp.mean(dxh, axis=-1, keepdims=True)
        - xh * jnp.mean(dxh * xh, axis=-1, keepdims=True)
    )
    for move in moves:
        move.wait()


def finish(
    nb, latents_out, byte_grad, wsum, vsum0, vsum1, direct_sum, gq, gains, norm_cols, latents,
    gain_query, w_query,
):
    rq, dl = latents.shape
    din = gains.size - dl
    vmem = pl.BlockSpec(memory_space=pltpu.VMEM)
    anywhere = pl.BlockSpec(memory_space=pl.ANY)
    shapes = (
        latents_out.shape, byte_grad.shape, (rq, dl), (1, dl // nb), (1, din // nb), (1, dl // nb), (dl // nb, DQK),
        (din // nb, DQK), (din // nb, DV), (dl // nb, dl), (dl // nb, dl), (dl // nb, dl),
    )
    return pl.pallas_call(
        functools.partial(finish_kernel, nb),
        out_shape=tuple(jax.ShapeDtypeStruct(s, F32) for s in shapes),
        in_specs=[anywhere] * 3 + [vmem] * 9,
        out_specs=(anywhere,) * 2 + (vmem,) * 10,
        scratch_shapes=[
            pltpu.VMEM((256, DQK), F32),
            pltpu.VMEM(wsum.shape, BF16),
            pltpu.VMEM(byte_grad.shape, BF16),
            pltpu.VMEM(byte_grad.shape, F32),
            pltpu.VMEM(latents_out.shape, F32),
            pltpu.SemaphoreType.DMA((byte_grad.shape[0] + 2,)),
            pltpu.SemaphoreType.DMA((byte_grad.shape[0] + 1,)),
        ],
        compiler_params=pltpu.CompilerParams(vmem_limit_bytes=60 * 2**20),
        name="finish",
    )(
        latents_out, byte_grad, wsum, vsum0, vsum1, direct_sum, gq, gains, norm_cols, latents,
        gain_query, w_query,
    )


def body(
    byte_embed,
    doc_lengths,
    key_mask,
    latents,
    gain_query,
    gain_bytes,
    gain_mlp,
    w_query,
    w_key,
    w_value,
    w_out,
    w_up,
    w_down,
    cotangent,
):
    nb, nd = lax.axis_size("blk"), lax.axis_size("doc")
    attended, lse, keys, values, norm_cols, queries, bias = forward(
        nb, byte_embed, doc_lengths, key_mask, latents, gain_query, gain_bytes, w_query, w_key,
        w_value,
    )
    latents_out, byte_grad, wsum, vsum0, vsum1, direct_sum, gq, gains = backward(
        nb, nd, byte_embed, keys, values, w_out, w_up, w_down, w_key, w_value, cotangent,
        attended, latents, gain_mlp, bias, gain_bytes, queries, lse,
    )
    (
        latents_out, byte_grad, latents_grad, gain_query_grad, gain_bytes_grad, gain_mlp_grad,
        grad_w_query, grad_w_key, grad_w_value, grad_w_out, grad_w_up, grad_w_down,
    ) = finish(
        nb, latents_out, byte_grad, wsum, vsum0, vsum1, direct_sum, gq, gains, norm_cols,
        latents, gain_query, w_query,
    )
    latents_out = latents_out.reshape(cotangent.shape)
    return (
        latents_out,
        byte_grad,
        latents_grad,
        gain_query_grad.reshape(-1),
        gain_bytes_grad.reshape(-1),
        gain_mlp_grad.reshape(-1),
        grad_w_query,
        grad_w_key,
        grad_w_value,
        grad_w_out,
        grad_w_up,
        grad_w_down,
    )


def solution(mesh):
    in_specs = (
        P("doc", "blk", None),
        P("doc"),
        P("doc", "blk"),
        P("blk", None),
        P(),
        P(),
        P(),
        P(),
        P(),
        P(),
        P(),
        P(),
        P(),
        P("doc", "blk", None),
    )
    out_specs = (
        P("doc", "blk", None),
        P("doc", "blk", None),
        P("blk", None),
        P("blk"),
        P("blk"),
        P("blk"),
        P("blk", None),
        P("blk", None),
        P("blk", None),
        P("blk", None),
        P("blk", None),
        P("blk", None),
    )
    return jax.shard_map(body, mesh=mesh, in_specs=in_specs, out_specs=out_specs, check_vma=False)
```
